32 devices in a mesh: dp: 16 (over z, y, x), section: 2 (over core).
Axes of the slice: x: 2, y: 2, z: 4, core: 2. Of those that a mesh axis runs over, the one named last changes fastest.
Arguments:
- activations: bfloat16 [2, 16, 4, 48, 4224], P('section', 'dp'), may hold values from -6 to 6
- key_grads: bfloat16 [2, 16, 4, 48, 640], P('section', 'dp'), may hold values from -6 to 6
- top_grad: bfloat16 [16, 4, 48, 4224], P('dp'), may hold values from -6 to 6
- norm_gains: float32 [2, 4224], P('section'), may hold values from 0.1 to 1.9
- w_key: bfloat16 [2, 4224, 640], P('section', 'dp'), may hold values from -0.09375 to 0.09375
- lengths: int32 [16, 4], P('dp'), may hold values from 1 to 48
Outputs:
- section_grads: bfloat16 [2, 16, 4, 48, 4224], P('section', 'dp')
- gain_grad: float32 [2, 4224], P('section', 'dp')
The draws below stay inside these ranges and needn't reach their ends.
All inputs are finite; a program needn't handle non-finite values.
Results may differ from the reference program's by a relative error of at most 0.0035.
Values may be sent and summed in bfloat16 or wider, within the bound.
No kernel may reach another device: no remote copies, remote signals or barrier semaphores. Data moves between devices by JAX's collectives and lax.ppermute only.
A program may use at most 64 MiB of HBM per device.

```python
import math
import jax
import jax.numpy as jnp
from jax import lax

DW = 4224
KVW = 640
MB = 4
MBLEN = 48
SECTIONS = 2
REPLICAS = 16


def set_ends(array, stream_key, smallest, top_value):
    extent = array.shape
    spot = [jax.random.randint(jax.random.fold_in(stream_key, axis), (), 0, extent[axis]) for axis in range(len(extent))]
    array = array.at[tuple(spot)].set(smallest)
    longest = extent.index(max(extent))
    spot[longest] = (spot[longest] + 1) % extent[longest]
    return array.at[tuple(spot)].set(top_value)


def strengthened(values, rng, source, target, shards_of, factor):
    def block_of(axis_at):
        return (jnp.arange(values.shape[axis_at]) // (values.shape[axis_at] // shards_of)).reshape((-1,) + (1,) * (values.ndim - 1 - axis_at))

    near = jax.random.permutation(rng, shards_of)[block_of(target)]
    second = (block_of(target) + shards_of // 2) % shards_of
    return jnp.where((block_of(source) == near) | (block_of(source) == second), factor * values, values)


def levels(stream_key, shape, pieces, smallest, largest):
    def one(dim, shards_of):
        heights = jax.random.uniform(jax.random.fold_in(jax.random.fold_in(stream_key, 6), dim), (shards_of,), jnp.float32, smallest / len(pieces), largest / len(pieces))
        return jnp.repeat(jnp.exp(heights), shape[dim] // shards_of).reshape((-1,) + (1,) * (len(shape) - dim - 1))

    loudness = one(*pieces[0])
    for cut in pieces[1:]:
        loudness = loudness * one(*cut)
    return loudness


def centred(rng, shape, deviation, bound, shards=(), kind=jnp.bfloat16):
    values = deviation * jax.random.normal(rng, shape, jnp.float32)
    if shards:
        values = values * levels(rng, shape, shards, -0.22, 0.18)
    return jnp.clip(values, -bound, bound).astype(kind)


def bell_draw_with(own_key, shape, scale, reach, cuts, heavy, held_as=jnp.bfloat16):
    entries = scale * jax.random.normal(own_key, shape, jnp.float32)
    if cuts:
        entries = entries * levels(own_key, shape, cuts, -0.22, 0.18)
    return jnp.clip(strengthened(entries, jax.random.fold_in(own_key, 3), *heavy), -reach, reach).astype(held_as)


def setup_inputs(seed: int = 0) -> dict:
    seeds = jax.random.split(jax.random.key(seed), 7)
    return {
        "activations": bell_draw_with(seeds[0], (SECTIONS, REPLICAS, MB, MBLEN, DW), 1.0, 6.0, ((0, 2), (1, 16)), (1, 4, 16, 2.0)),
        "key_grads": centred(seeds[1], (SECTIONS, REPLICAS, MB, MBLEN, KVW), 1.0, 6.0, ((0, 2), (1, 16))),
        "top_grad": centred(seeds[2], (REPLICAS, MB, MBLEN, DW), 1.0, 6.0, ((0, 16),)),
        "norm_gains": jnp.clip(1.0 + 0.18 * jax.random.normal(seeds[3], (SECTIONS, DW), jnp.float32), 0.1, 1.9),
        "w_key": centred(seeds[4], (SECTIONS, DW, KVW), DW ** -0.5, 0.09375, ((0, 2), (1, 16))),
        "lengths": set_ends(jax.random.randint(seeds[5], (REPLICAS, MB), 1, MBLEN + 1), jax.random.fold_in(seeds[5], 1), 1, MBLEN).astype(jnp.int32),
    }


norm_epsilon = 1e-05

def section_terms(inputs, key_cot, row_count, gain_row, weight):
    micro_count, seq_rows, feature_count = inputs.shape
    position = lax.broadcasted_iota(jnp.int32, (micro_count, seq_rows), 1)
    keep_row = position < row_count[:, None]
    masked = jnp.where(keep_row[:, :, None], key_cot, jnp.zeros_like(key_cot)).reshape(micro_count * seq_rows, key_cot.shape[2])
    wide_rows = inputs.astype(jnp.float32).reshape(micro_count * seq_rows, feature_count)
    inverse = lax.rsqrt(lax.optimization_barrier(jnp.mean(wide_rows * wide_rows, axis=1, keepdims=True)) + norm_epsilon)
    back_proj = lax.dot_general(masked, weight, (((1,), (1,)), ((), ())), preferred_element_type=jnp.float32)
    scaled = back_proj * gain_row[None, :]
    local_term = inverse * scaled - wide_rows * inverse ** 3 * lax.optimization_barrier(jnp.mean(wide_rows * scaled, axis=1, keepdims=True))
    gain_term = lax.optimization_barrier(jnp.sum(wide_rows * inverse * back_proj, axis=0))
    return (local_term.reshape(micro_count, seq_rows, feature_count), gain_term)

def reference(activations, key_grads, top_grad, norm_gains, w_key, lengths):
    grad_scale = 1.0 / math.sqrt(REPLICAS * MB * MBLEN)
    handed = top_grad
    handed_list = []
    gain_list = []
    for section_id in range(SECTIONS - 1, -1, -1):

        def one_replica(accumulated, carried, section_id=section_id):
            inputs, key_cot, row_count, incoming = carried
            local_term, gain_term = section_terms(inputs, key_cot, row_count, norm_gains[section_id], w_key[section_id])
            passed = (incoming.astype(jnp.float32) + local_term).astype(jnp.bfloat16)
            return (accumulated + gain_term, passed)
        accumulated, handed = lax.scan(one_replica, jnp.zeros((DW,), jnp.float32), (activations[section_id], key_grads[section_id], lengths, handed))
        handed_list.insert(0, handed)
        gain_list.insert(0, accumulated * grad_scale)
    return (jnp.stack(handed_list), jnp.stack(gain_list))
```

```python
import functools
import math

import jax
import jax.numpy as jnp
from jax import lax
from jax.experimental import pallas as pl
from jax.experimental.pallas import tpu as pltpu
from jax.sharding import PartitionSpec as P

norm_epsilon = 1e-05
vmem_bytes = 48 * 1024 * 1024


def plane_size(replicas):
    size = 1
    while (2 * size) ** 2 <= replicas and replicas % (2 * size) == 0:
        size *= 2
    return size


def ahead(place, step, count):
    if count & (count - 1) == 0:
        return place ^ step
    return (place + step) % count


def behind(place, step, count):
    if count & (count - 1) == 0:
        return place ^ step
    return (place + count - step) % count


def along_line(value, step, line, plane):
    pairs = [
        (z * plane + q, ahead(z, step, line) * plane + q)
        for z in range(line)
        for q in range(plane)
    ]
    return lax.ppermute(value, "dp", pairs)


def along_plane(value, step, line, plane, back=False):
    partner = behind if back else ahead
    pairs = [
        (z * plane + q, z * plane + partner(q, step, plane))
        for z in range(line)
        for q in range(plane)
    ]
    return lax.ppermute(value, "dp", pairs)


def product_kernel(token_count, weight_count, *refs):
    tokens = refs[:token_count]
    weights = refs[token_count : token_count + weight_count]
    outs = refs[token_count + weight_count :]
    for token_ref, out_ref in zip(tokens, outs):
        for index, weight_ref in enumerate(weights):
            out_ref[index] = lax.dot_general(
                token_ref[...],
                weight_ref[...],
                (((1,), (1,)), ((), ())),
                preferred_element_type=jnp.float32,
            ).astype(out_ref.dtype)


def products(tokens, weights):
    rows, depth = tokens[0].shape
    width = weights[0].shape[0]
    count = len(weights)
    return pl.pallas_call(
        functools.partial(product_kernel, len(tokens), count),
        out_shape=[jax.ShapeDtypeStruct((count, rows, width), jnp.bfloat16) for _ in tokens],
        in_specs=[pl.BlockSpec(memory_space=pltpu.VMEM)] * (len(tokens) + count),
        out_specs=[pl.BlockSpec(memory_space=pltpu.VMEM)] * len(tokens),
        compiler_params=pltpu.CompilerParams(vmem_limit_bytes=vmem_bytes),
        cost_estimate=pl.CostEstimate(
            flops=2 * rows * depth * width * count * len(tokens),
            bytes_accessed=2 * (rows * depth * len(tokens) + depth * width * count + rows * width * count * len(tokens)),
            transcendentals=0,
        ),
        name="token_products",
    )(*tokens, *weights)


def finish_kernel(
    line, plane, groups, seq_rows, chunk, place_ref, lengths_ref, act_ref, top_ref, gain_ref, *refs
):
    pieces = refs[: plane * len(groups)]
    passed_ref, local_ref, gain_out, held, back, copied = refs[plane * len(groups) :]
    blocks, rows, width = held.shape
    features = blocks * width
    z, q = place_ref[0], place_ref[1]
    copies = []
    for step in range(plane):
        owner_q = ahead(q, step, plane)
        for group_index, group in enumerate(groups):
            piece = pieces[step * len(groups) + group_index]
            for index, line_step in enumerate(group):
                owner_z = behind(z, line_step, line)
                copy = pltpu.make_async_copy(
                    piece.at[index], held.at[owner_z * plane + owner_q], copied.at[len(copies)]
                )
                copy.start()
                copies.append(copy)
    for copy in copies:
        copy.wait()
    for block in range(blocks):
        back[:, block * width : (block + 1) * width] = held[block].astype(jnp.float32)
    gain_row = gain_ref[...]
    total = jnp.zeros((1, features), jnp.float32)
    for start in range(0, rows, chunk):
        part = pl.ds(start, chunk)
        wide = act_ref[part, :].astype(jnp.float32)
        micro, first = divmod(start, seq_rows)
        position = lax.broadcasted_iota(jnp.int32, (chunk, 1), 0) + first
        keep = position < lengths_ref[micro]
        proj = jnp.where(keep, back[part, :], 0.0)
        inverse = lax.rsqrt(jnp.mean(wide * wide, axis=1, keepdims=True) + norm_epsilon)
        scaled = proj * gain_row
        pull = jnp.mean(wide * scaled, axis=1, keepdims=True)
        local = inverse * scaled - wide * (inverse * inverse * inverse * pull)
        local_ref[part, :] = local
        passed_ref[part, :] = (top_ref[part, :].astype(jnp.float32) + local).astype(jnp.bfloat16)
        total = total + jnp.sum(wide * inverse * proj, axis=0, keepdims=True)
    for block in range(blocks):
        gain_out[block : block + 1, :] = total[:, block * width : (block + 1) * width]


def finish(line, plane, groups, seq_rows, place, lengths, act, top, gain, pieces):
    rows, features = act.shape
    width = pieces[0].shape[2]
    blocks = line * plane
    chunk = math.gcd(seq_rows, 16)
    smem = pl.BlockSpec(memory_space=pltpu.SMEM)
    vmem = pl.BlockSpec(memory_space=pltpu.VMEM)
    return pl.pallas_call(
        functools.partial(finish_kernel, line, plane, groups, seq_rows, chunk),
        out_shape=[
            jax.ShapeDtypeStruct((rows, features), jnp.bfloat16),
            jax.ShapeDtypeStruct((rows, features), jnp.float32),
            jax.ShapeDtypeStruct((blocks, width), jnp.float32),
        ],
        in_specs=[smem, smem, vmem, vmem, vmem] + [pl.BlockSpec(memory_space=pl.ANY)] * len(pieces),
        out_specs=[vmem, vmem, vmem],
        scratch_shapes=[
            pltpu.VMEM((blocks, rows, width), jnp.bfloat16),
            pltpu.VMEM((rows, features), jnp.float32),
            pltpu.SemaphoreType.DMA((blocks,)),
        ],
        compiler_params=pltpu.CompilerParams(vmem_limit_bytes=vmem_bytes),
        cost_estimate=pl.CostEstimate(
            flops=16 * rows * features, bytes_accessed=12 * rows * features, transcendentals=rows
        ),
        name="norm_backward",
    )(place, lengths, act, top, gain, *pieces)


def on_device(activations, key_grads, top_grad, norm_gains, w_key, lengths):
    micro_count, seq_rows, features = activations.shape[2:]
    rows = micro_count * seq_rows
    replicas = lax.axis_size("dp")
    sections = lax.axis_size("section")
    plane = plane_size(replicas)
    line = replicas // plane
    grad_scale = 1.0 / math.sqrt(replicas * rows)
    me = lax.axis_index("dp")
    place = jnp.stack([me // plane, me % plane]).astype(jnp.int32)

    key_rows = key_grads.reshape(rows, key_grads.shape[-1])
    shard = w_key[0]
    tokens = [key_rows] + [along_plane(key_rows, step, line, plane) for step in range(1, plane)]
    weights = [shard] + [along_line(shard, step, line, plane) for step in range(1, line)]
    half = (line + 1) // 2
    groups = [tuple(range(half)), tuple(range(half, line))]
    sent = [products(tokens, [weights[step] for step in group]) for group in groups]
    pieces = []
    for step in range(plane):
        for group_products in sent:
            piece = group_products[step]
            pieces.append(piece if step == 0 else along_plane(piece, step, line, plane, back=True))
    passed, local, gain_blocks = finish(
        line,
        plane,
        groups,
        seq_rows,
        place,
        lengths[0],
        activations.reshape(rows, features),
        top_grad.reshape(rows, features),
        norm_gains,
        pieces,
    )
    gain_parts = lax.all_to_all(gain_blocks, "dp", split_axis=0, concat_axis=0, tiled=True)
    grad_shard = jnp.sum(gain_parts, axis=0) * grad_scale

    my_section = lax.axis_index("section")
    result = passed
    for turn in range(sections - 2, -1, -1):
        incoming = lax.ppermute(result, "section", [(turn + 1, turn)])
        result = jnp.where(
            my_section == turn, (incoming.astype(jnp.float32) + local).astype(jnp.bfloat16), result
        )
    return (result.reshape(activations.shape), grad_shard[None])


def solution(mesh):
    placed = (
        P("section", "dp", None, None, None),
        P("section", "dp", None, None, None),
        P("dp", None, None, None),
        P("section", None),
        P("section", "dp", None),
        P("dp", None),
    )
    return jax.shard_map(
        on_device,
        mesh=mesh,
        in_specs=placed,
        out_specs=(P("section", "dp", None, None, None), P("section", "dp")),
        check_vma=False,
    )
```

```python
import functools
import math

import jax
import jax.numpy as jnp
from jax import lax
from jax.experimental import pallas as pl
from jax.experimental.pallas import tpu as pltpu
from jax.sharding import PartitionSpec as P

norm_epsilon = 1e-05
vmem_bytes = 32 * 1024 * 1024


def plane_size(replicas):
    size = 1
    while (2 * size) ** 2 <= replicas and replicas % (2 * size) == 0:
        size *= 2
    return size


def ahead(place, step, count):
    if count & (count - 1) == 0:
        return place ^ step
    return (place + step) % count


def behind(place, step, count):
    if count & (count - 1) == 0:
        return place ^ step
    return (place + count - step) % count


def along_line(value, step, line, plane):
    pairs = [
        (z * plane + q, ahead(z, step, line) * plane + q)
        for z in range(line)
        for q in range(plane)
    ]
    return lax.ppermute(value, "dp", pairs)


def along_plane(value, step, line, plane, back=False):
    partner = behind if back else ahead
    pairs = [
        (z * plane + q, z * plane + partner(q, step, plane))
        for z in range(line)
        for q in range(plane)
    ]
    return lax.ppermute(value, "dp", pairs)


def product_kernel(token_count, weight_count, *refs):
    tokens = refs[:token_count]
    weights = refs[token_count : token_count + weight_count]
    outs = refs[token_count + weight_count :]
    for token_ref, out_ref in zip(tokens, outs):
        for index, weight_ref in enumerate(weights):
            out_ref[index] = lax.dot_general(
                token_ref[...],
                weight_ref[...],
                (((1,), (1,)), ((), ())),
                preferred_element_type=jnp.float32,
            ).astype(out_ref.dtype)


def products(tokens, weights):
    rows, depth = tokens[0].shape
    width = weights[0].shape[0]
    count = len(weights)
    return pl.pallas_call(
        functools.partial(product_kernel, len(tokens), count),
        out_shape=[jax.ShapeDtypeStruct((count, rows, width), jnp.bfloat16) for _ in tokens],
        in_specs=[pl.BlockSpec(memory_space=pltpu.VMEM)] * (len(tokens) + count),
        out_specs=[pl.BlockSpec(memory_space=pltpu.VMEM)] * len(tokens),
        compiler_params=pltpu.CompilerParams(vmem_limit_bytes=vmem_bytes),
        cost_estimate=pl.CostEstimate(
            flops=2 * rows * depth * width * count * len(tokens),
            bytes_accessed=2 * (rows * depth * len(tokens) + depth * width * count + rows * width * count * len(tokens)),
            transcendentals=0,
        ),
        name="token_products",
    )(*tokens, *weights)


def relative(owner, place, count):
    if count & (count - 1) == 0:
        return owner ^ place
    return (owner + count - place) % count


def column_tile(features, most=512):
    tile = 128
    for width in range(128, most + 1, 128):
        if features % width == 0:
            tile = width
    return tile


def inverse_kernel(seq_rows, chunk, tile, lengths_ref, act_ref, inverse_ref):
    rows, features = act_ref.shape

    def one_chunk(index, _):
        start = pl.multiple_of(index * chunk, chunk)
        part = pl.ds(start, chunk)
        squares = jnp.zeros((chunk, 128), jnp.float32)
        for left in range(0, features, tile):
            wide = act_ref[part, left : left + tile].astype(jnp.float32)
            wide = wide * wide
            for lane in range(0, tile, 128):
                squares = squares + wide[:, lane : lane + 128]
        mean = jnp.sum(squares, axis=1, keepdims=True) / features
        position = lax.broadcasted_iota(jnp.int32, (chunk, 1), 0) + lax.rem(start, seq_rows)
        keep = position < lengths_ref[lax.div(start, seq_rows)]
        inverse_ref[part, :] = jnp.where(keep, lax.rsqrt(mean + norm_epsilon), 0.0)
        return 0

    lax.fori_loop(0, rows // chunk, one_chunk, 0)


def live_inverse(seq_rows, lengths, act):
    rows, features = act.shape
    return pl.pallas_call(
        functools.partial(inverse_kernel, seq_rows, math.gcd(seq_rows, 16), column_tile(features)),
        out_shape=jax.ShapeDtypeStruct((rows, 1), jnp.float32),
        in_specs=[pl.BlockSpec(memory_space=pltpu.SMEM), pl.BlockSpec(memory_space=pltpu.VMEM)],
        out_specs=pl.BlockSpec(memory_space=pltpu.VMEM),
        compiler_params=pltpu.CompilerParams(vmem_limit_bytes=vmem_bytes),
        cost_estimate=pl.CostEstimate(
            flops=2 * rows * features, bytes_accessed=2 * rows * features, transcendentals=rows
        ),
        name="live_inverse",
    )(lengths, act)


def finish_kernel(line, plane, groups, chunk, tile, place_ref, inverse_ref, act_ref, top_ref, gain_ref, *refs):
    piece_count = plane * len(groups)
    pieces = refs[:piece_count]
    passed_ref, local_ref = refs[piece_count : piece_count + 2]
    gain_outs = refs[piece_count + 2 : piece_count + 2 + plane]
    held, back, gain_sum, gain_blocks = refs[piece_count + 2 + plane :]
    blocks, rows, width = held.shape
    features = blocks * width
    z, q = place_ref[0], place_ref[1]
    for step in range(plane):
        owner_q = ahead(q, step, plane)
        for group_index, group in enumerate(groups):
            piece = pieces[step * len(groups) + group_index]
            for index, line_step in enumerate(group):
                held[behind(z, line_step, line) * plane + owner_q] = piece[index]
    for block in range(blocks):
        back[:, block * width : (block + 1) * width] = held[block]
    gain_sum[...] = jnp.zeros_like(gain_sum)

    def one_chunk(index, _):
        part = pl.ds(pl.multiple_of(index * chunk, chunk), chunk)
        inverse = inverse_ref[part, :]
        pull = jnp.zeros((chunk, 128), jnp.float32)
        for left in range(0, features, tile):
            cols = slice(left, left + tile)
            both = act_ref[part, cols].astype(jnp.float32) * back[part, cols].astype(jnp.float32)
            gained = both * gain_ref[:, cols]
            for lane in range(0, tile, 128):
                pull = pull + gained[:, lane : lane + 128]
            both = both * inverse
            folded = both[:8, :]
            for row in range(8, chunk, 8):
                folded = folded + both[row : row + 8, :]
            gain_sum[:, cols] += folded
        pull = jnp.sum(pull, axis=1, keepdims=True) / features
        pull = pull * inverse * inverse * inverse
        for left in range(0, features, tile):
            cols = slice(left, left + tile)
            scaled = back[part, cols].astype(jnp.float32) * gain_ref[:, cols]
            local = inverse * scaled - act_ref[part, cols].astype(jnp.float32) * pull
            local_ref[part, cols] = local
            passed_ref[part, cols] = (top_ref[part, cols].astype(jnp.float32) + local).astype(jnp.bfloat16)
        return 0

    lax.fori_loop(0, rows // chunk, one_chunk, 0)
    total = jnp.sum(gain_sum[...], axis=0, keepdims=True)
    for block in range(blocks):
        owner_z, owner_q = divmod(block, plane)
        gain_blocks[
            relative(owner_q, q, plane), pl.ds(relative(owner_z, z, line), 1), :
        ] = total[:, block * width : (block + 1) * width]
    for step, gain_out in enumerate(gain_outs):
        gain_out[...] = gain_blocks[step]


def finish(line, plane, groups, place, inverse, act, top, gain, pieces):
    rows, features = act.shape
    width = pieces[0].shape[2]
    blocks = line * plane
    smem = pl.BlockSpec(memory_space=pltpu.SMEM)
    vmem = pl.BlockSpec(memory_space=pltpu.VMEM)
    return pl.pallas_call(
        functools.partial(finish_kernel, line, plane, groups, 16, column_tile(features)),
        out_shape=[
            jax.ShapeDtypeStruct((rows, features), jnp.bfloat16),
            jax.ShapeDtypeStruct((rows, features), jnp.float32),
        ]
        + [jax.ShapeDtypeStruct((line, width), jnp.float32)] * plane,
        in_specs=[smem] + [vmem] * (4 + len(pieces)),
        out_specs=[vmem] * (2 + plane),
        scratch_shapes=[
            pltpu.VMEM((blocks, rows, width), jnp.bfloat16),
            pltpu.VMEM((rows, features), jnp.bfloat16),
            pltpu.VMEM((8, features), jnp.float32),
            pltpu.VMEM((plane, line, width), jnp.float32),
        ],
        compiler_params=pltpu.CompilerParams(vmem_limit_bytes=vmem_bytes),
        cost_estimate=pl.CostEstimate(
            flops=16 * rows * features, bytes_accessed=12 * rows * features, transcendentals=0
        ),
        name="norm_backward",
    )(place, inverse, act, top, gain, *pieces)


def sum_kernel(scale, *refs):
    ins = refs[:-1] if scale is not None else refs[: len(refs) - refs[0].shape[0]]
    total = ins[0][...]
    for ref in ins[1:]:
        total = total + ref[...]
    if scale is None:
        for row, out in enumerate(refs[len(ins) :]):
            out[...] = total[row : row + 1, :]
    else:
        refs[-1][...] = total * scale


def sum_rows(parts):
    count, width = parts[0].shape
    vmem = pl.BlockSpec(memory_space=pltpu.VMEM)
    return pl.pallas_call(
        functools.partial(sum_kernel, None),
        out_shape=[jax.ShapeDtypeStruct((1, width), jnp.float32)] * count,
        in_specs=[vmem] * len(parts),
        out_specs=[vmem] * count,
        name="sum_rows",
    )(*parts)


def sum_scaled(parts, scale):
    vmem = pl.BlockSpec(memory_space=pltpu.VMEM)
    return pl.pallas_call(
        functools.partial(sum_kernel, scale),
        out_shape=jax.ShapeDtypeStruct(parts[0].shape, jnp.float32),
        in_specs=[vmem] * len(parts),
        out_specs=vmem,
        name="sum_scaled",
    )(*parts)


def hand_kernel(turn, chunk, tile, section_ref, incoming_ref, local_ref, result_ref, out_ref, staged, copied):
    rows, features = local_ref.shape
    count = rows // chunk
    is_turn = section_ref[0] == turn
    copies = [
        pltpu.make_async_copy(
            staged.at[pl.ds(index * chunk, chunk)], out_ref.at[pl.ds(index * chunk, chunk)], copied.at[index]
        )
        for index in range(count)
    ]
    for index in range(count):

        @pl.when(is_turn)
        def _():
            def one_part(step, _):
                part = pl.ds(pl.multiple_of(index * chunk + step * 16, 16), 16)
                for left in range(0, features, tile):
                    cols = slice(left, left + tile)
                    staged[part, cols] = (
                        incoming_ref[part, cols].astype(jnp.float32) + local_ref[part, cols]
                    ).astype(jnp.bfloat16)
                return 0

            lax.fori_loop(0, chunk // 16, one_part, 0)

        @pl.when(jnp.logical_not(is_turn))
        def _():
            part = pl.ds(index * chunk, chunk)
            staged[part, :] = result_ref[part, :]

        copies[index].start()
    for copy in copies:
        copy.wait()


def hand_on(turn, chunk, my_section, incoming, local, result):
    rows, features = local.shape
    vmem = pl.BlockSpec(memory_space=pltpu.VMEM)
    return pl.pallas_call(
        functools.partial(hand_kernel, turn, chunk, column_tile(features)),
        out_shape=jax.ShapeDtypeStruct((rows, features), jnp.bfloat16),
        in_specs=[pl.BlockSpec(memory_space=pltpu.SMEM), vmem, vmem, vmem],
        out_specs=pl.BlockSpec(memory_space=pl.ANY),
        scratch_shapes=[
            pltpu.VMEM((rows, features), jnp.bfloat16),
            pltpu.SemaphoreType.DMA((rows // chunk,)),
        ],
        compiler_params=pltpu.CompilerParams(vmem_limit_bytes=vmem_bytes),
        cost_estimate=pl.CostEstimate(
            flops=rows * features, bytes_accessed=8 * rows * features, transcendentals=0
        ),
        name="hand_on",
    )(my_section, incoming, local, result)


def gathered_along_line(shard, line, plane):
    if line & (line - 1):
        return [shard] + [along_line(shard, step, line, plane) for step in range(1, line)]
    held = {0: shard}
    distance = line // 2
    while distance:
        for step in list(held):
            held[step + distance] = along_line(held[step], distance, line, plane)
        distance //= 2
    return [held[step] for step in range(line)]


def send_groups(line):
    if line & (line - 1) or line == 1:
        half = (line + 1) // 2
        return [group for group in (tuple(range(half)), tuple(range(half, line))) if group]
    if line == 2:
        return [(0,), (1,)]
    quarter = line // 4
    return [
        tuple(range(0, 2 * quarter)),
        tuple(range(2 * quarter, 3 * quarter)),
        tuple(range(3 * quarter, line)),
    ]


def on_device(activations, key_grads, top_grad, norm_gains, w_key, lengths):
    micro_count, seq_rows, features = activations.shape[2:]
    rows = micro_count * seq_rows
    replicas = lax.axis_size("dp")
    sections = lax.axis_size("section")
    plane = plane_size(replicas)
    line = replicas // plane
    grad_scale = 1.0 / math.sqrt(replicas * rows)
    me = lax.axis_index("dp")
    place = jnp.stack([lax.div(me, plane), lax.rem(me, plane)]).astype(jnp.int32)
    act = activations.reshape(rows, features)

    key_rows = key_grads.reshape(rows, key_grads.shape[-1])
    weights = gathered_along_line(w_key[0], line, plane)
    tokens = [key_rows] + [along_plane(key_rows, step, line, plane) for step in range(1, plane)]
    inverse = live_inverse(seq_rows, lengths[0], act)
    groups = send_groups(line)
    sent = [products(tokens, [weights[step] for step in group]) for group in groups]
    pieces = []
    for step in range(plane):
        for group_products in sent:
            piece = group_products[step]
            pieces.append(piece if step == 0 else along_plane(piece, step, line, plane, back=True))
    passed, local, *gain_parts = finish(
        line, plane, groups, place, inverse, act, top_grad.reshape(rows, features), norm_gains, pieces
    )

    my_section = lax.axis_index("section").astype(jnp.int32).reshape(1)
    result = passed
    for turn in range(sections - 2, -1, -1):
        incoming = lax.ppermute(result, "section", [(turn + 1, turn)])
        result = hand_on(turn, seq_rows, my_section, incoming, local, result)

    in_plane = [gain_parts[0]] + [
        along_plane(gain_parts[step], step, line, plane) for step in range(1, plane)
    ]
    line_parts = sum_rows(in_plane)
    in_line = [line_parts[0]] + [
        along_line(line_parts[step], step, line, plane) for step in range(1, line)
    ]
    grad_shard = sum_scaled(in_line, grad_scale)
    return (result.reshape(activations.shape), grad_shard)


def solution(mesh):
    placed = (
        P("section", "dp", None, None, None),
        P("section", "dp", None, None, None),
        P("dp", None, None, None),
        P("section", None),
        P("section", "dp", None),
        P("dp", None),
    )
    return jax.shard_map(
        on_device,
        mesh=mesh,
        in_specs=placed,
        out_specs=(P("section", "dp", None, None, None), P("section", "dp")),
        check_vma=False,
    )
```

```python
import functools
import math

import jax
import jax.numpy as jnp
from jax import lax
from jax.experimental import pallas as pl
from jax.experimental.pallas import tpu as pltpu
from jax.sharding import PartitionSpec as P

norm_epsilon = 1e-05
mebibyte = 1024 * 1024


def grant(*arrays):
    total = 4 * mebibyte
    for array in arrays:
        lanes = -(-array.shape[-1] // 128) * 128
        total += math.prod(array.shape[:-1]) * lanes * jnp.dtype(array.dtype).itemsize
    return -(-total // mebibyte) * mebibyte


def plane_size(replicas):
    size = 1
    while (2 * size) ** 2 <= replicas and replicas % (2 * size) == 0:
        size *= 2
    return size


def ahead(place, step, count):
    if count & (count - 1) == 0:
        return place ^ step
    return (place + step) % count


def behind(place, step, count):
    if count & (count - 1) == 0:
        return place ^ step
    return (place + count - step) % count


def along_line(value, step, line, plane):
    pairs = [
        (z * plane + q, ahead(z, step, line) * plane + q)
        for z in range(line)
        for q in range(plane)
    ]
    return lax.ppermute(value, "dp", pairs)


def along_plane(value, step, line, plane, back=False):
    partner = behind if back else ahead
    pairs = [
        (z * plane + q, z * plane + partner(q, step, plane))
        for z in range(line)
        for q in range(plane)
    ]
    return lax.ppermute(value, "dp", pairs)


def product_kernel(token_count, weight_count, *refs):
    tokens = refs[:token_count]
    weights = refs[token_count : token_count + weight_count]
    outs = refs[token_count + weight_count :]
    for token_ref, out_ref in zip(tokens, outs):
        for index, weight_ref in enumerate(weights):
            out_ref[index] = lax.dot_general(
                token_ref[...],
                weight_ref[...],
                (((1,), (1,)), ((), ())),
                preferred_element_type=jnp.float32,
            ).astype(out_ref.dtype)


def products(tokens, weights):
    rows, depth = tokens[0].shape
    width = weights[0].shape[0]
    count = len(weights)
    outs = [jax.ShapeDtypeStruct((count, rows, width), jnp.bfloat16) for _ in tokens]
    return pl.pallas_call(
        functools.partial(product_kernel, len(tokens), count),
        out_shape=outs,
        in_specs=[pl.BlockSpec(memory_space=pltpu.VMEM)] * (len(tokens) + count),
        out_specs=[pl.BlockSpec(memory_space=pltpu.VMEM)] * len(tokens),
        compiler_params=pltpu.CompilerParams(vmem_limit_bytes=grant(*tokens, *weights, *outs)),
        cost_estimate=pl.CostEstimate(
            flops=2 * rows * depth * width * count * len(tokens),
            bytes_accessed=2 * (rows * depth * len(tokens) + depth * width * count + rows * width * count * len(tokens)),
            transcendentals=0,
        ),
        name="token_products",
    )(*tokens, *weights)


def column_tile(features, most=512):
    tile = 128
    for width in range(128, most + 1, 128):
        if features % width == 0:
            tile = width
    return tile


def inverse_kernel(seq_rows, chunk, tile, lengths_ref, act_ref, inverse_ref):
    rows, features = act_ref.shape

    def one_chunk(index, _):
        start = pl.multiple_of(index * chunk, chunk)
        part = pl.ds(start, chunk)
        squares = jnp.zeros((chunk, 128), jnp.float32)
        for left in range(0, features, tile):
            wide = act_ref[part, left : left + tile].astype(jnp.float32)
            wide = wide * wide
            for lane in range(0, tile, 128):
                squares = squares + wide[:, lane : lane + 128]
        mean = jnp.sum(squares, axis=1, keepdims=True) / features
        position = lax.broadcasted_iota(jnp.int32, (chunk, 1), 0) + lax.rem(start, seq_rows)
        keep = position < lengths_ref[lax.div(start, seq_rows)]
        inverse_ref[part, :] = jnp.where(keep, lax.rsqrt(mean + norm_epsilon), 0.0)
        return 0

    lax.fori_loop(0, rows // chunk, one_chunk, 0)


def live_inverse(seq_rows, lengths, act):
    rows, features = act.shape
    return pl.pallas_call(
        functools.partial(inverse_kernel, seq_rows, math.gcd(seq_rows, 16), column_tile(features)),
        out_shape=jax.ShapeDtypeStruct((rows, 1), jnp.float32),
        in_specs=[pl.BlockSpec(memory_space=pltpu.SMEM), pl.BlockSpec(memory_space=pltpu.VMEM)],
        out_specs=pl.BlockSpec(memory_space=pltpu.VMEM),
        compiler_params=pltpu.CompilerParams(vmem_limit_bytes=grant(act)),
        cost_estimate=pl.CostEstimate(
            flops=2 * rows * features, bytes_accessed=2 * rows * features, transcendentals=rows
        ),
        name="live_inverse",
    )(lengths, act)


def finish_kernel(line, plane, groups, chunk, tile, place_ref, inverse_ref, act_ref, top_ref, gain_ref, *refs):
    piece_count = plane * len(groups)
    pieces = refs[:piece_count]
    passed_ref, local_ref, gain_out, held, back, gain_sum, pulls = refs[piece_count:]
    blocks, rows, width = held.shape
    features = blocks * width
    z, q = place_ref[0], place_ref[1]
    for step in range(plane):
        owner_q = ahead(q, step, plane)
        for group_index, group in enumerate(groups):
            piece = pieces[step * len(groups) + group_index]
            for index, line_step in enumerate(group):
                held[behind(z, line_step, line) * plane + owner_q] = piece[index]
    for block in range(blocks):
        back[:, block * width : (block + 1) * width] = held[block]
    gain_sum[...] = jnp.zeros_like(gain_sum)

    def sums(index, _):
        part = pl.ds(pl.multiple_of(index * chunk, chunk), chunk)
        inverse = inverse_ref[part, :]
        pull = jnp.zeros((chunk, 128), jnp.float32)
        for left in range(0, features, tile):
            cols = slice(left, left + tile)
            both = act_ref[part, cols].astype(jnp.float32) * back[part, cols].astype(jnp.float32)
            gained = both * gain_ref[:, cols]
            for lane in range(0, tile, 128):
                pull = pull + gained[:, lane : lane + 128]
            both = both * inverse
            folded = both[:8, :]
            for row in range(8, chunk, 8):
                folded = folded + both[row : row + 8, :]
            gain_sum[:, cols] += folded
        pulls[part, :] = pull
        return 0

    lax.fori_loop(0, rows // chunk, sums, 0)
    total = jnp.sum(gain_sum[...], axis=0, keepdims=True)
    for block in range(blocks):
        gain_out[block] = total[:, block * width : (block + 1) * width]
    inverse = inverse_ref[...]
    pull = jnp.sum(pulls[...], axis=1, keepdims=True) / features
    pulls[...] = jnp.broadcast_to(pull * inverse * inverse * inverse, pulls.shape)

    def terms(index, _):
        part = pl.ds(pl.multiple_of(index * chunk, chunk), chunk)
        inverse = inverse_ref[part, :]
        pull = pulls[part, :1]
        for left in range(0, features, tile):
            cols = slice(left, left + tile)
            scaled = back[part, cols].astype(jnp.float32) * gain_ref[:, cols]
            local = inverse * scaled - act_ref[part, cols].astype(jnp.float32) * pull
            local_ref[part, cols] = local
            passed_ref[part, cols] = (top_ref[part, cols].astype(jnp.float32) + local).astype(jnp.bfloat16)
        return 0

    lax.fori_loop(0, rows // chunk, terms, 0)


def finish(line, plane, groups, place, inverse, act, top, gain, pieces):
    rows, features = act.shape
    width = pieces[0].shape[2]
    blocks = line * plane
    smem = pl.BlockSpec(memory_space=pltpu.SMEM)
    vmem = pl.BlockSpec(memory_space=pltpu.VMEM)
    outs = [
        jax.ShapeDtypeStruct((rows, features), jnp.bfloat16),
        jax.ShapeDtypeStruct((rows, features), jnp.float32),
        jax.ShapeDtypeStruct((blocks, 1, width), jnp.float32),
    ]
    scratch = [
        pltpu.VMEM((blocks, rows, width), jnp.bfloat16),
        pltpu.VMEM((rows, features), jnp.bfloat16),
        pltpu.VMEM((8, features), jnp.float32),
        pltpu.VMEM((rows, 128), jnp.float32),
    ]
    return pl.pallas_call(
        functools.partial(finish_kernel, line, plane, groups, 16, column_tile(features)),
        out_shape=outs,
        in_specs=[smem] + [vmem] * (4 + len(pieces)),
        out_specs=[vmem] * len(outs),
        scratch_shapes=scratch,
        compiler_params=pltpu.CompilerParams(
            vmem_limit_bytes=grant(act, top, *pieces, *outs, *scratch)
        ),
        cost_estimate=pl.CostEstimate(
            flops=16 * rows * features, bytes_accessed=12 * rows * features, transcendentals=0
        ),
        name="norm_backward",
    )(place, inverse, act, top, gain, *pieces)


def hand_kernel(turn, chunk, tile, section_ref, incoming_ref, local_ref, result_ref, out_ref, staged, copied):
    rows, features = local_ref.shape
    count = rows // chunk
    is_turn = section_ref[0] == turn
    copies = [
        pltpu.make_async_copy(
            staged.at[pl.ds(index * chunk, chunk)], out_ref.at[pl.ds(index * chunk, chunk)], copied.at[index]
        )
        for index in range(count)
    ]
    for index in range(count):

        @pl.when(is_turn)
        def _():
            def one_part(step, _):
                part = pl.ds(pl.multiple_of(index * chunk + step * 16, 16), 16)
                for left in range(0, features, tile):
                    cols = slice(left, left + tile)
                    staged[part, cols] = (
                        incoming_ref[part, cols].astype(jnp.float32) + local_ref[part, cols]
                    ).astype(jnp.bfloat16)
                return 0

            lax.fori_loop(0, chunk // 16, one_part, 0)

        @pl.when(jnp.logical_not(is_turn))
        def _():
            part = pl.ds(index * chunk, chunk)
            staged[part, :] = result_ref[part, :]

        copies[index].start()
    for copy in copies:
        copy.wait()


def hand_on(turn, chunk, my_section, incoming, local, result):
    rows, features = local.shape
    vmem = pl.BlockSpec(memory_space=pltpu.VMEM)
    return pl.pallas_call(
        functools.partial(hand_kernel, turn, chunk, column_tile(features)),
        out_shape=jax.ShapeDtypeStruct((rows, features), jnp.bfloat16),
        in_specs=[pl.BlockSpec(memory_space=pltpu.SMEM), vmem, vmem, vmem],
        out_specs=pl.BlockSpec(memory_space=pl.ANY),
        scratch_shapes=[
            pltpu.VMEM((rows, features), jnp.bfloat16),
            pltpu.SemaphoreType.DMA((rows // chunk,)),
        ],
        compiler_params=pltpu.CompilerParams(vmem_limit_bytes=grant(incoming, local, result, result)),
        cost_estimate=pl.CostEstimate(
            flops=rows * features, bytes_accessed=8 * rows * features, transcendentals=0
        ),
        name="hand_on",
    )(my_section, incoming, local, result)


def gathered_products(tokens, shard, line, plane):
    if line & (line - 1) or line < 4:
        held = [shard] + [along_line(shard, step, line, plane) for step in range(1, line)]
        half = (line + 1) // 2
        groups = [group for group in (tuple(range(half)), tuple(range(half, line))) if group]
        return groups, [products(tokens, [held[step] for step in group]) for group in groups]
    held = {0: shard}
    distance = line // 2
    while distance:
        held[distance] = along_line(shard, distance, line, plane)
        distance //= 2
    early = tuple(sorted(held))
    distance = line // 4
    while distance:
        for step in sorted(held):
            if step % (2 * distance) == 0 and step and step + distance not in held:
                held[step + distance] = along_line(held[step], distance, line, plane)
        distance //= 2
    late = tuple(step for step in range(line) if step not in early)
    groups = [early, late]
    return groups, [products(tokens, [held[step] for step in group]) for group in groups]


def on_device(activations, key_grads, top_grad, norm_gains, w_key, lengths):
    micro_count, seq_rows, features = activations.shape[2:]
    rows = micro_count * seq_rows
    replicas = lax.axis_size("dp")
    sections = lax.axis_size("section")
    plane = plane_size(replicas)
    line = replicas // plane
    grad_scale = 1.0 / math.sqrt(replicas * rows)
    me = lax.axis_index("dp")
    place = jnp.stack([lax.div(me, plane), lax.rem(me, plane)]).astype(jnp.int32)
    act = activations.reshape(rows, features)

    key_rows = key_grads.reshape(rows, key_grads.shape[-1])
    inverse, own_rows = lax.optimization_barrier((live_inverse(seq_rows, lengths[0], act), key_rows))
    tokens = [own_rows] + [along_plane(key_rows, step, line, plane) for step in range(1, plane)]
    groups, sent = gathered_products(tokens, w_key[0], line, plane)
    pieces = []
    for step in range(plane):
        for group_products in sent:
            piece = group_products[step]
            pieces.append(piece if step == 0 else along_plane(piece, step, line, plane, back=True))
    passed, local, gain_blocks = finish(
        line, plane, groups, place, inverse, act, top_grad.reshape(rows, features), norm_gains, pieces
    )

    my_section = lax.axis_index("section").astype(jnp.int32).reshape(1)
    result = passed
    for turn in range(sections - 2, -1, -1):
        incoming = lax.ppermute(result, "section", [(turn + 1, turn)])
        result = hand_on(turn, seq_rows, my_section, incoming, local, result)

    gain_parts = lax.all_to_all(gain_blocks, "dp", split_axis=0, concat_axis=0, tiled=True)
    grad_shard = jnp.sum(gain_parts, axis=0) * grad_scale
    return (result.reshape(activations.shape), grad_shard)


def solution(mesh):
    placed = (
        P("section", "dp", None, None, None),
        P("section", "dp", None, None, None),
        P("dp", None, None, None),
        P("section", None),
        P("section", "dp", None),
        P("dp", None),
    )
    return jax.shard_map(
        on_device,
        mesh=mesh,
        in_specs=placed,
        out_specs=(P("section", "dp", None, None, None), P("section", "dp")),
        check_vma=False,
    )
```

```python
import functools
import math

import jax
import jax.numpy as jnp
from jax import lax
from jax.experimental import pallas as pl
from jax.experimental.pallas import tpu as pltpu
from jax.sharding import PartitionSpec as P

norm_epsilon = 1e-05
mebibyte = 1024 * 1024


def grant(*arrays):
    total = 4 * mebibyte
    for array in arrays:
        lanes = -(-array.shape[-1] // 128) * 128
        total += math.prod(array.shape[:-1]) * lanes * jnp.dtype(array.dtype).itemsize
    return -(-total // mebibyte) * mebibyte


def plane_size(replicas):
    size = 1
    while (2 * size) ** 2 <= replicas and replicas % (2 * size) == 0:
        size *= 2
    return size


def ahead(place, step, count):
    if count & (count - 1) == 0:
        return place ^ step
    return (place + step) % count


def behind(place, step, count):
    if count & (count - 1) == 0:
        return place ^ step
    return (place + count - step) % count


def along_line(value, step, line, plane):
    pairs = [
        (z * plane + q, ahead(z, step, line) * plane + q)
        for z in range(line)
        for q in range(plane)
    ]
    return lax.ppermute(value, "dp", pairs)


def along_plane(value, step, line, plane, back=False):
    partner = behind if back else ahead
    pairs = [
        (z * plane + q, z * plane + partner(q, step, plane))
        for z in range(line)
        for q in range(plane)
    ]
    return lax.ppermute(value, "dp", pairs)


def product_kernel(token_count, weight_count, seq_rows, *refs):
    tokens = refs[:token_count]
    weights = refs[token_count : token_count + weight_count]
    outs = refs[token_count + weight_count :]
    for token_ref, out_ref in zip(tokens, outs):
        for index, weight_ref in enumerate(weights):
            product = lax.dot_general(
                token_ref[...],
                weight_ref[...],
                (((1,), (1,)), ((), ())),
                preferred_element_type=jnp.float32,
            ).astype(out_ref.dtype)
            width = product.shape[1]
            for micro in range(product.shape[0] // seq_rows):
                out_ref[index, :, micro * width : (micro + 1) * width] = product[
                    micro * seq_rows : (micro + 1) * seq_rows, :
                ]


def products(seq_rows, tokens, weights):
    rows, depth = tokens[0].shape
    width = weights[0].shape[0]
    count = len(weights)
    folded = (count, seq_rows, rows // seq_rows * width)
    outs = [jax.ShapeDtypeStruct(folded, jnp.bfloat16) for _ in tokens]
    return pl.pallas_call(
        functools.partial(product_kernel, len(tokens), count, seq_rows),
        out_shape=outs,
        in_specs=[pl.BlockSpec(memory_space=pltpu.VMEM)] * (len(tokens) + count),
        out_specs=[pl.BlockSpec(memory_space=pltpu.VMEM)] * len(tokens),
        compiler_params=pltpu.CompilerParams(vmem_limit_bytes=grant(*tokens, *weights, *outs)),
        cost_estimate=pl.CostEstimate(
            flops=2 * rows * depth * width * count * len(tokens),
            bytes_accessed=2 * (rows * depth * len(tokens) + depth * width * count + rows * width * count * len(tokens)),
            transcendentals=0,
        ),
        name="token_products",
    )(*tokens, *weights)


def column_tile(features, most=512):
    tile = 128
    for width in range(128, most + 1, 128):
        if features % width == 0:
            tile = width
    return tile


def inverse_kernel(seq_rows, chunk, tile, lengths_ref, act_ref, inverse_ref):
    rows, features = act_ref.shape

    def one_chunk(index, _):
        start = pl.multiple_of(index * chunk, chunk)
        part = pl.ds(start, chunk)
        squares = jnp.zeros((chunk, 128), jnp.float32)
        for left in range(0, features, tile):
            wide = act_ref[part, left : left + tile].astype(jnp.float32)
            wide = wide * wide
            for lane in range(0, tile, 128):
                squares = squares + wide[:, lane : lane + 128]
        mean = jnp.sum(squares, axis=1, keepdims=True) / features
        position = lax.broadcasted_iota(jnp.int32, (chunk, 1), 0) + lax.rem(start, seq_rows)
        keep = position < lengths_ref[lax.div(start, seq_rows)]
        inverse_ref[part, :] = jnp.where(keep, lax.rsqrt(mean + norm_epsilon), 0.0)
        return 0

    lax.fori_loop(0, rows // chunk, one_chunk, 0)


def live_inverse(seq_rows, lengths, act):
    rows, features = act.shape
    return pl.pallas_call(
        functools.partial(inverse_kernel, seq_rows, math.gcd(seq_rows, 16), column_tile(features)),
        out_shape=jax.ShapeDtypeStruct((rows, 1), jnp.float32),
        in_specs=[pl.BlockSpec(memory_space=pltpu.SMEM), pl.BlockSpec(memory_space=pltpu.VMEM)],
        out_specs=pl.BlockSpec(memory_space=pltpu.VMEM),
        compiler_params=pltpu.CompilerParams(vmem_limit_bytes=grant(act)),
        cost_estimate=pl.CostEstimate(
            flops=2 * rows * features, bytes_accessed=2 * rows * features, transcendentals=rows
        ),
        name="live_inverse",
    )(lengths, act)


def finish_kernel(line, plane, groups, seq_rows, chunk, tile, inverse_ref, act_ref, top_ref, gain_ref, *refs):
    piece_count = plane * len(groups)
    pieces = refs[:piece_count]
    passed_ref, local_ref, gain_out, held, back, gain_sum, pulls = refs[piece_count:]
    rows, features = back.shape
    width = features // (line * plane)
    me = lax.axis_index("dp")
    z, q = lax.div(me, plane), lax.rem(me, plane)
    for step in range(plane):
        owner_q = ahead(q, step, plane)
        for group_index, group in enumerate(groups):
            piece = pieces[step * len(groups) + group_index]
            for index, line_step in enumerate(group):
                held[behind(z, line_step, line) * plane + owner_q] = piece[index]
    for micro in range(rows // seq_rows):
        for block in range(line * plane):
            back[micro * seq_rows : (micro + 1) * seq_rows, block * width : (block + 1) * width] = held[
                block, :, micro * width : (micro + 1) * width
            ]
    gain_sum[...] = jnp.zeros_like(gain_sum)

    def sums(index, _):
        part = pl.ds(pl.multiple_of(index * chunk, chunk), chunk)
        inverse = inverse_ref[part, :]
        pull = jnp.zeros((chunk, 128), jnp.float32)
        for left in range(0, features, tile):
            cols = slice(left, left + tile)
            both = act_ref[part, cols].astype(jnp.float32) * back[part, cols].astype(jnp.float32)
            gained = both * gain_ref[:, cols]
            for lane in range(0, tile, 128):
                pull = pull + gained[:, lane : lane + 128]
            both = both * inverse
            folded = both[:8, :]
            for row in range(8, chunk, 8):
                folded = folded + both[row : row + 8, :]
            gain_sum[:, cols] += folded
        pulls[part, :] = pull
        return 0

    lax.fori_loop(0, rows // chunk, sums, 0)
    total = jnp.sum(gain_sum[...], axis=0, keepdims=True)
    for block in range(line * plane):
        gain_out[block] = total[:, block * width : (block + 1) * width]
    inverse = inverse_ref[...]
    pull = jnp.sum(pulls[...], axis=1, keepdims=True) / features
    pulls[...] = jnp.broadcast_to(pull * inverse * inverse * inverse, pulls.shape)

    def terms(index, _):
        part = pl.ds(pl.multiple_of(index * chunk, chunk), chunk)
        inverse = inverse_ref[part, :]
        pull = pulls[part, :1]
        for left in range(0, features, tile):
            cols = slice(left, left + tile)
            scaled = back[part, cols].astype(jnp.float32) * gain_ref[:, cols]
            local = inverse * scaled - act_ref[part, cols].astype(jnp.float32) * pull
            local_ref[part, cols] = local
            passed_ref[part, cols] = (top_ref[part, cols].astype(jnp.float32) + local).astype(jnp.bfloat16)
        return 0

    lax.fori_loop(0, rows // chunk, terms, 0)


def finish(line, plane, groups, seq_rows, inverse, act, top, gain, pieces):
    rows, features = act.shape
    blocks = line * plane
    vmem = pl.BlockSpec(memory_space=pltpu.VMEM)
    outs = [
        jax.ShapeDtypeStruct((rows, features), jnp.bfloat16),
        jax.ShapeDtypeStruct((rows, features), jnp.float32),
        jax.ShapeDtypeStruct((blocks, 1, features // blocks), jnp.float32),
    ]
    scratch = [
        pltpu.VMEM((blocks,) + pieces[0].shape[1:], jnp.bfloat16),
        pltpu.VMEM((rows, features), jnp.bfloat16),
        pltpu.VMEM((8, features), jnp.float32),
        pltpu.VMEM((rows, 128), jnp.float32),
    ]
    return pl.pallas_call(
        functools.partial(finish_kernel, line, plane, groups, seq_rows, 16, column_tile(features)),
        out_shape=outs,
        in_specs=[vmem] * (4 + len(pieces)),
        out_specs=[vmem] * len(outs),
        scratch_shapes=scratch,
        compiler_params=pltpu.CompilerParams(
            vmem_limit_bytes=grant(act, top, *pieces, *outs, *scratch)
        ),
        cost_estimate=pl.CostEstimate(
            flops=16 * rows * features, bytes_accessed=12 * rows * features, transcendentals=0
        ),
        name="norm_backward",
    )(inverse, act, top, gain, *pieces)


def hand_kernel(turn, chunk, tile, incoming_ref, local_ref, result_ref, out_ref, staged, copied):
    rows, features = local_ref.shape
    count = rows // chunk
    is_turn = lax.axis_index("section") == turn
    copies = [
        pltpu.make_async_copy(
            staged.at[pl.ds(index * chunk, chunk)], out_ref.at[pl.ds(index * chunk, chunk)], copied.at[index]
        )
        for index in range(count)
    ]
    for index in range(count):

        @pl.when(is_turn)
        def _():
            def one_part(step, _):
                part = pl.ds(pl.multiple_of(index * chunk + step * 16, 16), 16)
                for left in range(0, features, tile):
                    cols = slice(left, left + tile)
                    staged[part, cols] = (
                        incoming_ref[part, cols].astype(jnp.float32) + local_ref[part, cols]
                    ).astype(jnp.bfloat16)
                return 0

            lax.fori_loop(0, chunk // 16, one_part, 0)

        @pl.when(jnp.logical_not(is_turn))
        def _():
            part = pl.ds(index * chunk, chunk)
            staged[part, :] = result_ref[part, :]

        copies[index].start()
    for copy in copies:
        copy.wait()


def hand_on(turn, chunk, incoming, local, result):
    rows, features = local.shape
    vmem = pl.BlockSpec(memory_space=pltpu.VMEM)
    return pl.pallas_call(
        functools.partial(hand_kernel, turn, chunk, column_tile(features)),
        out_shape=jax.ShapeDtypeStruct((rows, features), jnp.bfloat16),
        in_specs=[vmem, vmem, vmem],
        out_specs=pl.BlockSpec(memory_space=pl.ANY),
        scratch_shapes=[
            pltpu.VMEM((rows, features), jnp.bfloat16),
            pltpu.SemaphoreType.DMA((rows // chunk,)),
        ],
        compiler_params=pltpu.CompilerParams(vmem_limit_bytes=grant(incoming, local, result, result)),
        cost_estimate=pl.CostEstimate(
            flops=rows * features, bytes_accessed=8 * rows * features, transcendentals=0
        ),
        name="hand_on",
    )(incoming, local, result)


def sum_kernel(scale, parts_ref, out_ref):
    total = parts_ref[0]
    for index in range(1, parts_ref.shape[0]):
        total = total + parts_ref[index]
    out_ref[...] = total * scale


def sum_scaled(parts, scale):
    vmem = pl.BlockSpec(memory_space=pltpu.VMEM)
    return pl.pallas_call(
        functools.partial(sum_kernel, scale),
        out_shape=jax.ShapeDtypeStruct(parts.shape[1:], jnp.float32),
        in_specs=[vmem],
        out_specs=vmem,
        compiler_params=pltpu.CompilerParams(vmem_limit_bytes=mebibyte),
        cost_estimate=pl.CostEstimate(flops=parts.size, bytes_accessed=4 * parts.size, transcendentals=0),
        name="sum_scaled",
    )(parts)


def gathered_products(seq_rows, tokens, shard, line, plane):
    if line & (line - 1) or line < 4:
        held = [shard] + [along_line(shard, step, line, plane) for step in range(1, line)]
        half = (line + 1) // 2
        groups = [group for group in (tuple(range(half)), tuple(range(half, line))) if group]
        return groups, [products(seq_rows, tokens, [held[step] for step in group]) for group in groups]
    held = {0: shard}
    distance = line // 2
    while distance:
        held[distance] = along_line(shard, distance, line, plane)
        distance //= 2
    early = tuple(sorted(held))
    distance = line // 4
    while distance:
        for step in sorted(held):
            if step % (2 * distance) == 0 and step and step + distance not in held:
                held[step + distance] = along_line(held[step], distance, line, plane)
        distance //= 2
    late = tuple(step for step in range(line) if step not in early)
    groups = [early, late]
    return groups, [products(seq_rows, tokens, [held[step] for step in group]) for group in groups]


def on_device(activations, key_grads, top_grad, norm_gains, w_key, lengths):
    micro_count, seq_rows, features = activations.shape[2:]
    rows = micro_count * seq_rows
    replicas = lax.axis_size("dp")
    sections = lax.axis_size("section")
    plane = plane_size(replicas)
    line = replicas // plane
    grad_scale = 1.0 / math.sqrt(replicas * rows)
    act = activations.reshape(rows, features)

    key_rows = key_grads.reshape(rows, key_grads.shape[-1])
    inverse, own_rows = lax.optimization_barrier((live_inverse(seq_rows, lengths[0], act), key_rows))
    tokens = [own_rows] + [along_plane(key_rows, step, line, plane) for step in range(1, plane)]
    groups, sent = gathered_products(seq_rows, tokens, w_key[0], line, plane)
    pieces = []
    for step in range(plane):
        for group_products in sent:
            piece = group_products[step]
            pieces.append(piece if step == 0 else along_plane(piece, step, line, plane, back=True))
    passed, local, gain_blocks = finish(
        line, plane, groups, seq_rows, inverse, act, top_grad.reshape(rows, features), norm_gains, pieces
    )

    result = passed
    for turn in range(sections - 2, -1, -1):
        incoming = lax.ppermute(result, "section", [(turn + 1, turn)])
        result = hand_on(turn, seq_rows, incoming, local, result)

    gain_parts = lax.all_to_all(gain_blocks, "dp", split_axis=0, concat_axis=0, tiled=True)
    gain_parts, result = lax.optimization_barrier((gain_parts, result))
    grad_shard = sum_scaled(gain_parts, grad_scale)
    return (result.reshape(activations.shape), grad_shard)


def solution(mesh):
    placed = (
        P("section", "dp", None, None, None),
        P("section", "dp", None, None, None),
        P("dp", None, None, None),
        P("section", None),
        P("section", "dp", None),
        P("dp", None),
    )
    return jax.shard_map(
        on_device,
        mesh=mesh,
        in_specs=placed,
        out_specs=(P("section", "dp", None, None, None), P("section", "dp")),
        check_vma=False,
    )
```

```python
import functools
import math

import jax
import jax.numpy as jnp
from jax import lax
from jax.experimental import pallas as pl
from jax.experimental.pallas import tpu as pltpu
from jax.sharding import PartitionSpec as P

norm_epsilon = 1e-05
mebibyte = 1024 * 1024
product_cost = 16


def grant(*arrays):
    total = 4 * mebibyte
    for array in arrays:
        lanes = -(-array.shape[-1] // 128) * 128
        total += math.prod(array.shape[:-1]) * lanes * jnp.dtype(array.dtype).itemsize
    return -(-total // mebibyte) * mebibyte


def plane_size(replicas):
    size = 1
    while (2 * size) ** 2 <= replicas and replicas % (2 * size) == 0:
        size *= 2
    return size


def ahead(place, step, count):
    if count & (count - 1) == 0:
        return place ^ step
    return (place + step) % count


def behind(place, step, count):
    if count & (count - 1) == 0:
        return place ^ step
    return (place + count - step) % count


def along_line(value, step, line, plane):
    pairs = [
        (z * plane + q, ahead(z, step, line) * plane + q)
        for z in range(line)
        for q in range(plane)
    ]
    return lax.ppermute(value, "dp", pairs)


def along_plane(value, step, line, plane, back=False):
    partner = behind if back else ahead
    pairs = [
        (z * plane + q, z * plane + partner(q, step, plane))
        for z in range(line)
        for q in range(plane)
    ]
    return lax.ppermute(value, "dp", pairs)


def product_kernel(token_count, weight_count, seq_rows, *refs):
    tokens = refs[:token_count]
    weights = refs[token_count : token_count + weight_count]
    outs = refs[token_count + weight_count :]
    for token_ref, out_ref in zip(tokens, outs):
        for index, weight_ref in enumerate(weights):
            product = lax.dot_general(
                token_ref[...],
                weight_ref[...],
                (((1,), (1,)), ((), ())),
                preferred_element_type=jnp.float32,
            ).astype(out_ref.dtype)
            width = product.shape[1]
            for micro in range(product.shape[0] // seq_rows):
                out_ref[index, :, micro * width : (micro + 1) * width] = product[
                    micro * seq_rows : (micro + 1) * seq_rows, :
                ]


def products(seq_rows, tokens, weights, cost=1):
    rows, depth = tokens[0].shape
    width = weights[0].shape[0]
    count = len(weights)
    folded = (count, seq_rows, rows // seq_rows * width)
    outs = [jax.ShapeDtypeStruct(folded, jnp.bfloat16) for _ in tokens]
    return pl.pallas_call(
        functools.partial(product_kernel, len(tokens), count, seq_rows),
        out_shape=outs,
        in_specs=[pl.BlockSpec(memory_space=pltpu.VMEM)] * (len(tokens) + count),
        out_specs=[pl.BlockSpec(memory_space=pltpu.VMEM)] * len(tokens),
        compiler_params=pltpu.CompilerParams(vmem_limit_bytes=grant(*tokens, *weights, *outs)),
        cost_estimate=pl.CostEstimate(
            flops=cost * 2 * rows * depth * width * count * len(tokens),
            bytes_accessed=2 * (rows * depth * len(tokens) + depth * width * count + rows * width * count * len(tokens)),
            transcendentals=0,
        ),
        name="token_products",
    )(*tokens, *weights)


def column_tile(features, most=512):
    tile = 128
    for width in range(128, most + 1, 128):
        if features % width == 0:
            tile = width
    return tile


def inverse_kernel(seq_rows, chunk, tile, lengths_ref, act_ref, inverse_ref):
    rows, features = act_ref.shape

    def one_chunk(index, _):
        start = pl.multiple_of(index * chunk, chunk)
        part = pl.ds(start, chunk)
        squares = jnp.zeros((chunk, 128), jnp.float32)
        for left in range(0, features, tile):
            wide = act_ref[part, left : left + tile].astype(jnp.float32)
            wide = wide * wide
            for lane in range(0, tile, 128):
                squares = squares + wide[:, lane : lane + 128]
        mean = jnp.sum(squares, axis=1, keepdims=True) / features
        position = lax.broadcasted_iota(jnp.int32, (chunk, 1), 0) + lax.rem(start, seq_rows)
        keep = position < lengths_ref[lax.div(start, seq_rows)]
        inverse_ref[part, :] = jnp.where(keep, lax.rsqrt(mean + norm_epsilon), 0.0)
        return 0

    lax.fori_loop(0, rows // chunk, one_chunk, 0)


def live_inverse(seq_rows, lengths, act):
    rows, features = act.shape
    return pl.pallas_call(
        functools.partial(inverse_kernel, seq_rows, math.gcd(seq_rows, 16), column_tile(features)),
        out_shape=jax.ShapeDtypeStruct((rows, 1), jnp.float32),
        in_specs=[pl.BlockSpec(memory_space=pltpu.SMEM), pl.BlockSpec(memory_space=pltpu.VMEM)],
        out_specs=pl.BlockSpec(memory_space=pltpu.VMEM),
        compiler_params=pltpu.CompilerParams(vmem_limit_bytes=grant(act)),
        cost_estimate=pl.CostEstimate(
            flops=2 * rows * features, bytes_accessed=2 * rows * features, transcendentals=rows
        ),
        name="live_inverse",
    )(lengths, act)


def relative(owner, place, count):
    if count & (count - 1) == 0:
        return owner ^ place
    return (place + count - owner) % count


def place_pieces(line, plane, groups, seq_rows, pieces, held, back):
    width = back.shape[1] // (line * plane)
    me = lax.axis_index("dp")
    z, q = lax.div(me, plane), lax.rem(me, plane)
    for step in range(plane):
        owner_q = ahead(q, step, plane)
        for group_index, group in enumerate(groups):
            piece = pieces[step * len(groups) + group_index]
            for index, line_step in enumerate(group):
                held[behind(z, line_step, line) * plane + owner_q] = piece[index]
    steps = [line_step for group in groups for line_step in group]
    for owner_z in range(line):
        line_step = relative(owner_z, z, line)
        here = functools.reduce(jnp.logical_or, [line_step == step for step in steps])

        @pl.when(here)
        def _():
            for micro in range(back.shape[0] // seq_rows):
                rows = slice(micro * seq_rows, (micro + 1) * seq_rows)
                for block in range(owner_z * plane, (owner_z + 1) * plane):
                    back[rows, block * width : (block + 1) * width] = held[
                        block, :, micro * width : (micro + 1) * width
                    ]


def early_kernel(line, plane, groups, seq_rows, *refs):
    place_pieces(line, plane, groups, seq_rows, refs[:-2], refs[-1], refs[-2])


def placed_early(line, plane, groups, seq_rows, features, pieces):
    micro_count = pieces[0].shape[2] * line * plane // features
    vmem = pl.BlockSpec(memory_space=pltpu.VMEM)
    out = jax.ShapeDtypeStruct((micro_count * seq_rows, features), jnp.bfloat16)
    held = pltpu.VMEM((line * plane,) + pieces[0].shape[1:], jnp.bfloat16)
    return pl.pallas_call(
        functools.partial(early_kernel, line, plane, groups, seq_rows),
        out_shape=out,
        in_specs=[vmem] * len(pieces),
        out_specs=vmem,
        scratch_shapes=[held],
        compiler_params=pltpu.CompilerParams(vmem_limit_bytes=grant(*pieces, out, held)),
        cost_estimate=pl.CostEstimate(flops=out.size, bytes_accessed=8 * out.size, transcendentals=0),
        name="placed_early",
    )(*pieces)


def finish_kernel(line, plane, groups, seq_rows, chunk, tile, early_ref, inverse_ref, act_ref, top_ref, gain_ref, *refs):
    piece_count = plane * len(groups)
    pieces = refs[:piece_count]
    passed_ref, local_ref, gain_out, held, back, gain_sum, pulls = refs[piece_count:]
    rows, features = back.shape
    width = features // (line * plane)
    back[...] = early_ref[...]
    place_pieces(line, plane, groups, seq_rows, pieces, held, back)
    gain_sum[...] = jnp.zeros_like(gain_sum)

    def sums(index, _):
        part = pl.ds(pl.multiple_of(index * chunk, chunk), chunk)
        inverse = inverse_ref[part, :]
        pull = jnp.zeros((chunk, 128), jnp.float32)
        for left in range(0, features, tile):
            cols = slice(left, left + tile)
            both = act_ref[part, cols].astype(jnp.float32) * back[part, cols].astype(jnp.float32)
            gained = both * gain_ref[:, cols]
            for lane in range(0, tile, 128):
                pull = pull + gained[:, lane : lane + 128]
            both = both * inverse
            folded = both[:8, :]
            for row in range(8, chunk, 8):
                folded = folded + both[row : row + 8, :]
            gain_sum[:, cols] += folded
        pulls[part, :] = pull
        return 0

    lax.fori_loop(0, rows // chunk, sums, 0)
    total = jnp.sum(gain_sum[...], axis=0, keepdims=True)
    for block in range(line * plane):
        gain_out[block] = total[:, block * width : (block + 1) * width]
    inverse = inverse_ref[...]
    pull = jnp.sum(pulls[...], axis=1, keepdims=True) / features
    pulls[...] = jnp.broadcast_to(pull * inverse * inverse * inverse, pulls.shape)

    def terms(index, _):
        part = pl.ds(pl.multiple_of(index * chunk, chunk), chunk)
        inverse = inverse_ref[part, :]
        pull = pulls[part, :1]
        for left in range(0, features, tile):
            cols = slice(left, left + tile)
            scaled = back[part, cols].astype(jnp.float32) * gain_ref[:, cols]
            local = inverse * scaled - act_ref[part, cols].astype(jnp.float32) * pull
            local_ref[part, cols] = local
            passed_ref[part, cols] = (top_ref[part, cols].astype(jnp.float32) + local).astype(jnp.bfloat16)
        return 0

    lax.fori_loop(0, rows // chunk, terms, 0)


def finish(line, plane, groups, seq_rows, early, inverse, act, top, gain, pieces):
    rows, features = act.shape
    blocks = line * plane
    vmem = pl.BlockSpec(memory_space=pltpu.VMEM)
    outs = [
        jax.ShapeDtypeStruct((rows, features), jnp.bfloat16),
        jax.ShapeDtypeStruct((rows, features), jnp.float32),
        jax.ShapeDtypeStruct((blocks, 1, features // blocks), jnp.float32),
    ]
    scratch = [
        pltpu.VMEM((blocks,) + pieces[0].shape[1:], jnp.bfloat16),
        pltpu.VMEM((rows, features), jnp.bfloat16),
        pltpu.VMEM((8, features), jnp.float32),
        pltpu.VMEM((rows, 128), jnp.float32),
    ]
    return pl.pallas_call(
        functools.partial(finish_kernel, line, plane, groups, seq_rows, 16, column_tile(features)),
        out_shape=outs,
        in_specs=[vmem] * (5 + len(pieces)),
        out_specs=[vmem] * len(outs),
        scratch_shapes=scratch,
        compiler_params=pltpu.CompilerParams(
            vmem_limit_bytes=grant(early, act, top, *pieces, *outs, *scratch)
        ),
        cost_estimate=pl.CostEstimate(
            flops=16 * rows * features, bytes_accessed=12 * rows * features, transcendentals=0
        ),
        name="norm_backward",
    )(early, inverse, act, top, gain, *pieces)


def hand_kernel(turn, chunk, tile, incoming_ref, local_ref, result_ref, out_ref, staged, copied):
    rows, features = local_ref.shape
    count = rows // chunk
    is_turn = lax.axis_index("section") == turn
    copies = [
        pltpu.make_async_copy(
            staged.at[pl.ds(index * chunk, chunk)], out_ref.at[pl.ds(index * chunk, chunk)], copied.at[index]
        )
        for index in range(count)
    ]
    for index in range(count):

        @pl.when(is_turn)
        def _():
            def one_part(step, _):
                part = pl.ds(pl.multiple_of(index * chunk + step * 16, 16), 16)
                for left in range(0, features, tile):
                    cols = slice(left, left + tile)
                    staged[part, cols] = (
                        incoming_ref[part, cols].astype(jnp.float32) + local_ref[part, cols]
                    ).astype(jnp.bfloat16)
                return 0

            lax.fori_loop(0, chunk // 16, one_part, 0)

        @pl.when(jnp.logical_not(is_turn))
        def _():
            part = pl.ds(index * chunk, chunk)
            staged[part, :] = result_ref[part, :]

        copies[index].start()
    for copy in copies:
        copy.wait()


def hand_on(turn, chunk, incoming, local, result):
    rows, features = local.shape
    vmem = pl.BlockSpec(memory_space=pltpu.VMEM)
    return pl.pallas_call(
        functools.partial(hand_kernel, turn, chunk, column_tile(features)),
        out_shape=jax.ShapeDtypeStruct((rows, features), jnp.bfloat16),
        in_specs=[vmem, vmem, vmem],
        out_specs=pl.BlockSpec(memory_space=pl.ANY),
        scratch_shapes=[
            pltpu.VMEM((rows, features), jnp.bfloat16),
            pltpu.SemaphoreType.DMA((rows // chunk,)),
        ],
        compiler_params=pltpu.CompilerParams(vmem_limit_bytes=grant(incoming, local, result, result)),
        cost_estimate=pl.CostEstimate(
            flops=rows * features, bytes_accessed=8 * rows * features, transcendentals=0
        ),
        name="hand_on",
    )(incoming, local, result)


def sum_kernel(scale, parts_ref, out_ref):
    total = parts_ref[0]
    for index in range(1, parts_ref.shape[0]):
        total = total + parts_ref[index]
    out_ref[...] = total * scale


def sum_scaled(parts, scale):
    vmem = pl.BlockSpec(memory_space=pltpu.VMEM)
    return pl.pallas_call(
        functools.partial(sum_kernel, scale),
        out_shape=jax.ShapeDtypeStruct(parts.shape[1:], jnp.float32),
        in_specs=[vmem],
        out_specs=vmem,
        compiler_params=pltpu.CompilerParams(vmem_limit_bytes=mebibyte),
        cost_estimate=pl.CostEstimate(flops=parts.size, bytes_accessed=4 * parts.size, transcendentals=0),
        name="sum_scaled",
    )(parts)


def sent_back(group_products, line, plane):
    return [group_products[0]] + [
        along_plane(group_products[step], step, line, plane, back=True) for step in range(1, plane)
    ]


def gathered_products(seq_rows, tokens, shard, line, plane):
    held = {0: shard}
    groups = [(0,)]
    first = products(seq_rows, tokens, [shard])
    if line & (line - 1):
        for step in range(1, line):
            held[step] = along_line(shard, step, line, plane)
        groups.append(tuple(range(1, (line + 1) // 2)))
    elif line > 1:
        distance = line // 2
        while distance:
            held[distance] = along_line(shard, distance, line, plane)
            distance //= 2
        groups.append(tuple(sorted(step for step in held if step)))
        far = line // 2
        held[far], own = lax.optimization_barrier((held[far], first[0]))
        first = [own] + list(first[1:])
        distance = line // 4
        while distance:
            for step in sorted(held):
                if step and step % (2 * distance) == 0 and step + distance not in held:
                    held[step + distance] = along_line(held[step], distance, line, plane)
            distance //= 2
    groups.append(tuple(step for step in range(line) if not any(step in group for group in groups)))
    groups = [group for group in groups if group]
    pieces = [sent_back(first, line, plane)]
    for group in groups[1:]:
        shards = [held[step] for step in group]
        pieces.append(sent_back(products(seq_rows, tokens, shards, product_cost), line, plane))
    return groups, pieces


def on_device(activations, key_grads, top_grad, norm_gains, w_key, lengths):
    micro_count, seq_rows, features = activations.shape[2:]
    rows = micro_count * seq_rows
    replicas = lax.axis_size("dp")
    sections = lax.axis_size("section")
    plane = plane_size(replicas)
    line = replicas // plane
    grad_scale = 1.0 / math.sqrt(replicas * rows)
    act = activations.reshape(rows, features)

    key_rows = key_grads.reshape(rows, key_grads.shape[-1])
    inverse, own_rows = lax.optimization_barrier((live_inverse(seq_rows, lengths[0], act), key_rows))
    tokens = [own_rows] + [along_plane(key_rows, step, line, plane) for step in range(1, plane)]
    groups, pieces = gathered_products(seq_rows, tokens, w_key[0], line, plane)
    split = max(1, len(groups) - 1)
    early, late = ([part[step] for step in range(plane) for part in some] for some in (pieces[:split], pieces[split:]))
    early = placed_early(line, plane, groups[:split], seq_rows, features, early)
    passed, local, gain_blocks = finish(
        line,
        plane,
        groups[split:],
        seq_rows,
        early,
        inverse,
        act,
        top_grad.reshape(rows, features),
        norm_gains,
        late,
    )

    result = passed
    for turn in range(sections - 2, -1, -1):
        incoming = lax.ppermute(result, "section", [(turn + 1, turn)])
        result = hand_on(turn, seq_rows, incoming, local, result)

    gain_parts = lax.all_to_all(gain_blocks, "dp", split_axis=0, concat_axis=0, tiled=True)
    gain_parts, result = lax.optimization_barrier((gain_parts, result))
    grad_shard = sum_scaled(gain_parts, grad_scale)
    return (result.reshape(activations.shape), grad_shard)


def solution(mesh):
    placed = (
        P("section", "dp", None, None, None),
        P("section", "dp", None, None, None),
        P("dp", None, None, None),
        P("section", None),
        P("section", "dp", None),
        P("dp", None),
    )
    return jax.shard_map(
        on_device,
        mesh=mesh,
        in_specs=placed,
        out_specs=(P("section", "dp", None, None, None), P("section", "dp")),
        check_vma=False,
    )
```

```python
import functools
import math

import jax
import jax.numpy as jnp
from jax import lax
from jax.experimental import pallas as pl
from jax.experimental.pallas import tpu as pltpu
from jax.sharding import PartitionSpec as P

norm_epsilon = 1e-05
mebibyte = 1024 * 1024
product_cost = 10


def grant(*arrays):
    total = 4 * mebibyte
    for array in arrays:
        lanes = -(-array.shape[-1] // 128) * 128
        total += math.prod(array.shape[:-1]) * lanes * jnp.dtype(array.dtype).itemsize
    return -(-total // mebibyte) * mebibyte


def plane_size(replicas):
    size = 1
    while (2 * size) ** 2 <= replicas and replicas % (2 * size) == 0:
        size *= 2
    return size


def ahead(place, step, count):
    if count & (count - 1) == 0:
        return place ^ step
    return (place + step) % count


def behind(place, step, count):
    if count & (count - 1) == 0:
        return place ^ step
    return (place + count - step) % count


def along_line(value, step, line, plane):
    pairs = [
        (z * plane + q, ahead(z, step, line) * plane + q)
        for z in range(line)
        for q in range(plane)
    ]
    return lax.ppermute(value, "dp", pairs)


def along_plane(value, step, line, plane, back=False):
    partner = behind if back else ahead
    pairs = [
        (z * plane + q, z * plane + partner(q, step, plane))
        for z in range(line)
        for q in range(plane)
    ]
    return lax.ppermute(value, "dp", pairs)


def product_kernel(token_count, weight_count, seq_rows, *refs):
    tokens = refs[:token_count]
    weights = refs[token_count : token_count + weight_count]
    outs = refs[token_count + weight_count :]
    for token_ref, out_ref in zip(tokens, outs):
        for index, weight_ref in enumerate(weights):
            product = lax.dot_general(
                token_ref[...],
                weight_ref[...],
                (((1,), (1,)), ((), ())),
                preferred_element_type=jnp.float32,
            ).astype(out_ref.dtype)
            width = product.shape[1]
            for micro in range(product.shape[0] // seq_rows):
                out_ref[index, :, micro * width : (micro + 1) * width] = product[
                    micro * seq_rows : (micro + 1) * seq_rows, :
                ]


def products(seq_rows, tokens, weights):
    rows, depth = tokens[0].shape
    width = weights[0].shape[0]
    count = len(weights)
    folded = (count, seq_rows, rows // seq_rows * width)
    outs = [jax.ShapeDtypeStruct(folded, jnp.bfloat16) for _ in tokens]
    return pl.pallas_call(
        functools.partial(product_kernel, len(tokens), count, seq_rows),
        out_shape=outs,
        in_specs=[pl.BlockSpec(memory_space=pltpu.VMEM)] * (len(tokens) + count),
        out_specs=[pl.BlockSpec(memory_space=pltpu.VMEM)] * len(tokens),
        compiler_params=pltpu.CompilerParams(vmem_limit_bytes=grant(*tokens, *weights, *outs)),
        cost_estimate=pl.CostEstimate(
            flops=product_cost * 2 * rows * depth * width * count * len(tokens),
            bytes_accessed=2 * (rows * depth * len(tokens) + depth * width * count + rows * width * count * len(tokens)),
            transcendentals=0,
        ),
        name="token_products",
    )(*tokens, *weights)


def column_tile(features, most=512):
    tile = 128
    for width in range(128, most + 1, 128):
        if features % width == 0:
            tile = width
    return tile


def inverse_kernel(seq_rows, chunk, tile, lengths_ref, act_ref, inverse_ref):
    rows, features = act_ref.shape

    def one_chunk(index, _):
        start = pl.multiple_of(index * chunk, chunk)
        part = pl.ds(start, chunk)
        squares = jnp.zeros((chunk, 128), jnp.float32)
        for left in range(0, features, tile):
            wide = act_ref[part, left : left + tile].astype(jnp.float32)
            wide = wide * wide
            for lane in range(0, tile, 128):
                squares = squares + wide[:, lane : lane + 128]
        mean = jnp.sum(squares, axis=1, keepdims=True) / features
        position = lax.broadcasted_iota(jnp.int32, (chunk, 1), 0) + lax.rem(start, seq_rows)
        keep = position < lengths_ref[lax.div(start, seq_rows)]
        inverse = jnp.where(keep, lax.rsqrt(mean + norm_epsilon), 0.0)
        inverse_ref[part, :] = jnp.broadcast_to(inverse, (chunk, 128))
        return 0

    lax.fori_loop(0, rows // chunk, one_chunk, 0)


def live_inverse(seq_rows, lengths, act):
    rows, features = act.shape
    return pl.pallas_call(
        functools.partial(inverse_kernel, seq_rows, math.gcd(seq_rows, 16), column_tile(features)),
        out_shape=jax.ShapeDtypeStruct((rows, 128), jnp.float32),
        in_specs=[pl.BlockSpec(memory_space=pltpu.SMEM), pl.BlockSpec(memory_space=pltpu.VMEM)],
        out_specs=pl.BlockSpec(memory_space=pltpu.VMEM),
        compiler_params=pltpu.CompilerParams(vmem_limit_bytes=grant(act)),
        cost_estimate=pl.CostEstimate(
            flops=2 * rows * features, bytes_accessed=2 * rows * features, transcendentals=rows
        ),
        name="live_inverse",
    )(lengths, act)


def relative(owner, place, count):
    if count & (count - 1) == 0:
        return owner ^ place
    return (place + count - owner) % count


def place_pieces(line, plane, groups, seq_rows, pieces, held, back):
    width = back.shape[1] // (line * plane)
    me = lax.axis_index("dp")
    z, q = lax.div(me, plane), lax.rem(me, plane)
    for step in range(plane):
        owner_q = ahead(q, step, plane)
        for group_index, group in enumerate(groups):
            piece = pieces[step * len(groups) + group_index]
            for index, line_step in enumerate(group):
                held[behind(z, line_step, line) * plane + owner_q] = piece[index]
    steps = [line_step for group in groups for line_step in group]
    for owner_z in range(line):
        line_step = relative(owner_z, z, line)
        here = functools.reduce(jnp.logical_or, [line_step == step for step in steps])

        @pl.when(here)
        def _():
            for micro in range(back.shape[0] // seq_rows):
                rows = slice(micro * seq_rows, (micro + 1) * seq_rows)
                for block in range(owner_z * plane, (owner_z + 1) * plane):
                    back[rows, block * width : (block + 1) * width] = held[
                        block, :, micro * width : (micro + 1) * width
                    ]


def early_kernel(line, plane, groups, seq_rows, *refs):
    place_pieces(line, plane, groups, seq_rows, refs[:-2], refs[-1], refs[-2])


def placed_early(line, plane, groups, seq_rows, features, pieces):
    micro_count = pieces[0].shape[2] * line * plane // features
    vmem = pl.BlockSpec(memory_space=pltpu.VMEM)
    out = jax.ShapeDtypeStruct((micro_count * seq_rows, features), jnp.bfloat16)
    held = pltpu.VMEM((line * plane,) + pieces[0].shape[1:], jnp.bfloat16)
    return pl.pallas_call(
        functools.partial(early_kernel, line, plane, groups, seq_rows),
        out_shape=out,
        in_specs=[vmem] * len(pieces),
        out_specs=vmem,
        scratch_shapes=[held],
        compiler_params=pltpu.CompilerParams(vmem_limit_bytes=grant(*pieces, out, held)),
        cost_estimate=pl.CostEstimate(flops=out.size, bytes_accessed=8 * out.size, transcendentals=0),
        name="placed_early",
    )(*pieces)


def finish_kernel(line, plane, groups, seq_rows, chunk, early_ref, inverse_ref, act_ref, top_ref, gain_ref, *refs):
    piece_count = plane * len(groups)
    pieces = refs[:piece_count]
    passed_ref, local_ref, gain_out, held, back, gain_sum, pulls = refs[piece_count:]
    rows, features = back.shape
    width = features // (line * plane)
    back[...] = early_ref[...]
    place_pieces(line, plane, groups, seq_rows, pieces, held, back)
    gain_sum[...] = jnp.zeros_like(gain_sum)

    def sums(index, _):
        part = pl.ds(pl.multiple_of(index * chunk, chunk), chunk)
        inverse = inverse_ref[part, :]
        pull = jnp.zeros((chunk, 128), jnp.float32)
        for left in range(0, features, 128):
            cols = slice(left, left + 128)
            both = act_ref[part, cols].astype(jnp.float32) * back[part, cols].astype(jnp.float32)
            pull = pull + both * gain_ref[:, cols]
            both = both * inverse
            folded = both[:8, :]
            for row in range(8, chunk, 8):
                folded = folded + both[row : row + 8, :]
            gain_sum[:, cols] += folded
        pulls[part, :] = pull
        return 0

    lax.fori_loop(0, rows // chunk, sums, 0)
    total = jnp.sum(gain_sum[...], axis=0, keepdims=True)
    for block in range(line * plane):
        gain_out[block] = total[:, block * width : (block + 1) * width]
    inverse = inverse_ref[...]
    pull = jnp.broadcast_to(jnp.sum(pulls[...], axis=1, keepdims=True), pulls.shape) / features
    pulls[...] = pull * inverse * inverse * inverse

    def terms(index, _):
        part = pl.ds(pl.multiple_of(index * chunk, chunk), chunk)
        inverse = inverse_ref[part, :]
        pull = pulls[part, :]
        for left in range(0, features, 128):
            cols = slice(left, left + 128)
            scaled = back[part, cols].astype(jnp.float32) * gain_ref[:, cols]
            local = inverse * scaled - act_ref[part, cols].astype(jnp.float32) * pull
            local_ref[part, cols] = local
            passed_ref[part, cols] = (top_ref[part, cols].astype(jnp.float32) + local).astype(jnp.bfloat16)
        return 0

    lax.fori_loop(0, rows // chunk, terms, 0)


def finish(line, plane, groups, seq_rows, early, inverse, act, top, gain, pieces):
    rows, features = act.shape
    blocks = line * plane
    vmem = pl.BlockSpec(memory_space=pltpu.VMEM)
    outs = [
        jax.ShapeDtypeStruct((rows, features), jnp.bfloat16),
        jax.ShapeDtypeStruct((rows, features), jnp.float32),
        jax.ShapeDtypeStruct((blocks, 1, features // blocks), jnp.float32),
    ]
    scratch = [
        pltpu.VMEM((blocks,) + pieces[0].shape[1:], jnp.bfloat16),
        pltpu.VMEM((rows, features), jnp.bfloat16),
        pltpu.VMEM((8, features), jnp.float32),
        pltpu.VMEM((rows, 128), jnp.float32),
    ]
    return pl.pallas_call(
        functools.partial(finish_kernel, line, plane, groups, seq_rows, math.gcd(rows, 32)),
        out_shape=outs,
        in_specs=[vmem] * (5 + len(pieces)),
        out_specs=[vmem] * len(outs),
        scratch_shapes=scratch,
        compiler_params=pltpu.CompilerParams(
            vmem_limit_bytes=grant(early, act, top, *pieces, *outs, *scratch)
        ),
        cost_estimate=pl.CostEstimate(
            flops=16 * rows * features, bytes_accessed=12 * rows * features, transcendentals=0
        ),
        name="norm_backward",
    )(early, inverse, act, top, gain, *pieces)


def hand_kernel(turn, chunk, incoming_ref, local_ref, result_ref, out_ref, staged, copied):
    rows, features = local_ref.shape
    parts = [pl.ds(start, chunk) for start in range(0, rows, chunk)]
    is_turn = lax.axis_index("section") == turn

    @pl.when(is_turn)
    def _():
        for index, part in enumerate(parts):
            for left in range(0, features, 128):
                cols = slice(left, left + 128)
                staged[part, cols] = (incoming_ref[part, cols].astype(jnp.float32) + local_ref[part, cols]).astype(
                    jnp.bfloat16
                )
            pltpu.make_async_copy(staged.at[part], out_ref.at[part], copied.at[index]).start()
        for index, part in enumerate(parts):
            pltpu.make_async_copy(staged.at[part], out_ref.at[part], copied.at[index]).wait()

    @pl.when(jnp.logical_not(is_turn))
    def _():
        copies = [
            pltpu.make_async_copy(result_ref.at[part], out_ref.at[part], copied.at[index])
            for index, part in enumerate(parts)
        ]
        for copy in copies:
            copy.start()
        for copy in copies:
            copy.wait()


def hand_on(turn, chunk, incoming, local, result):
    rows, features = local.shape
    vmem = pl.BlockSpec(memory_space=pltpu.VMEM)
    return pl.pallas_call(
        functools.partial(hand_kernel, turn, chunk),
        out_shape=jax.ShapeDtypeStruct((rows, features), jnp.bfloat16),
        in_specs=[vmem, vmem, vmem],
        out_specs=pl.BlockSpec(memory_space=pl.ANY),
        scratch_shapes=[
            pltpu.VMEM((rows, features), jnp.bfloat16),
            pltpu.SemaphoreType.DMA((rows // chunk,)),
        ],
        compiler_params=pltpu.CompilerParams(vmem_limit_bytes=grant(incoming, local, result, result)),
        cost_estimate=pl.CostEstimate(
            flops=rows * features, bytes_accessed=8 * rows * features, transcendentals=0
        ),
        name="hand_on",
    )(incoming, local, result)


def sum_kernel(scale, parts_ref, out_ref):
    total = parts_ref[0]
    for index in range(1, parts_ref.shape[0]):
        total = total + parts_ref[index]
    out_ref[...] = total * scale


def sum_scaled(parts, scale):
    vmem = pl.BlockSpec(memory_space=pltpu.VMEM)
    return pl.pallas_call(
        functools.partial(sum_kernel, scale),
        out_shape=jax.ShapeDtypeStruct(parts.shape[1:], jnp.float32),
        in_specs=[vmem],
        out_specs=vmem,
        compiler_params=pltpu.CompilerParams(vmem_limit_bytes=mebibyte),
        cost_estimate=pl.CostEstimate(flops=parts.size, bytes_accessed=4 * parts.size, transcendentals=0),
        name="sum_scaled",
    )(parts)


def sent_back(group_products, line, plane):
    return [group_products[0]] + [
        along_plane(group_products[step], step, line, plane, back=True) for step in range(1, plane)
    ]


def gathered_products(seq_rows, tokens, shard, line, plane):
    held = {0: shard}
    groups = [(0,)]
    first = products(seq_rows, tokens, [shard])
    if line & (line - 1):
        for step in range(1, line):
            held[step] = along_line(shard, step, line, plane)
        groups.append(tuple(range(1, (line + 1) // 2)))
    elif line > 1:
        distance = line // 2
        while distance:
            held[distance] = along_line(shard, distance, line, plane)
            distance //= 2
        groups.append(tuple(sorted(step for step in held if step)))
        far = line // 2
        held[far], own = lax.optimization_barrier((held[far], first[0]))
        first = [own] + list(first[1:])
        distance = line // 4
        while distance:
            for step in sorted(held):
                if step and step % (2 * distance) == 0 and step + distance not in held:
                    held[step + distance] = along_line(held[step], distance, line, plane)
            distance //= 2
    groups.append(tuple(step for step in range(line) if not any(step in group for group in groups)))
    groups = [group for group in groups if group]
    pieces = [sent_back(first, line, plane)]
    for group in groups[1:]:
        shards = [held[step] for step in group]
        made = list(products(seq_rows, tokens, shards))
        if len(pieces) == 1:
            made[-1], pieces[0] = lax.optimization_barrier((made[-1], pieces[0]))
        pieces.append(sent_back(made, line, plane))
    return groups, pieces


def on_device(activations, key_grads, top_grad, norm_gains, w_key, lengths):
    micro_count, seq_rows, features = activations.shape[2:]
    rows = micro_count * seq_rows
    replicas = lax.axis_size("dp")
    sections = lax.axis_size("section")
    plane = plane_size(replicas)
    line = replicas // plane
    grad_scale = 1.0 / math.sqrt(replicas * rows)
    act = activations.reshape(rows, features)

    key_rows = key_grads.reshape(rows, key_grads.shape[-1])
    inverse, own_rows = lax.optimization_barrier((live_inverse(seq_rows, lengths[0], act), key_rows))
    tokens = [own_rows] + [along_plane(key_rows, step, line, plane) for step in range(1, plane)]
    groups, pieces = gathered_products(seq_rows, tokens, w_key[0], line, plane)
    split = max(1, len(groups) - 1)
    early, late = ([part[step] for step in range(plane) for part in some] for some in (pieces[:split], pieces[split:]))
    early = placed_early(line, plane, groups[:split], seq_rows, features, early)
    passed, local, gain_blocks = finish(
        line,
        plane,
        groups[split:],
        seq_rows,
        early,
        inverse,
        act,
        top_grad.reshape(rows, features),
        norm_gains,
        late,
    )

    result = passed
    for turn in range(sections - 2, -1, -1):
        incoming = lax.ppermute(result, "section", [(turn + 1, turn)])
        result = hand_on(turn, seq_rows, incoming, local, result)

    gain_parts = lax.all_to_all(gain_blocks, "dp", split_axis=0, concat_axis=0, tiled=True)
    gain_parts, result = lax.optimization_barrier((gain_parts, result))
    grad_shard = sum_scaled(gain_parts, grad_scale)
    return (result.reshape(activations.shape), grad_shard)


def solution(mesh):
    placed = (
        P("section", "dp", None, None, None),
        P("section", "dp", None, None, None),
        P("dp", None, None, None),
        P("section", None),
        P("section", "dp", None),
        P("dp", None),
    )
    return jax.shard_map(
        on_device,
        mesh=mesh,
        in_specs=placed,
        out_specs=(P("section", "dp", None, None, None), P("section", "dp")),
        check_vma=False,
    )
```

```python
import functools
import math

import jax
import jax.numpy as jnp
from jax import lax
from jax.experimental import pallas as pl
from jax.experimental.pallas import tpu as pltpu
from jax.sharding import PartitionSpec as P

norm_epsilon = 1e-05
mebibyte = 1024 * 1024
product_cost = 10


def grant(*arrays):
    total = 4 * mebibyte
    for array in arrays:
        lanes = -(-array.shape[-1] // 128) * 128
        total += math.prod(array.shape[:-1]) * lanes * jnp.dtype(array.dtype).itemsize
    return -(-total // mebibyte) * mebibyte


def plane_size(replicas):
    size = 1
    while (2 * size) ** 2 <= replicas and replicas % (2 * size) == 0:
        size *= 2
    return size


def ahead(place, step, count):
    if count & (count - 1) == 0:
        return place ^ step
    return (place + step) % count


def behind(place, step, count):
    if count & (count - 1) == 0:
        return place ^ step
    return (place + count - step) % count


def along_line(value, step, line, plane):
    pairs = [
        (z * plane + q, ahead(z, step, line) * plane + q)
        for z in range(line)
        for q in range(plane)
    ]
    return lax.ppermute(value, "dp", pairs)


def along_plane(value, step, line, plane, back=False):
    partner = behind if back else ahead
    pairs = [
        (z * plane + q, z * plane + partner(q, step, plane))
        for z in range(line)
        for q in range(plane)
    ]
    return lax.ppermute(value, "dp", pairs)


def product_kernel(token_count, weight_count, seq_rows, *refs):
    tokens = refs[:token_count]
    weights = refs[token_count : token_count + weight_count]
    outs = refs[token_count + weight_count :]
    for token_ref, out_ref in zip(tokens, outs):
        for index, weight_ref in enumerate(weights):
            product = lax.dot_general(
                token_ref[...],
                weight_ref[...],
                (((1,), (1,)), ((), ())),
                preferred_element_type=jnp.float32,
            ).astype(out_ref.dtype)
            width = product.shape[1]
            for micro in range(product.shape[0] // seq_rows):
                out_ref[index, :, micro * width : (micro + 1) * width] = product[
                    micro * seq_rows : (micro + 1) * seq_rows, :
                ]


def products(seq_rows, tokens, weights):
    rows, depth = tokens[0].shape
    width = weights[0].shape[0]
    count = len(weights)
    folded = (count, seq_rows, rows // seq_rows * width)
    outs = [jax.ShapeDtypeStruct(folded, jnp.bfloat16) for _ in tokens]
    return pl.pallas_call(
        functools.partial(product_kernel, len(tokens), count, seq_rows),
        out_shape=outs,
        in_specs=[pl.BlockSpec(memory_space=pltpu.VMEM)] * (len(tokens) + count),
        out_specs=[pl.BlockSpec(memory_space=pltpu.VMEM)] * len(tokens),
        compiler_params=pltpu.CompilerParams(vmem_limit_bytes=grant(*tokens, *weights, *outs)),
        cost_estimate=pl.CostEstimate(
            flops=product_cost * 2 * rows * depth * width * count * len(tokens),
            bytes_accessed=2 * (rows * depth * len(tokens) + depth * width * count + rows * width * count * len(tokens)),
            transcendentals=0,
        ),
        name="token_products",
    )(*tokens, *weights)


def column_tile(features, most=512):
    tile = 128
    for width in range(128, most + 1, 128):
        if features % width == 0:
            tile = width
    return tile


def inverse_kernel(seq_rows, chunk, tile, lengths_ref, act_ref, inverse_ref):
    rows, features = act_ref.shape

    def one_chunk(index, _):
        start = pl.multiple_of(index * chunk, chunk)
        part = pl.ds(start, chunk)
        squares = jnp.zeros((chunk, 128), jnp.float32)
        for left in range(0, features, tile):
            wide = act_ref[part, left : left + tile].astype(jnp.float32)
            wide = wide * wide
            for lane in range(0, tile, 128):
                squares = squares + wide[:, lane : lane + 128]
        mean = jnp.sum(squares, axis=1, keepdims=True) / features
        position = lax.broadcasted_iota(jnp.int32, (chunk, 1), 0) + lax.rem(start, seq_rows)
        keep = position < lengths_ref[lax.div(start, seq_rows)]
        inverse = jnp.where(keep, lax.rsqrt(mean + norm_epsilon), 0.0)
        inverse_ref[part, :] = jnp.broadcast_to(inverse, (chunk, 128))
        return 0

    lax.fori_loop(0, rows // chunk, one_chunk, 0)


def live_inverse(seq_rows, lengths, act):
    rows, features = act.shape
    return pl.pallas_call(
        functools.partial(inverse_kernel, seq_rows, math.gcd(seq_rows, 16), column_tile(features)),
        out_shape=jax.ShapeDtypeStruct((rows, 128), jnp.float32),
        in_specs=[pl.BlockSpec(memory_space=pltpu.SMEM), pl.BlockSpec(memory_space=pltpu.VMEM)],
        out_specs=pl.BlockSpec(memory_space=pltpu.VMEM),
        compiler_params=pltpu.CompilerParams(vmem_limit_bytes=grant(act)),
        cost_estimate=pl.CostEstimate(
            flops=2 * rows * features, bytes_accessed=2 * rows * features, transcendentals=rows
        ),
        name="live_inverse",
    )(lengths, act)


def relative(owner, place, count):
    if count & (count - 1) == 0:
        return owner ^ place
    return (place + count - owner) % count


def place_pieces(line, plane, groups, seq_rows, pieces, held, back):
    width = back.shape[1] // (line * plane)
    me = lax.axis_index("dp")
    z, q = lax.div(me, plane), lax.rem(me, plane)
    for step in range(plane):
        owner_q = ahead(q, step, plane)
        for group_index, group in enumerate(groups):
            piece = pieces[step * len(groups) + group_index]
            for index, line_step in enumerate(group):
                held[behind(z, line_step, line) * plane + owner_q] = piece[index]
    steps = [line_step for group in groups for line_step in group]
    for owner_z in range(line):
        line_step = relative(owner_z, z, line)
        here = functools.reduce(jnp.logical_or, [line_step == step for step in steps])

        @pl.when(here)
        def _():
            for micro in range(back.shape[0] // seq_rows):
                rows = slice(micro * seq_rows, (micro + 1) * seq_rows)
                for block in range(owner_z * plane, (owner_z + 1) * plane):
                    back[rows, block * width : (block + 1) * width] = held[
                        block, :, micro * width : (micro + 1) * width
                    ]


def add_sums(lefts, chunk, project, inverse_ref, act_ref, gain_ref, gain_sum, pulls):
    rows = act_ref.shape[0]

    def one_chunk(index, _):
        part = pl.ds(pl.multiple_of(index * chunk, chunk), chunk)
        inverse = inverse_ref[part, :]
        pull = pulls[part, :]
        for left in lefts:
            cols = slice(left, left + 128)
            both = act_ref[part, cols].astype(jnp.float32) * project(part, cols)
            pull = pull + both * gain_ref[:, cols]
            both = both * inverse
            folded = both[:8, :]
            for row in range(8, chunk, 8):
                folded = folded + both[row : row + 8, :]
            gain_sum[:, cols] += folded
        pulls[part, :] = pull
        return 0

    lax.fori_loop(0, rows // chunk, one_chunk, 0)


def early_kernel(line, plane, groups, seq_rows, chunk, inverse_ref, act_ref, gain_ref, *refs):
    piece_count = plane * len(groups)
    pieces, refs = refs[:piece_count], refs[piece_count:]
    back, pulls = refs[:2]
    gain_outs = refs[2:-3]
    held, gain_sum, gain_blocks = refs[-3:]
    features = back.shape[1]
    width = features // (line * plane)
    back[...] = jnp.zeros_like(back)
    place_pieces(line, plane, groups, seq_rows, pieces, held, back)
    gain_sum[...] = jnp.zeros_like(gain_sum)
    pulls[...] = jnp.zeros_like(pulls)
    add_sums(
        range(0, features, 128),
        chunk,
        lambda part, cols: back[part, cols].astype(jnp.float32),
        inverse_ref,
        act_ref,
        gain_ref,
        gain_sum,
        pulls,
    )
    total = jnp.sum(gain_sum[...], axis=0, keepdims=True)
    if len(gain_outs) == 1:
        for block in range(line * plane):
            gain_outs[0][block] = total[:, block * width : (block + 1) * width]
        return
    q = lax.rem(lax.axis_index("dp"), plane)
    for block in range(line * plane):
        gain_blocks[block] = total[:, block * width : (block + 1) * width]
    for step, gain_out in enumerate(gain_outs):
        for owner_z in range(line):
            gain_out[owner_z] = gain_blocks[owner_z * plane + ahead(q, step, plane)]


def placed_early(line, plane, groups, seq_rows, direct, inverse, act, gain, pieces):
    rows, features = act.shape
    blocks = line * plane
    width = features // blocks
    vmem = pl.BlockSpec(memory_space=pltpu.VMEM)
    outs = [
        jax.ShapeDtypeStruct((rows, features), jnp.bfloat16),
        jax.ShapeDtypeStruct((rows, 128), jnp.float32),
    ]
    if direct:
        outs += [jax.ShapeDtypeStruct((line, 1, width), jnp.float32)] * plane
    else:
        outs += [jax.ShapeDtypeStruct((blocks, 1, width), jnp.float32)]
    scratch = [
        pltpu.VMEM((blocks,) + pieces[0].shape[1:], jnp.bfloat16),
        pltpu.VMEM((8, features), jnp.float32),
        pltpu.VMEM((blocks, 1, width), jnp.float32),
    ]
    return pl.pallas_call(
        functools.partial(early_kernel, line, plane, groups, seq_rows, math.gcd(rows, 32)),
        out_shape=outs,
        in_specs=[vmem] * (3 + len(pieces)),
        out_specs=[vmem] * len(outs),
        scratch_shapes=scratch,
        compiler_params=pltpu.CompilerParams(
            vmem_limit_bytes=grant(inverse, act, gain, *pieces, *outs, *scratch)
        ),
        cost_estimate=pl.CostEstimate(
            flops=8 * rows * features, bytes_accessed=8 * rows * features, transcendentals=0
        ),
        name="placed_early",
    )(inverse, act, gain, *pieces)


def finish_kernel(
    line,
    plane,
    groups,
    early_steps,
    seq_rows,
    chunk,
    early_ref,
    early_pulls,
    inverse_ref,
    act_ref,
    top_ref,
    gain_ref,
    *refs,
):
    piece_count = plane * len(groups)
    pieces, refs = refs[:piece_count], refs[piece_count:]
    if early_steps:
        in_plane, refs = refs[:plane], refs[plane:]
    passed_ref, local_ref = refs[:2]
    gain_outs = refs[2:-5]
    held, back, gain_sum, pulls, gain_blocks = refs[-5:]
    rows, features = back.shape
    width = features // (line * plane)
    me = lax.axis_index("dp")
    z, q = lax.div(me, plane), lax.rem(me, plane)
    back[...] = early_ref[...]
    place_pieces(line, plane, groups, seq_rows, pieces, held, back)
    gain_sum[...] = jnp.zeros_like(gain_sum)
    pulls[...] = early_pulls[...]

    def add_late(lefts):
        def project(part, cols):
            return back[part, cols].astype(jnp.float32) - early_ref[part, cols].astype(jnp.float32)

        add_sums(lefts, chunk, project, inverse_ref, act_ref, gain_ref, gain_sum, pulls)

    steps = [step for group in groups for step in group]
    if len(steps) == 1:
        late_z = behind(z, steps[0], line)
        for owner_z in range(line):
            first = owner_z * plane * width // 128 * 128
            after = (owner_z + 1) * plane * width

            @pl.when(late_z == owner_z)
            def _():
                add_late(range(first, after, 128))
    else:
        add_late(range(0, features, 128))
    inverse = inverse_ref[...]
    pull = jnp.broadcast_to(jnp.sum(pulls[...], axis=1, keepdims=True), pulls.shape) / features
    pulls[...] = pull * inverse * inverse * inverse

    def terms(index, _):
        part = pl.ds(pl.multiple_of(index * chunk, chunk), chunk)
        inverse = inverse_ref[part, :]
        pull = pulls[part, :]
        for left in range(0, features, 128):
            cols = slice(left, left + 128)
            scaled = back[part, cols].astype(jnp.float32) * gain_ref[:, cols]
            local = inverse * scaled - act_ref[part, cols].astype(jnp.float32) * pull
            local_ref[part, cols] = local
            passed_ref[part, cols] = (top_ref[part, cols].astype(jnp.float32) + local).astype(jnp.bfloat16)
        return 0

    lax.fori_loop(0, rows // chunk, terms, 0)
    total = jnp.sum(gain_sum[...], axis=0, keepdims=True)
    for block in range(line * plane):
        gain_blocks[block] = total[:, block * width : (block + 1) * width]
    if not early_steps:
        gain_outs[0][...] = gain_blocks[...]
        return
    for step, gain_out in enumerate(gain_outs[:plane]):
        gain_out[...] = gain_blocks[late_z * plane + ahead(q, step, plane)]
    for line_step, gain_out in zip(early_steps, gain_outs[plane:]):
        gain_out[...] = sum(part[behind(z, line_step, line)] for part in in_plane[1:]) + in_plane[0][
            behind(z, line_step, line)
        ]


def finish(line, plane, groups, early_steps, seq_rows, early, early_pulls, inverse, act, top, gain, pieces, in_plane):
    rows, features = act.shape
    blocks = line * plane
    width = features // blocks
    vmem = pl.BlockSpec(memory_space=pltpu.VMEM)
    outs = [
        jax.ShapeDtypeStruct((rows, features), jnp.bfloat16),
        jax.ShapeDtypeStruct((rows, features), jnp.float32),
    ]
    if early_steps:
        outs += [jax.ShapeDtypeStruct((1, width), jnp.float32)] * (plane + len(early_steps))
    else:
        outs += [jax.ShapeDtypeStruct((blocks, 1, width), jnp.float32)]
    scratch = [
        pltpu.VMEM((blocks,) + pieces[0].shape[1:], jnp.bfloat16),
        pltpu.VMEM((rows, features), jnp.bfloat16),
        pltpu.VMEM((8, features), jnp.float32),
        pltpu.VMEM((rows, 128), jnp.float32),
        pltpu.VMEM((blocks, 1, width), jnp.float32),
    ]
    return pl.pallas_call(
        functools.partial(finish_kernel, line, plane, groups, early_steps, seq_rows, math.gcd(rows, 32)),
        out_shape=outs,
        in_specs=[vmem] * (6 + len(pieces) + len(in_plane)),
        out_specs=[vmem] * len(outs),
        scratch_shapes=scratch,
        compiler_params=pltpu.CompilerParams(
            vmem_limit_bytes=grant(early, early_pulls, act, top, *pieces, *outs, *scratch)
        ),
        cost_estimate=pl.CostEstimate(
            flops=16 * rows * features, bytes_accessed=12 * rows * features, transcendentals=0
        ),
        name="norm_backward",
    )(early, early_pulls, inverse, act, top, gain, *pieces, *in_plane)


def hand_kernel(turn, chunk, incoming_ref, local_ref, result_ref, out_ref, loaded, staged, arrived, copied):
    rows, features = local_ref.shape
    parts = [pl.ds(start, chunk) for start in range(0, rows, chunk)]
    is_turn = lax.axis_index("section") == turn

    @pl.when(is_turn)
    def _():
        loads = [
            pltpu.make_async_copy(incoming_ref.at[part], loaded.at[part], arrived.at[index])
            for index, part in enumerate(parts)
        ]
        stores = [
            pltpu.make_async_copy(staged.at[part], out_ref.at[part], copied.at[index])
            for index, part in enumerate(parts)
        ]
        for load in loads:
            load.start()
        for part, load, store in zip(parts, loads, stores):
            load.wait()
            for left in range(0, features, 128):
                cols = slice(left, left + 128)
                staged[part, cols] = (loaded[part, cols].astype(jnp.float32) + local_ref[part, cols]).astype(
                    jnp.bfloat16
                )
            store.start()
        for store in stores:
            store.wait()

    @pl.when(jnp.logical_not(is_turn))
    def _():
        copies = [
            pltpu.make_async_copy(result_ref.at[part], out_ref.at[part], copied.at[index])
            for index, part in enumerate(parts)
        ]
        for copy in copies:
            copy.start()
        for copy in copies:
            copy.wait()


def hand_on(turn, chunk, incoming, local, result):
    rows, features = local.shape
    vmem = pl.BlockSpec(memory_space=pltpu.VMEM)
    hbm = pl.BlockSpec(memory_space=pl.ANY)
    return pl.pallas_call(
        functools.partial(hand_kernel, turn, chunk),
        out_shape=jax.ShapeDtypeStruct((rows, features), jnp.bfloat16),
        in_specs=[hbm, vmem, hbm],
        out_specs=hbm,
        scratch_shapes=[
            pltpu.VMEM((rows, features), jnp.bfloat16),
            pltpu.VMEM((rows, features), jnp.bfloat16),
            pltpu.SemaphoreType.DMA((rows // chunk,)),
            pltpu.SemaphoreType.DMA((rows // chunk,)),
        ],
        compiler_params=pltpu.CompilerParams(vmem_limit_bytes=grant(incoming, local, result)),
        cost_estimate=pl.CostEstimate(
            flops=rows * features, bytes_accessed=8 * rows * features, transcendentals=0
        ),
        name="hand_on",
    )(incoming, local, result)


def sum_kernel(scale, *refs):
    total = None
    for ref in refs[:-1]:
        rows = [ref[index] for index in range(ref.shape[0])] if len(ref.shape) == 3 else [ref[...]]
        for row in rows:
            total = row if total is None else total + row
    refs[-1][...] = total * scale


def sum_scaled(parts, scale):
    vmem = pl.BlockSpec(memory_space=pltpu.VMEM)
    size = sum(part.size for part in parts)
    return pl.pallas_call(
        functools.partial(sum_kernel, scale),
        out_shape=jax.ShapeDtypeStruct((1, parts[0].shape[-1]), jnp.float32),
        in_specs=[vmem] * len(parts),
        out_specs=vmem,
        compiler_params=pltpu.CompilerParams(vmem_limit_bytes=mebibyte),
        cost_estimate=pl.CostEstimate(flops=size, bytes_accessed=4 * size, transcendentals=0),
        name="sum_scaled",
    )(*parts)


def owners_sums(blocks):
    return lax.all_to_all(blocks, "dp", split_axis=0, concat_axis=0, tiled=True)


def to_owners(blocks, plane_steps, line_steps, line, plane):
    landed = []
    for block, plane_step, line_step in zip(blocks, plane_steps, line_steps):
        pairs = [
            (z * plane + q, behind(z, line_step, line) * plane + ahead(q, plane_step, plane))
            for z in range(line)
            for q in range(plane)
        ]
        landed.append(lax.ppermute(block, "dp", pairs) if plane_step or line_step else block)
    return landed


def sent_back(group_products, line, plane):
    return [group_products[0]] + [
        along_plane(group_products[step], step, line, plane, back=True) for step in range(1, plane)
    ]


def gathered_products(seq_rows, tokens, shard, line, plane):
    held = {0: shard}
    groups = [(0,)]
    first = products(seq_rows, tokens, [shard])
    if line & (line - 1):
        for step in range(1, line):
            held[step] = along_line(shard, step, line, plane)
        groups.append(tuple(range(1, (line + 1) // 2)))
    elif line > 1:
        distance = line // 2
        while distance:
            held[distance] = along_line(shard, distance, line, plane)
            distance //= 2
        groups.append(tuple(sorted(step for step in held if step)))
        far = line // 2
        held[far], own = lax.optimization_barrier((held[far], first[0]))
        first = [own] + list(first[1:])
        distance = line // 4
        while distance:
            for step in sorted(held):
                if step and step % (2 * distance) == 0 and step + distance not in held:
                    held[step + distance] = along_line(held[step], distance, line, plane)
            distance //= 2
    groups.append(tuple(step for step in range(line) if not any(step in group for group in groups)))
    groups = [group for group in groups if group]
    pieces = [sent_back(first, line, plane)]
    for group in groups[1:]:
        shards = [held[step] for step in group]
        made = list(products(seq_rows, tokens, shards))
        if len(pieces) == 1:
            made[-1], pieces[0] = lax.optimization_barrier((made[-1], pieces[0]))
        pieces.append(sent_back(made, line, plane))
    return groups, pieces


def on_device(activations, key_grads, top_grad, norm_gains, w_key, lengths):
    micro_count, seq_rows, features = activations.shape[2:]
    rows = micro_count * seq_rows
    replicas = lax.axis_size("dp")
    sections = lax.axis_size("section")
    plane = plane_size(replicas)
    line = replicas // plane
    grad_scale = 1.0 / math.sqrt(replicas * rows)
    act = activations.reshape(rows, features)

    key_rows = key_grads.reshape(rows, key_grads.shape[-1])
    inverse, own_rows = lax.optimization_barrier((live_inverse(seq_rows, lengths[0], act), key_rows))
    tokens = [own_rows] + [along_plane(key_rows, step, line, plane) for step in range(1, plane)]
    groups, pieces = gathered_products(seq_rows, tokens, w_key[0], line, plane)
    split = max(1, len(groups) - 1)
    early, late = ([part[step] for step in range(plane) for part in some] for some in (pieces[:split], pieces[split:]))
    early_steps, late_steps = (
        [step for group in some for step in group] for some in (groups[:split], groups[split:])
    )
    direct = len(late_steps) == 1
    early, pulls, *early_gains = placed_early(
        line, plane, groups[:split], seq_rows, direct, inverse, act, norm_gains, early
    )
    in_plane = []
    if direct:
        in_plane = to_owners(early_gains, range(plane), [0] * plane, line, plane)
    passed, local, *gains = finish(
        line,
        plane,
        groups[split:],
        early_steps if direct else [],
        seq_rows,
        early,
        pulls,
        inverse,
        act,
        top_grad.reshape(rows, features),
        norm_gains,
        late,
        in_plane,
    )
    if direct:
        gain_parts = to_owners(gains[:plane], range(plane), late_steps * plane, line, plane)
        gain_parts += to_owners(gains[plane:], [0] * len(early_steps), early_steps, line, plane)
    else:
        gain_parts = [owners_sums(blocks) for blocks in early_gains + gains]

    result = passed
    for turn in range(sections - 2, -1, -1):
        incoming = lax.ppermute(result, "section", [(turn + 1, turn)])
        result = hand_on(turn, seq_rows, incoming, local, result)

    gain_parts, result = lax.optimization_barrier((gain_parts, result))
    grad_shard = sum_scaled(gain_parts, grad_scale)
    return (result.reshape(activations.shape), grad_shard)


def solution(mesh):
    placed = (
        P("section", "dp", None, None, None),
        P("section", "dp", None, None, None),
        P("dp", None, None, None),
        P("section", None),
        P("section", "dp", None),
        P("dp", None),
    )
    return jax.shard_map(
        on_device,
        mesh=mesh,
        in_specs=placed,
        out_specs=(P("section", "dp", None, None, None), P("section", "dp")),
        check_vma=False,
    )
```

```python
import functools
import math

import jax
import jax.numpy as jnp
from jax import lax
from jax.experimental import pallas as pl
from jax.experimental.pallas import tpu as pltpu
from jax.sharding import PartitionSpec as P

norm_epsilon = 1e-05
mebibyte = 1024 * 1024
product_cost = 10


def grant(*arrays):
    total = 4 * mebibyte
    for array in arrays:
        lanes = -(-array.shape[-1] // 128) * 128
        total += math.prod(array.shape[:-1]) * lanes * jnp.dtype(array.dtype).itemsize
    return -(-total // mebibyte) * mebibyte


def plane_size(replicas):
    size = 1
    while (2 * size) ** 2 <= replicas and replicas % (2 * size) == 0:
        size *= 2
    return size


def ahead(place, step, count):
    if count & (count - 1) == 0:
        return place ^ step
    return (place + step) % count


def behind(place, step, count):
    if count & (count - 1) == 0:
        return place ^ step
    return (place + count - step) % count


def along_line(value, step, line, plane):
    pairs = [
        (z * plane + q, ahead(z, step, line) * plane + q)
        for z in range(line)
        for q in range(plane)
    ]
    return lax.ppermute(value, "dp", pairs)


def along_plane(value, step, line, plane, back=False):
    partner = behind if back else ahead
    pairs = [
        (z * plane + q, z * plane + partner(q, step, plane))
        for z in range(line)
        for q in range(plane)
    ]
    return lax.ppermute(value, "dp", pairs)


def product_kernel(token_count, weight_count, seq_rows, *refs):
    tokens = refs[:token_count]
    weights = refs[token_count : token_count + weight_count]
    outs = refs[token_count + weight_count :]
    for token_ref, out_ref in zip(tokens, outs):
        for index, weight_ref in enumerate(weights):
            product = lax.dot_general(
                token_ref[...],
                weight_ref[...],
                (((1,), (1,)), ((), ())),
                preferred_element_type=jnp.float32,
            ).astype(out_ref.dtype)
            width = product.shape[1]
            for micro in range(product.shape[0] // seq_rows):
                out_ref[index, :, micro * width : (micro + 1) * width] = product[
                    micro * seq_rows : (micro + 1) * seq_rows, :
                ]


def products(seq_rows, tokens, weights):
    rows, depth = tokens[0].shape
    width = weights[0].shape[0]
    count = len(weights)
    folded = (count, seq_rows, rows // seq_rows * width)
    outs = [jax.ShapeDtypeStruct(folded, jnp.bfloat16) for _ in tokens]
    return pl.pallas_call(
        functools.partial(product_kernel, len(tokens), count, seq_rows),
        out_shape=outs,
        in_specs=[pl.BlockSpec(memory_space=pltpu.VMEM)] * (len(tokens) + count),
        out_specs=[pl.BlockSpec(memory_space=pltpu.VMEM)] * len(tokens),
        compiler_params=pltpu.CompilerParams(vmem_limit_bytes=grant(*tokens, *weights, *outs)),
        cost_estimate=pl.CostEstimate(
            flops=product_cost * 2 * rows * depth * width * count * len(tokens),
            bytes_accessed=2 * (rows * depth * len(tokens) + depth * width * count + rows * width * count * len(tokens)),
            transcendentals=0,
        ),
        name="token_products",
    )(*tokens, *weights)


def column_tile(features, most=512):
    tile = 128
    for width in range(128, most + 1, 128):
        if features % width == 0:
            tile = width
    return tile


def inverse_kernel(seq_rows, chunk, tile, lengths_ref, act_ref, inverse_ref):
    rows, features = act_ref.shape

    def one_chunk(index, _):
        start = pl.multiple_of(index * chunk, chunk)
        part = pl.ds(start, chunk)
        squares = jnp.zeros((chunk, 128), jnp.float32)
        for left in range(0, features, tile):
            wide = act_ref[part, left : left + tile].astype(jnp.float32)
            wide = wide * wide
            for lane in range(0, tile, 128):
                squares = squares + wide[:, lane : lane + 128]
        mean = jnp.sum(squares, axis=1, keepdims=True) / features
        position = lax.broadcasted_iota(jnp.int32, (chunk, 1), 0) + lax.rem(start, seq_rows)
        keep = position < lengths_ref[lax.div(start, seq_rows)]
        inverse = jnp.where(keep, lax.rsqrt(mean + norm_epsilon), 0.0)
        inverse_ref[part, :] = jnp.broadcast_to(inverse, (chunk, 128))
        return 0

    lax.fori_loop(0, rows // chunk, one_chunk, 0)


def live_inverse(seq_rows, lengths, act):
    rows, features = act.shape
    return pl.pallas_call(
        functools.partial(inverse_kernel, seq_rows, math.gcd(seq_rows, 16), column_tile(features)),
        out_shape=jax.ShapeDtypeStruct((rows, 128), jnp.float32),
        in_specs=[pl.BlockSpec(memory_space=pltpu.SMEM), pl.BlockSpec(memory_space=pltpu.VMEM)],
        out_specs=pl.BlockSpec(memory_space=pltpu.VMEM),
        compiler_params=pltpu.CompilerParams(vmem_limit_bytes=grant(act)),
        cost_estimate=pl.CostEstimate(
            flops=2 * rows * features, bytes_accessed=2 * rows * features, transcendentals=rows
        ),
        name="live_inverse",
    )(lengths, act)


def relative(owner, place, count):
    if count & (count - 1) == 0:
        return owner ^ place
    return (place + count - owner) % count


def place_pieces(line, plane, groups, seq_rows, pieces, held, back):
    width = back.shape[1] // (line * plane)
    me = lax.axis_index("dp")
    z, q = lax.div(me, plane), lax.rem(me, plane)
    for step in range(plane):
        owner_q = ahead(q, step, plane)
        for group_index, group in enumerate(groups):
            piece = pieces[step * len(groups) + group_index]
            for index, line_step in enumerate(group):
                held[behind(z, line_step, line) * plane + owner_q] = piece[index]
    steps = [line_step for group in groups for line_step in group]
    for owner_z in range(line):
        line_step = relative(owner_z, z, line)
        here = functools.reduce(jnp.logical_or, [line_step == step for step in steps])

        @pl.when(here)
        def _():
            for micro in range(back.shape[0] // seq_rows):
                rows = slice(micro * seq_rows, (micro + 1) * seq_rows)
                for block in range(owner_z * plane, (owner_z + 1) * plane):
                    back[rows, block * width : (block + 1) * width] = held[
                        block, :, micro * width : (micro + 1) * width
                    ]


def add_sums(lefts, chunk, project, inverse_ref, act_ref, gain_ref, gain_sum, pulls):
    rows = act_ref.shape[0]

    def one_chunk(index, _):
        part = pl.ds(pl.multiple_of(index * chunk, chunk), chunk)
        inverse = inverse_ref[part, :]
        pull = pulls[part, :]
        for left in lefts:
            cols = slice(left, left + 128)
            both = act_ref[part, cols].astype(jnp.float32) * project(part, cols)
            pull = pull + both * gain_ref[:, cols]
            both = both * inverse
            folded = both[:8, :]
            for row in range(8, chunk, 8):
                folded = folded + both[row : row + 8, :]
            gain_sum[:, cols] += folded
        pulls[part, :] = pull
        return 0

    lax.fori_loop(0, rows // chunk, one_chunk, 0)


def early_kernel(line, plane, groups, seq_rows, chunk, inverse_ref, act_ref, gain_ref, *refs):
    pieces = refs[:-4]
    back, pulls, gain_sum, held = refs[-4:]
    back[...] = jnp.zeros_like(back)
    place_pieces(line, plane, groups, seq_rows, pieces, held, back)
    gain_sum[...] = jnp.zeros_like(gain_sum)
    pulls[...] = jnp.zeros_like(pulls)
    add_sums(
        range(0, back.shape[1], 128),
        chunk,
        lambda part, cols: back[part, cols].astype(jnp.float32),
        inverse_ref,
        act_ref,
        gain_ref,
        gain_sum,
        pulls,
    )


def placed_early(line, plane, groups, seq_rows, inverse, act, gain, pieces):
    rows, features = act.shape
    vmem = pl.BlockSpec(memory_space=pltpu.VMEM)
    outs = [
        jax.ShapeDtypeStruct((rows, features), jnp.bfloat16),
        jax.ShapeDtypeStruct((rows, 128), jnp.float32),
        jax.ShapeDtypeStruct((8, features), jnp.float32),
    ]
    scratch = [pltpu.VMEM((line * plane,) + pieces[0].shape[1:], jnp.bfloat16)]
    return pl.pallas_call(
        functools.partial(early_kernel, line, plane, groups, seq_rows, math.gcd(rows, 32)),
        out_shape=outs,
        in_specs=[vmem] * (3 + len(pieces)),
        out_specs=[vmem] * len(outs),
        scratch_shapes=scratch,
        compiler_params=pltpu.CompilerParams(
            vmem_limit_bytes=grant(inverse, act, gain, *pieces, *outs, *scratch)
        ),
        cost_estimate=pl.CostEstimate(
            flops=8 * rows * features, bytes_accessed=8 * rows * features, transcendentals=0
        ),
        name="placed_early",
    )(inverse, act, gain, *pieces)


def finish_kernel(
    line, plane, groups, seq_rows, chunk, early_ref, early_pulls, early_gains, inverse_ref, act_ref, top_ref, gain_ref, *refs
):
    pieces = refs[:-7]
    passed_ref, local_ref, gain_out, held, back, gain_sum, pulls = refs[-7:]
    rows, features = back.shape
    width = features // (line * plane)
    me = lax.axis_index("dp")
    back[...] = early_ref[...]
    place_pieces(line, plane, groups, seq_rows, pieces, held, back)
    gain_sum[...] = early_gains[...]
    pulls[...] = early_pulls[...]

    def add_late(lefts):
        def project(part, cols):
            return back[part, cols].astype(jnp.float32) - early_ref[part, cols].astype(jnp.float32)

        add_sums(lefts, chunk, project, inverse_ref, act_ref, gain_ref, gain_sum, pulls)

    steps = [step for group in groups for step in group]
    if len(steps) == 1:
        late_z = behind(lax.div(me, plane), steps[0], line)
        for owner_z in range(line):
            first = owner_z * plane * width // 128 * 128
            after = (owner_z + 1) * plane * width

            @pl.when(late_z == owner_z)
            def _():
                add_late(range(first, after, 128))
    else:
        add_late(range(0, features, 128))
    total = jnp.sum(gain_sum[...], axis=0, keepdims=True)
    for block in range(line * plane):
        gain_out[block] = total[:, block * width : (block + 1) * width]
    inverse = inverse_ref[...]
    pull = jnp.broadcast_to(jnp.sum(pulls[...], axis=1, keepdims=True), pulls.shape) / features
    pulls[...] = pull * inverse * inverse * inverse

    def terms(index, _):
        part = pl.ds(pl.multiple_of(index * chunk, chunk), chunk)
        inverse = inverse_ref[part, :]
        pull = pulls[part, :]
        for left in range(0, features, 128):
            cols = slice(left, left + 128)
            scaled = back[part, cols].astype(jnp.float32) * gain_ref[:, cols]
            local = inverse * scaled - act_ref[part, cols].astype(jnp.float32) * pull
            local_ref[part, cols] = local
            passed_ref[part, cols] = (top_ref[part, cols].astype(jnp.float32) + local).astype(jnp.bfloat16)
        return 0

    lax.fori_loop(0, rows // chunk, terms, 0)


def finish(line, plane, groups, seq_rows, early, inverse, act, top, gain, pieces):
    rows, features = act.shape
    blocks = line * plane
    vmem = pl.BlockSpec(memory_space=pltpu.VMEM)
    outs = [
        jax.ShapeDtypeStruct((rows, features), jnp.bfloat16),
        jax.ShapeDtypeStruct((rows, features), jnp.float32),
        jax.ShapeDtypeStruct((blocks, 1, features // blocks), jnp.float32),
    ]
    scratch = [
        pltpu.VMEM((blocks,) + pieces[0].shape[1:], jnp.bfloat16),
        pltpu.VMEM((rows, features), jnp.bfloat16),
        pltpu.VMEM((8, features), jnp.float32),
        pltpu.VMEM((rows, 128), jnp.float32),
    ]
    return pl.pallas_call(
        functools.partial(finish_kernel, line, plane, groups, seq_rows, math.gcd(rows, 32)),
        out_shape=outs,
        in_specs=[vmem] * (4 + len(early) + len(pieces)),
        out_specs=[vmem] * len(outs),
        scratch_shapes=scratch,
        compiler_params=pltpu.CompilerParams(
            vmem_limit_bytes=grant(*early, act, top, *pieces, *outs, *scratch)
        ),
        cost_estimate=pl.CostEstimate(
            flops=16 * rows * features, bytes_accessed=12 * rows * features, transcendentals=0
        ),
        name="norm_backward",
    )(*early, inverse, act, top, gain, *pieces)


def hand_kernel(turn, chunk, incoming_ref, local_ref, result_ref, out_ref, loaded, staged, arrived, copied):
    rows, features = local_ref.shape
    parts = [pl.ds(start, chunk) for start in range(0, rows, chunk)]
    is_turn = lax.axis_index("section") == turn

    @pl.when(is_turn)
    def _():
        loads = [
            pltpu.make_async_copy(incoming_ref.at[part], loaded.at[part], arrived.at[index])
            for index, part in enumerate(parts)
        ]
        stores = [
            pltpu.make_async_copy(staged.at[part], out_ref.at[part], copied.at[index])
            for index, part in enumerate(parts)
        ]
        for load in loads:
            load.start()
        for part, load, store in zip(parts, loads, stores):
            load.wait()
            for left in range(0, features, 128):
                cols = slice(left, left + 128)
                staged[part, cols] = (loaded[part, cols].astype(jnp.float32) + local_ref[part, cols]).astype(
                    jnp.bfloat16
                )
            store.start()
        for store in stores:
            store.wait()

    @pl.when(jnp.logical_not(is_turn))
    def _():
        copies = [
            pltpu.make_async_copy(result_ref.at[part], out_ref.at[part], copied.at[index])
            for index, part in enumerate(parts)
        ]
        for copy in copies:
            copy.start()
        for copy in copies:
            copy.wait()


def hand_on(turn, chunk, incoming, local, result):
    rows, features = local.shape
    vmem = pl.BlockSpec(memory_space=pltpu.VMEM)
    hbm = pl.BlockSpec(memory_space=pl.ANY)
    return pl.pallas_call(
        functools.partial(hand_kernel, turn, chunk),
        out_shape=jax.ShapeDtypeStruct((rows, features), jnp.bfloat16),
        in_specs=[hbm, vmem, hbm],
        out_specs=hbm,
        scratch_shapes=[
            pltpu.VMEM((rows, features), jnp.bfloat16),
            pltpu.VMEM((rows, features), jnp.bfloat16),
            pltpu.SemaphoreType.DMA((rows // chunk,)),
            pltpu.SemaphoreType.DMA((rows // chunk,)),
        ],
        compiler_params=pltpu.CompilerParams(vmem_limit_bytes=grant(incoming, local, result)),
        cost_estimate=pl.CostEstimate(
            flops=rows * features, bytes_accessed=8 * rows * features, transcendentals=0
        ),
        name="hand_on",
    )(incoming, local, result)


def sum_kernel(scale, parts_ref, out_ref):
    total = parts_ref[0]
    for index in range(1, parts_ref.shape[0]):
        total = total + parts_ref[index]
    out_ref[...] = total * scale


def sum_scaled(parts, scale):
    vmem = pl.BlockSpec(memory_space=pltpu.VMEM)
    return pl.pallas_call(
        functools.partial(sum_kernel, scale),
        out_shape=jax.ShapeDtypeStruct(parts.shape[1:], jnp.float32),
        in_specs=[vmem],
        out_specs=vmem,
        compiler_params=pltpu.CompilerParams(vmem_limit_bytes=mebibyte),
        cost_estimate=pl.CostEstimate(flops=parts.size, bytes_accessed=4 * parts.size, transcendentals=0),
        name="sum_scaled",
    )(parts)


def sent_back(group_products, line, plane):
    return [group_products[0]] + [
        along_plane(group_products[step], step, line, plane, back=True) for step in range(1, plane)
    ]


def gathered_products(seq_rows, tokens, shard, line, plane):
    held = {0: shard}
    groups = [(0,)]
    first = products(seq_rows, tokens, [shard])
    if line & (line - 1):
        for step in range(1, line):
            held[step] = along_line(shard, step, line, plane)
        groups.append(tuple(range(1, (line + 1) // 2)))
    elif line > 1:
        distance = line // 2
        while distance:
            held[distance] = along_line(shard, distance, line, plane)
            distance //= 2
        groups.append(tuple(sorted(step for step in held if step)))
        far = line // 2
        held[far], own = lax.optimization_barrier((held[far], first[0]))
        first = [own] + list(first[1:])
        distance = line // 4
        while distance:
            for step in sorted(held):
                if step and step % (2 * distance) == 0 and step + distance not in held:
                    held[step + distance] = along_line(held[step], distance, line, plane)
            distance //= 2
    groups.append(tuple(step for step in range(line) if not any(step in group for group in groups)))
    groups = [group for group in groups if group]
    pieces = [sent_back(first, line, plane)]
    for group in groups[1:]:
        shards = [held[step] for step in group]
        made = list(products(seq_rows, tokens, shards))
        if len(pieces) == 1:
            made[-1], pieces[0] = lax.optimization_barrier((made[-1], pieces[0]))
        pieces.append(sent_back(made, line, plane))
    return groups, pieces


def on_device(activations, key_grads, top_grad, norm_gains, w_key, lengths):
    micro_count, seq_rows, features = activations.shape[2:]
    rows = micro_count * seq_rows
    replicas = lax.axis_size("dp")
    sections = lax.axis_size("section")
    plane = plane_size(replicas)
    line = replicas // plane
    grad_scale = 1.0 / math.sqrt(replicas * rows)
    act = activations.reshape(rows, features)

    key_rows = key_grads.reshape(rows, key_grads.shape[-1])
    inverse, own_rows = lax.optimization_barrier((live_inverse(seq_rows, lengths[0], act), key_rows))
    tokens = [own_rows] + [along_plane(key_rows, step, line, plane) for step in range(1, plane)]
    groups, pieces = gathered_products(seq_rows, tokens, w_key[0], line, plane)
    split = max(1, len(groups) - 1)
    early, late = ([part[step] for step in range(plane) for part in some] for some in (pieces[:split], pieces[split:]))
    early = placed_early(line, plane, groups[:split], seq_rows, inverse, act, norm_gains, early)
    top = top_grad.reshape(rows, features)
    passed, local, gain_blocks = finish(
        line, plane, groups[split:], seq_rows, early, inverse, act, top, norm_gains, late
    )

    result = passed
    for turn in range(sections - 2, -1, -1):
        incoming = lax.ppermute(result, "section", [(turn + 1, turn)])
        result = hand_on(turn, seq_rows, incoming, local, result)

    gain_parts = lax.all_to_all(gain_blocks, "dp", split_axis=0, concat_axis=0, tiled=True)
    gain_parts, result = lax.optimization_barrier((gain_parts, result))
    grad_shard = sum_scaled(gain_parts, grad_scale)
    return (result.reshape(activations.shape), grad_shard)


def solution(mesh):
    placed = (
        P("section", "dp", None, None, None),
        P("section", "dp", None, None, None),
        P("dp", None, None, None),
        P("section", None),
        P("section", "dp", None),
        P("dp", None),
    )
    return jax.shard_map(
        on_device,
        mesh=mesh,
        in_specs=placed,
        out_specs=(P("section", "dp", None, None, None), P("section", "dp")),
        check_vma=False,
    )
```

```python
import functools
import math

import jax
import jax.numpy as jnp
from jax import lax
from jax.experimental import pallas as pl
from jax.experimental.pallas import tpu as pltpu
from jax.sharding import PartitionSpec as P

norm_epsilon = 1e-05
mebibyte = 1024 * 1024
product_cost = 4


def grant(*arrays):
    total = 4 * mebibyte
    for array in arrays:
        lanes = -(-array.shape[-1] // 128) * 128
        total += math.prod(array.shape[:-1]) * lanes * jnp.dtype(array.dtype).itemsize
    return -(-total // mebibyte) * mebibyte


def plane_size(replicas):
    size = 1
    while (2 * size) ** 2 <= replicas and replicas % (2 * size) == 0:
        size *= 2
    return size


def ahead(place, step, count):
    if count & (count - 1) == 0:
        return place ^ step
    return (place + step) % count


def behind(place, step, count):
    if count & (count - 1) == 0:
        return place ^ step
    return (place + count - step) % count


def along_line(value, step, line, plane):
    pairs = [
        (z * plane + q, ahead(z, step, line) * plane + q)
        for z in range(line)
        for q in range(plane)
    ]
    return lax.ppermute(value, "dp", pairs)


def along_plane(value, step, line, plane, back=False):
    partner = behind if back else ahead
    pairs = [
        (z * plane + q, z * plane + partner(q, step, plane))
        for z in range(line)
        for q in range(plane)
    ]
    return lax.ppermute(value, "dp", pairs)


def product_kernel(token_count, weight_count, seq_rows, *refs):
    tokens = refs[:token_count]
    weights = refs[token_count : token_count + weight_count]
    outs = refs[token_count + weight_count :]
    for token_ref, out_ref in zip(tokens, outs):
        for index, weight_ref in enumerate(weights):
            product = lax.dot_general(
                token_ref[...],
                weight_ref[...],
                (((1,), (1,)), ((), ())),
                preferred_element_type=jnp.float32,
            ).astype(out_ref.dtype)
            width = product.shape[1]
            for micro in range(product.shape[0] // seq_rows):
                out_ref[index, :, micro * width : (micro + 1) * width] = product[
                    micro * seq_rows : (micro + 1) * seq_rows, :
                ]


def products(seq_rows, tokens, weights):
    rows, depth = tokens[0].shape
    width = weights[0].shape[0]
    count = len(weights)
    folded = (count, seq_rows, rows // seq_rows * width)
    outs = [jax.ShapeDtypeStruct(folded, jnp.bfloat16) for _ in tokens]
    return pl.pallas_call(
        functools.partial(product_kernel, len(tokens), count, seq_rows),
        out_shape=outs,
        in_specs=[pl.BlockSpec(memory_space=pltpu.VMEM)] * (len(tokens) + count),
        out_specs=[pl.BlockSpec(memory_space=pltpu.VMEM)] * len(tokens),
        compiler_params=pltpu.CompilerParams(vmem_limit_bytes=grant(*tokens, *weights, *outs)),
        cost_estimate=pl.CostEstimate(
            flops=product_cost * 2 * rows * depth * width * count * len(tokens),
            bytes_accessed=2 * (rows * depth * len(tokens) + depth * width * count + rows * width * count * len(tokens)),
            transcendentals=0,
        ),
        name="token_products",
    )(*tokens, *weights)


def column_tile(features, most=512):
    tile = 128
    for width in range(128, most + 1, 128):
        if features % width == 0:
            tile = width
    return tile


def inverse_kernel(seq_rows, chunk, tile, lengths_ref, act_ref, inverse_ref):
    rows, features = act_ref.shape

    def one_chunk(index, _):
        start = pl.multiple_of(index * chunk, chunk)
        part = pl.ds(start, chunk)
        squares = jnp.zeros((chunk, 128), jnp.float32)
        for left in range(0, features, tile):
            wide = act_ref[part, left : left + tile].astype(jnp.float32)
            wide = wide * wide
            for lane in range(0, tile, 128):
                squares = squares + wide[:, lane : lane + 128]
        mean = jnp.sum(squares, axis=1, keepdims=True) / features
        position = lax.broadcasted_iota(jnp.int32, (chunk, 1), 0) + lax.rem(start, seq_rows)
        keep = position < lengths_ref[lax.div(start, seq_rows)]
        inverse = jnp.where(keep, lax.rsqrt(mean + norm_epsilon), 0.0)
        inverse_ref[part, :] = jnp.broadcast_to(inverse, (chunk, 128))
        return 0

    lax.fori_loop(0, rows // chunk, one_chunk, 0)


def live_inverse(seq_rows, lengths, act):
    rows, features = act.shape
    return pl.pallas_call(
        functools.partial(inverse_kernel, seq_rows, math.gcd(seq_rows, 16), column_tile(features)),
        out_shape=jax.ShapeDtypeStruct((rows, 128), jnp.float32),
        in_specs=[pl.BlockSpec(memory_space=pltpu.SMEM), pl.BlockSpec(memory_space=pltpu.VMEM)],
        out_specs=pl.BlockSpec(memory_space=pltpu.VMEM),
        compiler_params=pltpu.CompilerParams(vmem_limit_bytes=grant(act)),
        cost_estimate=pl.CostEstimate(
            flops=2 * rows * features, bytes_accessed=2 * rows * features, transcendentals=rows
        ),
        name="live_inverse",
    )(lengths, act)


def relative(owner, place, count):
    if count & (count - 1) == 0:
        return owner ^ place
    return (place + count - owner) % count


def place_pieces(line, plane, groups, seq_rows, pieces, held, back):
    width = back.shape[1] // (line * plane)
    me = lax.axis_index("dp")
    z, q = lax.div(me, plane), lax.rem(me, plane)
    for step in range(plane):
        owner_q = ahead(q, step, plane)
        for group_index, group in enumerate(groups):
            piece = pieces[step * len(groups) + group_index]
            for index, line_step in enumerate(group):
                held[behind(z, line_step, line) * plane + owner_q] = piece[index]
    steps = [line_step for group in groups for line_step in group]
    for owner_z in range(line):
        line_step = relative(owner_z, z, line)
        here = functools.reduce(jnp.logical_or, [line_step == step for step in steps])

        @pl.when(here)
        def _():
            for micro in range(back.shape[0] // seq_rows):
                rows = slice(micro * seq_rows, (micro + 1) * seq_rows)
                for block in range(owner_z * plane, (owner_z + 1) * plane):
                    back[rows, block * width : (block + 1) * width] = held[
                        block, :, micro * width : (micro + 1) * width
                    ]


def add_sums(lefts, chunk, project, inverse_ref, act_ref, gain_ref, gain_sum, pulls):
    rows = act_ref.shape[0]

    def one_chunk(index, _):
        part = pl.ds(pl.multiple_of(index * chunk, chunk), chunk)
        inverse = inverse_ref[part, :]
        pull = pulls[part, :]
        for left in lefts:
            cols = slice(left, left + 128)
            both = act_ref[part, cols].astype(jnp.float32) * project(part, cols)
            pull = pull + both * gain_ref[:, cols]
            both = both * inverse
            folded = both[:8, :]
            for row in range(8, chunk, 8):
                folded = folded + both[row : row + 8, :]
            gain_sum[:, cols] += folded
        pulls[part, :] = pull
        return 0

    lax.fori_loop(0, rows // chunk, one_chunk, 0)


def early_kernel(line, plane, groups, seq_rows, chunk, inverse_ref, act_ref, gain_ref, *refs):
    pieces = refs[:-4]
    back, pulls, gain_sum, held = refs[-4:]
    back[...] = jnp.zeros_like(back)
    place_pieces(line, plane, groups, seq_rows, pieces, held, back)
    gain_sum[...] = jnp.zeros_like(gain_sum)
    pulls[...] = jnp.zeros_like(pulls)
    add_sums(
        range(0, back.shape[1], 128),
        chunk,
        lambda part, cols: back[part, cols].astype(jnp.float32),
        inverse_ref,
        act_ref,
        gain_ref,
        gain_sum,
        pulls,
    )


def placed_early(line, plane, groups, seq_rows, inverse, act, gain, pieces):
    rows, features = act.shape
    vmem = pl.BlockSpec(memory_space=pltpu.VMEM)
    outs = [
        jax.ShapeDtypeStruct((rows, features), jnp.bfloat16),
        jax.ShapeDtypeStruct((rows, 128), jnp.float32),
        jax.ShapeDtypeStruct((8, features), jnp.float32),
    ]
    scratch = [pltpu.VMEM((line * plane,) + pieces[0].shape[1:], jnp.bfloat16)]
    return pl.pallas_call(
        functools.partial(early_kernel, line, plane, groups, seq_rows, math.gcd(rows, 32)),
        out_shape=outs,
        in_specs=[vmem] * (3 + len(pieces)),
        out_specs=[vmem] * len(outs),
        scratch_shapes=scratch,
        compiler_params=pltpu.CompilerParams(
            vmem_limit_bytes=grant(inverse, act, gain, *pieces, *outs, *scratch)
        ),
        cost_estimate=pl.CostEstimate(
            flops=8 * rows * features, bytes_accessed=8 * rows * features, transcendentals=0
        ),
        name="placed_early",
    )(inverse, act, gain, *pieces)


def finish_kernel(
    line, plane, groups, seq_rows, chunk, early_ref, early_pulls, early_gains, inverse_ref, act_ref, top_ref, gain_ref, *refs
):
    pieces = refs[:-9]
    passed_ref, local_ref, gain_out, held, back, gain_sum, pulls, passing, copied = refs[-9:]
    rows, features = back.shape
    width = features // (line * plane)
    me = lax.axis_index("dp")
    back[...] = early_ref[...]
    place_pieces(line, plane, groups, seq_rows, pieces, held, back)
    gain_sum[...] = early_gains[...]
    pulls[...] = early_pulls[...]

    def add_late(lefts):
        def project(part, cols):
            return back[part, cols].astype(jnp.float32) - early_ref[part, cols].astype(jnp.float32)

        add_sums(lefts, chunk, project, inverse_ref, act_ref, gain_ref, gain_sum, pulls)

    steps = [step for group in groups for step in group]
    if len(steps) == 1:
        late_z = behind(lax.div(me, plane), steps[0], line)
        for owner_z in range(line):
            first = owner_z * plane * width // 128 * 128
            after = (owner_z + 1) * plane * width

            @pl.when(late_z == owner_z)
            def _():
                add_late(range(first, after, 128))
    else:
        add_late(range(0, features, 128))
    total = jnp.sum(gain_sum[...], axis=0, keepdims=True)
    for block in range(line * plane):
        gain_out[block] = total[:, block * width : (block + 1) * width]
    inverse = inverse_ref[...]
    pull = jnp.broadcast_to(jnp.sum(pulls[...], axis=1, keepdims=True), pulls.shape) / features
    pulls[...] = pull * inverse * inverse * inverse

    def out_copy(index):
        part = pl.ds(pl.multiple_of(index * chunk, chunk), chunk)
        return pltpu.make_async_copy(passing.at[part], passed_ref.at[part], copied.at[index])

    def terms(index, _):
        part = pl.ds(pl.multiple_of(index * chunk, chunk), chunk)
        inverse = inverse_ref[part, :]
        pull = pulls[part, :]
        for left in range(0, features, 128):
            cols = slice(left, left + 128)
            scaled = back[part, cols].astype(jnp.float32) * gain_ref[:, cols]
            local = inverse * scaled - act_ref[part, cols].astype(jnp.float32) * pull
            local_ref[part, cols] = local
            passing[part, cols] = (top_ref[part, cols].astype(jnp.float32) + local).astype(jnp.bfloat16)
        out_copy(index).start()
        return 0

    lax.fori_loop(0, rows // chunk, terms, 0)
    for index in range(rows // chunk):
        out_copy(index).wait()


def finish(line, plane, groups, seq_rows, early, inverse, act, top, gain, pieces):
    rows, features = act.shape
    blocks = line * plane
    vmem = pl.BlockSpec(memory_space=pltpu.VMEM)
    outs = [
        jax.ShapeDtypeStruct((rows, features), jnp.bfloat16),
        jax.ShapeDtypeStruct((rows, features), jnp.float32),
        jax.ShapeDtypeStruct((blocks, 1, features // blocks), jnp.float32),
    ]
    scratch = [
        pltpu.VMEM((blocks,) + pieces[0].shape[1:], jnp.bfloat16),
        pltpu.VMEM((rows, features), jnp.bfloat16),
        pltpu.VMEM((8, features), jnp.float32),
        pltpu.VMEM((rows, 128), jnp.float32),
        pltpu.VMEM((rows, features), jnp.bfloat16),
    ]
    chunk = math.gcd(rows, 32)
    return pl.pallas_call(
        functools.partial(finish_kernel, line, plane, groups, seq_rows, chunk),
        out_shape=outs,
        in_specs=[vmem] * (4 + len(early) + len(pieces)),
        out_specs=[pl.BlockSpec(memory_space=pl.ANY), vmem, vmem],
        scratch_shapes=scratch + [pltpu.SemaphoreType.DMA((rows // chunk,))],
        compiler_params=pltpu.CompilerParams(
            vmem_limit_bytes=grant(*early, act, top, *pieces, *outs, *scratch)
        ),
        cost_estimate=pl.CostEstimate(
            flops=16 * rows * features, bytes_accessed=12 * rows * features, transcendentals=0
        ),
        name="norm_backward",
    )(*early, inverse, act, top, gain, *pieces)


def hand_kernel(turn, chunk, incoming_ref, local_ref, result_ref, out_ref, loaded, staged, arrived, copied):
    rows, features = local_ref.shape
    parts = [pl.ds(start, chunk) for start in range(0, rows, chunk)]
    is_turn = lax.axis_index("section") == turn

    def through(source, staging, work):
        loads = [
            pltpu.make_async_copy(source.at[part], loaded.at[part], arrived.at[index])
            for index, part in enumerate(parts)
        ]
        stores = [
            pltpu.make_async_copy(staging.at[part], out_ref.at[part], copied.at[index])
            for index, part in enumerate(parts)
        ]
        for load in loads:
            load.start()
        for part, load, store in zip(parts, loads, stores):
            load.wait()
            work(part)
            store.start()
        for store in stores:
            store.wait()

    def add_local(part):
        for left in range(0, features, 128):
            cols = slice(left, left + 128)
            staged[part, cols] = (loaded[part, cols].astype(jnp.float32) + local_ref[part, cols]).astype(jnp.bfloat16)

    @pl.when(is_turn)
    def _():
        through(incoming_ref, staged, add_local)

    @pl.when(jnp.logical_not(is_turn))
    def _():
        through(result_ref, loaded, lambda part: None)


def hand_on(turn, chunk, incoming, local, result):
    rows, features = local.shape
    vmem = pl.BlockSpec(memory_space=pltpu.VMEM)
    hbm = pl.BlockSpec(memory_space=pl.ANY)
    return pl.pallas_call(
        functools.partial(hand_kernel, turn, chunk),
        out_shape=jax.ShapeDtypeStruct((rows, features), jnp.bfloat16),
        in_specs=[hbm, vmem, hbm],
        out_specs=hbm,
        scratch_shapes=[
            pltpu.VMEM((rows, features), jnp.bfloat16),
            pltpu.VMEM((rows, features), jnp.bfloat16),
            pltpu.SemaphoreType.DMA((rows // chunk,)),
            pltpu.SemaphoreType.DMA((rows // chunk,)),
        ],
        compiler_params=pltpu.CompilerParams(vmem_limit_bytes=grant(incoming, local, result)),
        cost_estimate=pl.CostEstimate(
            flops=rows * features, bytes_accessed=8 * rows * features, transcendentals=0
        ),
        name="hand_on",
    )(incoming, local, result)


def sum_kernel(scale, parts_ref, out_ref):
    total = parts_ref[0]
    for index in range(1, parts_ref.shape[0]):
        total = total + parts_ref[index]
    out_ref[...] = total * scale


def sum_scaled(parts, scale):
    vmem = pl.BlockSpec(memory_space=pltpu.VMEM)
    return pl.pallas_call(
        functools.partial(sum_kernel, scale),
        out_shape=jax.ShapeDtypeStruct(parts.shape[1:], jnp.float32),
        in_specs=[vmem],
        out_specs=vmem,
        compiler_params=pltpu.CompilerParams(vmem_limit_bytes=mebibyte),
        cost_estimate=pl.CostEstimate(flops=parts.size, bytes_accessed=4 * parts.size, transcendentals=0),
        name="sum_scaled",
    )(parts)


def sent_back(group_products, line, plane):
    return [group_products[0]] + [
        along_plane(group_products[step], step, line, plane, back=True) for step in range(1, plane)
    ]


def gathered_products(seq_rows, tokens, shard, line, plane):
    held = {0: shard}
    groups = [(0,)]
    first = products(seq_rows, tokens, [shard])
    if line & (line - 1):
        for step in range(1, line):
            held[step] = along_line(shard, step, line, plane)
        groups.append(tuple(range(1, (line + 1) // 2)))
    elif line > 1:
        distance = line // 2
        while distance:
            held[distance] = along_line(shard, distance, line, plane)
            distance //= 2
        groups.append(tuple(sorted(step for step in held if step)))
        distance = line // 4
        while distance:
            for step in sorted(held):
                if step and step % (2 * distance) == 0 and step + distance not in held:
                    held[step + distance] = along_line(held[step], distance, line, plane)
            distance //= 2
    groups.append(tuple(step for step in range(line) if not any(step in group for group in groups)))
    groups = [group for group in groups if group]
    pieces = [sent_back(first, line, plane)]
    for group in groups[1:]:
        shards = [held[step] for step in group]
        made = list(products(seq_rows, tokens, shards))
        if len(pieces) == 1:
            made[-1], pieces[0] = lax.optimization_barrier((made[-1], pieces[0]))
        pieces.append(sent_back(made, line, plane))
    return groups, pieces


def on_device(activations, key_grads, top_grad, norm_gains, w_key, lengths):
    micro_count, seq_rows, features = activations.shape[2:]
    rows = micro_count * seq_rows
    replicas = lax.axis_size("dp")
    sections = lax.axis_size("section")
    plane = plane_size(replicas)
    line = replicas // plane
    grad_scale = 1.0 / math.sqrt(replicas * rows)
    act = activations.reshape(rows, features)

    key_rows = key_grads.reshape(rows, key_grads.shape[-1])
    inverse, own_rows = lax.optimization_barrier((live_inverse(seq_rows, lengths[0], act), key_rows))
    tokens = [own_rows] + [along_plane(key_rows, step, line, plane) for step in range(1, plane)]
    groups, pieces = gathered_products(seq_rows, tokens, w_key[0], line, plane)
    split = max(1, len(groups) - 1)
    early, late = ([part[step] for step in range(plane) for part in some] for some in (pieces[:split], pieces[split:]))
    early = placed_early(line, plane, groups[:split], seq_rows, inverse, act, norm_gains, early)
    top = top_grad.reshape(rows, features)
    passed, local, gain_blocks = finish(
        line, plane, groups[split:], seq_rows, early, inverse, act, top, norm_gains, late
    )

    result = passed
    for turn in range(sections - 2, -1, -1):
        incoming = lax.ppermute(result, "section", [(turn + 1, turn)])
        result = hand_on(turn, seq_rows, incoming, local, result)

    gain_parts = lax.all_to_all(gain_blocks, "dp", split_axis=0, concat_axis=0, tiled=True)
    gain_parts, result = lax.optimization_barrier((gain_parts, result))
    grad_shard = sum_scaled(gain_parts, grad_scale)
    return (result.reshape(activations.shape), grad_shard)


def solution(mesh):
    placed = (
        P("section", "dp", None, None, None),
        P("section", "dp", None, None, None),
        P("dp", None, None, None),
        P("section", None),
        P("section", "dp", None),
        P("dp", None),
    )
    return jax.shard_map(
        on_device,
        mesh=mesh,
        in_specs=placed,
        out_specs=(P("section", "dp", None, None, None), P("section", "dp")),
        check_vma=False,
    )
```

```python
import functools
import math

import jax
import jax.numpy as jnp
from jax import lax
from jax.experimental import pallas as pl
from jax.experimental.pallas import tpu as pltpu
from jax.sharding import PartitionSpec as P

norm_epsilon = 1e-05
mebibyte = 1024 * 1024
product_cost = 10


def grant(*arrays):
    total = 4 * mebibyte
    for array in arrays:
        lanes = -(-array.shape[-1] // 128) * 128
        total += math.prod(array.shape[:-1]) * lanes * jnp.dtype(array.dtype).itemsize
    return -(-total // mebibyte) * mebibyte


def plane_size(replicas):
    size = 1
    while (2 * size) ** 2 <= replicas and replicas % (2 * size) == 0:
        size *= 2
    return size


def ahead(place, step, count):
    if count & (count - 1) == 0:
        return place ^ step
    return (place + step) % count


def behind(place, step, count):
    if count & (count - 1) == 0:
        return place ^ step
    return (place + count - step) % count


def along_line(value, step, line, plane):
    pairs = [
        (z * plane + q, ahead(z, step, line) * plane + q)
        for z in range(line)
        for q in range(plane)
    ]
    return lax.ppermute(value, "dp", pairs)


def along_plane(value, step, line, plane, back=False):
    partner = behind if back else ahead
    pairs = [
        (z * plane + q, z * plane + partner(q, step, plane))
        for z in range(line)
        for q in range(plane)
    ]
    return lax.ppermute(value, "dp", pairs)


def product_kernel(token_count, weight_count, fold, *refs):
    tokens = refs[:token_count]
    weights = refs[token_count : token_count + weight_count]
    outs = refs[token_count + weight_count :]
    for token_ref, out_ref in zip(tokens, outs):
        for index, weight_ref in enumerate(weights):
            product = lax.dot_general(
                token_ref[...],
                weight_ref[...],
                (((1,), (1,)), ((), ())),
                preferred_element_type=jnp.float32,
            ).astype(out_ref.dtype)
            width = product.shape[1]
            for part in range(product.shape[0] // fold):
                out_ref[index, :, part * width : (part + 1) * width] = product[part * fold : (part + 1) * fold, :]


def products(fold, tokens, weights):
    rows, depth = tokens[0].shape
    width = weights[0].shape[0]
    count = len(weights)
    folded = (count, fold, rows // fold * width)
    outs = [jax.ShapeDtypeStruct(folded, jnp.bfloat16) for _ in tokens]
    return pl.pallas_call(
        functools.partial(product_kernel, len(tokens), count, fold),
        out_shape=outs,
        in_specs=[pl.BlockSpec(memory_space=pltpu.VMEM)] * (len(tokens) + count),
        out_specs=[pl.BlockSpec(memory_space=pltpu.VMEM)] * len(tokens),
        compiler_params=pltpu.CompilerParams(vmem_limit_bytes=grant(*tokens, *weights, *outs)),
        cost_estimate=pl.CostEstimate(
            flops=product_cost * 2 * rows * depth * width * count * len(tokens),
            bytes_accessed=2 * (rows * depth * len(tokens) + depth * width * count + rows * width * count * len(tokens)),
            transcendentals=0,
        ),
        name="token_products",
    )(*tokens, *weights)


def column_tile(features, most=512):
    tile = 128
    for width in range(128, most + 1, 128):
        if features % width == 0:
            tile = width
    return tile


def inverse_kernel(seq_rows, chunk, tile, lengths_ref, act_ref, inverse_ref):
    rows, features = act_ref.shape

    def one_chunk(index, _):
        start = pl.multiple_of(index * chunk, chunk)
        part = pl.ds(start, chunk)
        squares = jnp.zeros((chunk, 128), jnp.float32)
        for left in range(0, features, tile):
            wide = act_ref[part, left : left + tile].astype(jnp.float32)
            wide = wide * wide
            for lane in range(0, tile, 128):
                squares = squares + wide[:, lane : lane + 128]
        mean = jnp.sum(squares, axis=1, keepdims=True) / features
        position = lax.broadcasted_iota(jnp.int32, (chunk, 1), 0) + lax.rem(start, seq_rows)
        keep = position < lengths_ref[lax.div(start, seq_rows)]
        inverse = jnp.where(keep, lax.rsqrt(mean + norm_epsilon), 0.0)
        inverse_ref[part, :] = jnp.broadcast_to(inverse, (chunk, 128))
        return 0

    lax.fori_loop(0, rows // chunk, one_chunk, 0)


def live_inverse(seq_rows, lengths, act):
    rows, features = act.shape
    return pl.pallas_call(
        functools.partial(inverse_kernel, seq_rows, math.gcd(seq_rows, 16), column_tile(features)),
        out_shape=jax.ShapeDtypeStruct((rows, 128), jnp.float32),
        in_specs=[pl.BlockSpec(memory_space=pltpu.SMEM), pl.BlockSpec(memory_space=pltpu.VMEM)],
        out_specs=pl.BlockSpec(memory_space=pltpu.VMEM),
        compiler_params=pltpu.CompilerParams(vmem_limit_bytes=grant(act)),
        cost_estimate=pl.CostEstimate(
            flops=2 * rows * features, bytes_accessed=2 * rows * features, transcendentals=rows
        ),
        name="live_inverse",
    )(lengths, act)


def relative(owner, place, count):
    if count & (count - 1) == 0:
        return owner ^ place
    return (place + count - owner) % count


def place_pieces(line, plane, groups, fold, pieces, held, back):
    width = back.shape[1] // (line * plane)
    me = lax.axis_index("dp")
    z, q = lax.div(me, plane), lax.rem(me, plane)
    for step in range(plane):
        owner_q = ahead(q, step, plane)
        for group_index, group in enumerate(groups):
            piece = pieces[step * len(groups) + group_index]
            for index, line_step in enumerate(group):
                held[behind(z, line_step, line) * plane + owner_q] = piece[index]
    steps = [line_step for group in groups for line_step in group]
    for owner_z in range(line):
        line_step = relative(owner_z, z, line)
        here = functools.reduce(jnp.logical_or, [line_step == step for step in steps])

        @pl.when(here)
        def _():
            for part in range(back.shape[0] // fold):
                rows = slice(part * fold, (part + 1) * fold)
                for block in range(owner_z * plane, (owner_z + 1) * plane):
                    back[rows, block * width : (block + 1) * width] = held[
                        block, :, part * width : (part + 1) * width
                    ]


def add_sums(lefts, chunk, project, inverse_ref, act_ref, gain_ref, gain_sum, pulls):
    rows = act_ref.shape[0]

    def one_chunk(index, _):
        part = pl.ds(pl.multiple_of(index * chunk, chunk), chunk)
        inverse = inverse_ref[part, :]
        pull = pulls[part, :]
        for left in lefts:
            cols = slice(left, left + 128)
            both = act_ref[part, cols].astype(jnp.float32) * project(part, cols)
            pull = pull + both * gain_ref[:, cols]
            both = both * inverse
            folded = both[:8, :]
            for row in range(8, chunk, 8):
                folded = folded + both[row : row + 8, :]
            gain_sum[:, cols] += folded
        pulls[part, :] = pull
        return 0

    lax.fori_loop(0, rows // chunk, one_chunk, 0)


def early_kernel(line, plane, groups, fold, chunk, inverse_ref, act_ref, gain_ref, *refs):
    pieces = refs[:-4]
    back, pulls, gain_sum, held = refs[-4:]
    back[...] = jnp.zeros_like(back)
    place_pieces(line, plane, groups, fold, pieces, held, back)
    gain_sum[...] = jnp.zeros_like(gain_sum)
    pulls[...] = jnp.zeros_like(pulls)
    add_sums(
        range(0, back.shape[1], 128),
        chunk,
        lambda part, cols: back[part, cols].astype(jnp.float32),
        inverse_ref,
        act_ref,
        gain_ref,
        gain_sum,
        pulls,
    )


def placed_early(line, plane, groups, fold, inverse, act, gain, pieces):
    rows, features = act.shape
    vmem = pl.BlockSpec(memory_space=pltpu.VMEM)
    outs = [
        jax.ShapeDtypeStruct((rows, features), jnp.bfloat16),
        jax.ShapeDtypeStruct((rows, 128), jnp.float32),
        jax.ShapeDtypeStruct((8, features), jnp.float32),
    ]
    scratch = [pltpu.VMEM((line * plane,) + pieces[0].shape[1:], jnp.bfloat16)]
    return pl.pallas_call(
        functools.partial(early_kernel, line, plane, groups, fold, math.gcd(rows, 32)),
        out_shape=outs,
        in_specs=[vmem] * (3 + len(pieces)),
        out_specs=[vmem] * len(outs),
        scratch_shapes=scratch,
        compiler_params=pltpu.CompilerParams(
            vmem_limit_bytes=grant(inverse, act, gain, *pieces, *outs, *scratch)
        ),
        cost_estimate=pl.CostEstimate(
            flops=8 * rows * features, bytes_accessed=8 * rows * features, transcendentals=0
        ),
        name="placed_early",
    )(inverse, act, gain, *pieces)


def finish_kernel(
    line, plane, groups, fold, chunk, early_ref, early_pulls, early_gains, inverse_ref, act_ref, top_ref, gain_ref, *refs
):
    pieces = refs[:-9]
    passed_ref, local_ref, gain_out, held, back, gain_sum, pulls, passing, copied = refs[-9:]
    rows, features = back.shape
    width = features // (line * plane)
    me = lax.axis_index("dp")
    back[...] = early_ref[...]
    place_pieces(line, plane, groups, fold, pieces, held, back)
    gain_sum[...] = early_gains[...]
    pulls[...] = early_pulls[...]

    def add_late(lefts):
        def project(part, cols):
            return back[part, cols].astype(jnp.float32) - early_ref[part, cols].astype(jnp.float32)

        add_sums(lefts, chunk, project, inverse_ref, act_ref, gain_ref, gain_sum, pulls)

    steps = [step for group in groups for step in group]
    if len(steps) == 1:
        late_z = behind(lax.div(me, plane), steps[0], line)
        for owner_z in range(line):
            first = owner_z * plane * width // 128 * 128
            after = (owner_z + 1) * plane * width

            @pl.when(late_z == owner_z)
            def _():
                add_late(range(first, after, 128))
    else:
        add_late(range(0, features, 128))
    total = jnp.sum(gain_sum[...], axis=0, keepdims=True)
    for block in range(line * plane):
        gain_out[block] = total[:, block * width : (block + 1) * width]
    inverse = inverse_ref[...]
    pull = jnp.broadcast_to(jnp.sum(pulls[...], axis=1, keepdims=True), pulls.shape) / features
    pulls[...] = pull * inverse * inverse * inverse

    def out_copy(index):
        part = pl.ds(pl.multiple_of(index * chunk, chunk), chunk)
        return pltpu.make_async_copy(passing.at[part], passed_ref.at[part], copied.at[index])

    def terms(index, _):
        part = pl.ds(pl.multiple_of(index * chunk, chunk), chunk)
        inverse = inverse_ref[part, :]
        pull = pulls[part, :]
        for left in range(0, features, 128):
            cols = slice(left, left + 128)
            scaled = back[part, cols].astype(jnp.float32) * gain_ref[:, cols]
            local = inverse * scaled - act_ref[part, cols].astype(jnp.float32) * pull
            local_ref[part, cols] = local
            passing[part, cols] = (top_ref[part, cols].astype(jnp.float32) + local).astype(jnp.bfloat16)
        out_copy(index).start()
        return 0

    lax.fori_loop(0, rows // chunk, terms, 0)
    for index in range(rows // chunk):
        out_copy(index).wait()


def finish(line, plane, groups, fold, early, inverse, act, top, gain, pieces):
    rows, features = act.shape
    blocks = line * plane
    vmem = pl.BlockSpec(memory_space=pltpu.VMEM)
    outs = [
        jax.ShapeDtypeStruct((rows, features), jnp.bfloat16),
        jax.ShapeDtypeStruct((rows, features), jnp.float32),
        jax.ShapeDtypeStruct((blocks, 1, features // blocks), jnp.float32),
    ]
    scratch = [
        pltpu.VMEM((blocks,) + pieces[0].shape[1:], jnp.bfloat16),
        pltpu.VMEM((rows, features), jnp.bfloat16),
        pltpu.VMEM((8, features), jnp.float32),
        pltpu.VMEM((rows, 128), jnp.float32),
        pltpu.VMEM((rows, features), jnp.bfloat16),
    ]
    chunk = math.gcd(rows, 32)
    return pl.pallas_call(
        functools.partial(finish_kernel, line, plane, groups, fold, chunk),
        out_shape=outs,
        in_specs=[vmem] * (4 + len(early) + len(pieces)),
        out_specs=[pl.BlockSpec(memory_space=pl.ANY), vmem, vmem],
        scratch_shapes=scratch + [pltpu.SemaphoreType.DMA((rows // chunk,))],
        compiler_params=pltpu.CompilerParams(
            vmem_limit_bytes=grant(*early, act, top, *pieces, *outs, *scratch)
        ),
        cost_estimate=pl.CostEstimate(
            flops=16 * rows * features, bytes_accessed=12 * rows * features, transcendentals=0
        ),
        name="norm_backward",
    )(*early, inverse, act, top, gain, *pieces)


def hand_kernel(turn, chunk, incoming_ref, local_ref, result_ref, out_ref, loaded, staged, arrived, copied):
    rows, features = local_ref.shape
    parts = [pl.ds(start, chunk) for start in range(0, rows, chunk)]
    is_turn = lax.axis_index("section") == turn

    def through(source, staging, work):
        loads = [
            pltpu.make_async_copy(source.at[part], loaded.at[part], arrived.at[index])
            for index, part in enumerate(parts)
        ]
        stores = [
            pltpu.make_async_copy(staging.at[part], out_ref.at[part], copied.at[index])
            for index, part in enumerate(parts)
        ]
        for load in loads:
            load.start()
        for part, load, store in zip(parts, loads, stores):
            load.wait()
            work(part)
            store.start()
        for store in stores:
            store.wait()

    def add_local(part):
        for left in range(0, features, 128):
            cols = slice(left, left + 128)
            staged[part, cols] = (loaded[part, cols].astype(jnp.float32) + local_ref[part, cols]).astype(jnp.bfloat16)

    @pl.when(is_turn)
    def _():
        through(incoming_ref, staged, add_local)

    @pl.when(jnp.logical_not(is_turn))
    def _():
        through(result_ref, loaded, lambda part: None)


def hand_on(turn, chunk, incoming, local, result):
    rows, features = local.shape
    vmem = pl.BlockSpec(memory_space=pltpu.VMEM)
    hbm = pl.BlockSpec(memory_space=pl.ANY)
    return pl.pallas_call(
        functools.partial(hand_kernel, turn, chunk),
        out_shape=jax.ShapeDtypeStruct((rows, features), jnp.bfloat16),
        in_specs=[hbm, vmem, hbm],
        out_specs=hbm,
        scratch_shapes=[
            pltpu.VMEM((rows, features), jnp.bfloat16),
            pltpu.VMEM((rows, features), jnp.bfloat16),
            pltpu.SemaphoreType.DMA((rows // chunk,)),
            pltpu.SemaphoreType.DMA((rows // chunk,)),
        ],
        compiler_params=pltpu.CompilerParams(vmem_limit_bytes=grant(incoming, local, result)),
        cost_estimate=pl.CostEstimate(flops=0, bytes_accessed=0, transcendentals=0),
        name="hand_on",
    )(incoming, local, result)


def sum_kernel(scale, parts_ref, out_ref):
    total = parts_ref[0]
    for index in range(1, parts_ref.shape[0]):
        total = total + parts_ref[index]
    out_ref[...] = total * scale


def sum_scaled(parts, scale):
    vmem = pl.BlockSpec(memory_space=pltpu.VMEM)
    return pl.pallas_call(
        functools.partial(sum_kernel, scale),
        out_shape=jax.ShapeDtypeStruct(parts.shape[1:], jnp.float32),
        in_specs=[vmem],
        out_specs=vmem,
        compiler_params=pltpu.CompilerParams(vmem_limit_bytes=mebibyte),
        cost_estimate=pl.CostEstimate(flops=parts.size, bytes_accessed=4 * parts.size, transcendentals=0),
        name="sum_scaled",
    )(parts)


def sent_back(group_products, line, plane):
    return [group_products[0]] + [
        along_plane(group_products[step], step, line, plane, back=True) for step in range(1, plane)
    ]


def gathered_products(fold, tokens, shard, line, plane):
    held = {0: shard}
    groups = [(0,)]
    first = products(fold, tokens, [shard])
    if line & (line - 1):
        for step in range(1, line):
            held[step] = along_line(shard, step, line, plane)
        groups.append(tuple(range(1, (line + 1) // 2)))
    elif line > 1:
        distance = line // 2
        while distance:
            held[distance] = along_line(shard, distance, line, plane)
            distance //= 2
        groups.append(tuple(sorted(step for step in held if step)))
        far = line // 2
        held[far], own = lax.optimization_barrier((held[far], first[0]))
        first = [own] + list(first[1:])
        distance = line // 4
        while distance:
            for step in sorted(held):
                if step and step % (2 * distance) == 0 and step + distance not in held:
                    held[step + distance] = along_line(held[step], distance, line, plane)
            distance //= 2
    groups.append(tuple(step for step in range(line) if not any(step in group for group in groups)))
    groups = [group for group in groups if group]
    pieces = [sent_back(first, line, plane)]
    for group in groups[1:]:
        shards = [held[step] for step in group]
        made = list(products(fold, tokens, shards))
        if len(pieces) == 1:
            made[-1], pieces[0] = lax.optimization_barrier((made[-1], pieces[0]))
        pieces.append(sent_back(made, line, plane))
    return groups, pieces


def on_device(activations, key_grads, top_grad, norm_gains, w_key, lengths):
    micro_count, seq_rows, features = activations.shape[2:]
    rows = micro_count * seq_rows
    fold = math.gcd(rows, 16)
    replicas = lax.axis_size("dp")
    sections = lax.axis_size("section")
    plane = plane_size(replicas)
    line = replicas // plane
    grad_scale = 1.0 / math.sqrt(replicas * rows)
    act = activations.reshape(rows, features)

    key_rows = key_grads.reshape(rows, key_grads.shape[-1])
    inverse, own_rows = lax.optimization_barrier((live_inverse(seq_rows, lengths[0], act), key_rows))
    tokens = [own_rows] + [along_plane(key_rows, step, line, plane) for step in range(1, plane)]
    groups, pieces = gathered_products(fold, tokens, w_key[0], line, plane)
    split = max(1, len(groups) - 1)
    early, late = ([part[step] for step in range(plane) for part in some] for some in (pieces[:split], pieces[split:]))
    early = placed_early(line, plane, groups[:split], fold, inverse, act, norm_gains, early)
    top = top_grad.reshape(rows, features)
    passed, local, gain_blocks = finish(
        line, plane, groups[split:], fold, early, inverse, act, top, norm_gains, late
    )

    result = passed
    for turn in range(sections - 2, -1, -1):
        incoming = lax.ppermute(result, "section", [(turn + 1, turn)])
        result = hand_on(turn, seq_rows, incoming, local, result)

    gain_parts = lax.all_to_all(gain_blocks, "dp", split_axis=0, concat_axis=0, tiled=True)
    gain_parts, result = lax.optimization_barrier((gain_parts, result))
    grad_shard = sum_scaled(gain_parts, grad_scale)
    return (result.reshape(activations.shape), grad_shard)


def solution(mesh):
    placed = (
        P("section", "dp", None, None, None),
        P("section", "dp", None, None, None),
        P("dp", None, None, None),
        P("section", None),
        P("section", "dp", None),
        P("dp", None),
    )
    return jax.shard_map(
        on_device,
        mesh=mesh,
        in_specs=placed,
        out_specs=(P("section", "dp", None, None, None), P("section", "dp")),
        check_vma=False,
    )
```

```python
import functools
import math

import jax
import jax.numpy as jnp
from jax import lax
from jax.experimental import pallas as pl
from jax.experimental.pallas import tpu as pltpu
from jax.sharding import PartitionSpec as P

norm_epsilon = 1e-05
mebibyte = 1024 * 1024
product_cost = 10


def grant(*arrays):
    total = 4 * mebibyte
    for array in arrays:
        lanes = -(-array.shape[-1] // 128) * 128
        total += math.prod(array.shape[:-1]) * lanes * jnp.dtype(array.dtype).itemsize
    return -(-total // mebibyte) * mebibyte


def plane_size(replicas):
    size = 1
    while (2 * size) ** 2 <= replicas and replicas % (2 * size) == 0:
        size *= 2
    return size


def ahead(place, step, count):
    if count & (count - 1) == 0:
        return place ^ step
    return (place + step) % count


def behind(place, step, count):
    if count & (count - 1) == 0:
        return place ^ step
    return (place + count - step) % count


def along_line(value, step, line, plane):
    pairs = [
        (z * plane + q, ahead(z, step, line) * plane + q)
        for z in range(line)
        for q in range(plane)
    ]
    return lax.ppermute(value, "dp", pairs)


def along_plane(value, step, line, plane, back=False):
    partner = behind if back else ahead
    pairs = [
        (z * plane + q, z * plane + partner(q, step, plane))
        for z in range(line)
        for q in range(plane)
    ]
    return lax.ppermute(value, "dp", pairs)


def product_kernel(token_count, weight_count, fold, *refs):
    tokens = refs[:token_count]
    weights = refs[token_count : token_count + weight_count]
    outs = refs[token_count + weight_count :]
    for token_ref, out_ref in zip(tokens, outs):
        for index, weight_ref in enumerate(weights):
            product = lax.dot_general(
                token_ref[...],
                weight_ref[...],
                (((1,), (1,)), ((), ())),
                preferred_element_type=jnp.float32,
            ).astype(out_ref.dtype)
            width = product.shape[1]
            for part in range(product.shape[0] // fold):
                out_ref[index, :, part * width : (part + 1) * width] = product[part * fold : (part + 1) * fold, :]


def products(fold, tokens, weights):
    rows, depth = tokens[0].shape
    width = weights[0].shape[0]
    count = len(weights)
    folded = (count, fold, rows // fold * width)
    outs = [jax.ShapeDtypeStruct(folded, jnp.bfloat16) for _ in tokens]
    return pl.pallas_call(
        functools.partial(product_kernel, len(tokens), count, fold),
        out_shape=outs,
        in_specs=[pl.BlockSpec(memory_space=pltpu.VMEM)] * (len(tokens) + count),
        out_specs=[pl.BlockSpec(memory_space=pltpu.VMEM)] * len(tokens),
        compiler_params=pltpu.CompilerParams(vmem_limit_bytes=grant(*tokens, *weights, *outs)),
        cost_estimate=pl.CostEstimate(
            flops=product_cost * 2 * rows * depth * width * count * len(tokens),
            bytes_accessed=2 * (rows * depth * len(tokens) + depth * width * count + rows * width * count * len(tokens)),
            transcendentals=0,
        ),
        name="token_products",
    )(*tokens, *weights)


def column_tile(features, most=512):
    tile = 128
    for width in range(128, most + 1, 128):
        if features % width == 0:
            tile = width
    return tile


def inverse_kernel(seq_rows, chunk, tile, lengths_ref, act_ref, inverse_ref):
    rows, features = act_ref.shape

    def one_chunk(index, _):
        start = pl.multiple_of(index * chunk, chunk)
        part = pl.ds(start, chunk)
        squares = jnp.zeros((chunk, 128), jnp.float32)
        for left in range(0, features, tile):
            wide = act_ref[part, left : left + tile].astype(jnp.float32)
            wide = wide * wide
            for lane in range(0, tile, 128):
                squares = squares + wide[:, lane : lane + 128]
        mean = jnp.sum(squares, axis=1, keepdims=True) / features
        position = lax.broadcasted_iota(jnp.int32, (chunk, 1), 0) + lax.rem(start, seq_rows)
        keep = position < lengths_ref[lax.div(start, seq_rows)]
        inverse = jnp.where(keep, lax.rsqrt(mean + norm_epsilon), 0.0)
        inverse_ref[part, :] = jnp.broadcast_to(inverse, (chunk, 128))
        return 0

    lax.fori_loop(0, rows // chunk, one_chunk, 0)


def live_inverse(seq_rows, lengths, act):
    rows, features = act.shape
    return pl.pallas_call(
        functools.partial(inverse_kernel, seq_rows, math.gcd(seq_rows, 16), column_tile(features)),
        out_shape=jax.ShapeDtypeStruct((rows, 128), jnp.float32),
        in_specs=[pl.BlockSpec(memory_space=pltpu.SMEM), pl.BlockSpec(memory_space=pltpu.VMEM)],
        out_specs=pl.BlockSpec(memory_space=pltpu.VMEM),
        compiler_params=pltpu.CompilerParams(vmem_limit_bytes=grant(act)),
        cost_estimate=pl.CostEstimate(
            flops=2 * rows * features, bytes_accessed=2 * rows * features, transcendentals=rows
        ),
        name="live_inverse",
    )(lengths, act)


def relative(owner, place, count):
    if count & (count - 1) == 0:
        return owner ^ place
    return (place + count - owner) % count


def place_pieces(line, plane, groups, fold, pieces, held, back):
    width = back.shape[1] // (line * plane)
    me = lax.axis_index("dp")
    z, q = lax.div(me, plane), lax.rem(me, plane)
    for step in range(plane):
        owner_q = ahead(q, step, plane)
        for group_index, group in enumerate(groups):
            piece = pieces[step * len(groups) + group_index]
            for index, line_step in enumerate(group):
                held[behind(z, line_step, line) * plane + owner_q] = piece[index]
    steps = [line_step for group in groups for line_step in group]
    for owner_z in range(line):
        line_step = relative(owner_z, z, line)
        here = functools.reduce(jnp.logical_or, [line_step == step for step in steps])

        @pl.when(here)
        def _():
            for part in range(back.shape[0] // fold):
                rows = slice(part * fold, (part + 1) * fold)
                for block in range(owner_z * plane, (owner_z + 1) * plane):
                    back[rows, block * width : (block + 1) * width] = held[
                        block, :, part * width : (part + 1) * width
                    ]


def add_sums(lefts, part, project, inverse_ref, act_ref, gain_ref, gain_sum, pulls):
    inverse = inverse_ref[part, :]
    pull = pulls[part, :]
    for left in lefts:
        cols = slice(left, left + 128)
        both = act_ref[part, cols].astype(jnp.float32) * project(part, cols)
        pull = pull + both * gain_ref[:, cols]
        both = both * inverse
        folded = both[:8, :]
        for row in range(8, both.shape[0], 8):
            folded = folded + both[row : row + 8, :]
        gain_sum[:, cols] += folded
    pulls[part, :] = pull


def early_kernel(line, plane, groups, fold, chunk, inverse_ref, act_ref, gain_ref, *refs):
    pieces = refs[:-4]
    back, pulls, gain_sum, held = refs[-4:]
    back[...] = jnp.zeros_like(back)
    place_pieces(line, plane, groups, fold, pieces, held, back)
    gain_sum[...] = jnp.zeros_like(gain_sum)
    pulls[...] = jnp.zeros_like(pulls)

    def project(part, cols):
        return back[part, cols].astype(jnp.float32)

    def one_chunk(index, _):
        part = pl.ds(pl.multiple_of(index * chunk, chunk), chunk)
        add_sums(range(0, back.shape[1], 128), part, project, inverse_ref, act_ref, gain_ref, gain_sum, pulls)
        return 0

    lax.fori_loop(0, back.shape[0] // chunk, one_chunk, 0)


def placed_early(line, plane, groups, fold, inverse, act, gain, pieces):
    rows, features = act.shape
    vmem = pl.BlockSpec(memory_space=pltpu.VMEM)
    outs = [
        jax.ShapeDtypeStruct((rows, features), jnp.bfloat16),
        jax.ShapeDtypeStruct((rows, 128), jnp.float32),
        jax.ShapeDtypeStruct((8, features), jnp.float32),
    ]
    scratch = [pltpu.VMEM((line * plane,) + pieces[0].shape[1:], jnp.bfloat16)]
    return pl.pallas_call(
        functools.partial(early_kernel, line, plane, groups, fold, math.gcd(rows, 32)),
        out_shape=outs,
        in_specs=[vmem] * (3 + len(pieces)),
        out_specs=[vmem] * len(outs),
        scratch_shapes=scratch,
        compiler_params=pltpu.CompilerParams(
            vmem_limit_bytes=grant(inverse, act, gain, *pieces, *outs, *scratch)
        ),
        cost_estimate=pl.CostEstimate(
            flops=8 * rows * features, bytes_accessed=8 * rows * features, transcendentals=0
        ),
        name="placed_early",
    )(inverse, act, gain, *pieces)


def finish_kernel(
    line, plane, groups, fold, chunk, early_ref, early_pulls, early_gains, inverse_ref, act_ref, top_ref, gain_ref, *refs
):
    pieces = refs[:-9]
    passed_ref, local_ref, gain_out, held, back, gain_sum, pulls, passing, gain_blocks, copied = refs[-10:]
    rows, features = back.shape
    width = features // (line * plane)
    late_steps = [step for group in groups for step in group]
    late_z = behind(lax.div(lax.axis_index("dp"), plane), late_steps[0], line)
    back[...] = early_ref[...]
    place_pieces(line, plane, groups, fold, pieces, held, back)
    gain_sum[...] = early_gains[...]
    pulls[...] = early_pulls[...]

    def project(part, cols):
        return back[part, cols].astype(jnp.float32) - early_ref[part, cols].astype(jnp.float32)

    def add_late(part, lefts):
        add_sums(lefts, part, project, inverse_ref, act_ref, gain_ref, gain_sum, pulls)

    def out_copy(index):
        part = pl.ds(pl.multiple_of(index * chunk, chunk), chunk)
        return pltpu.make_async_copy(passing.at[part], passed_ref.at[part], copied.at[index])

    def one_chunk(index, _):
        part = pl.ds(pl.multiple_of(index * chunk, chunk), chunk)
        if len(late_steps) > 1:
            add_late(part, range(0, features, 128))
        else:
            for owner_z in range(line):
                first = owner_z * plane * width // 128 * 128
                after = (owner_z + 1) * plane * width

                @pl.when(late_z == owner_z)
                def _():
                    add_late(part, range(first, after, 128))

        inverse = inverse_ref[part, :]
        pull = jnp.sum(pulls[part, :], axis=1, keepdims=True) / features
        pull = jnp.broadcast_to(pull, inverse.shape) * inverse * inverse * inverse
        for left in range(0, features, 128):
            cols = slice(left, left + 128)
            scaled = back[part, cols].astype(jnp.float32) * gain_ref[:, cols]
            local = inverse * scaled - act_ref[part, cols].astype(jnp.float32) * pull
            local_ref[part, cols] = local
            passing[part, cols] = (top_ref[part, cols].astype(jnp.float32) + local).astype(jnp.bfloat16)
        out_copy(index).start()
        return 0

    lax.fori_loop(0, rows // chunk, one_chunk, 0)
    total = jnp.sum(gain_sum[...], axis=0, keepdims=True)
    for block in range(line * plane):
        gain_blocks[block] = total[:, block * width : (block + 1) * width]
    gain_copy = pltpu.make_async_copy(gain_blocks, gain_out, copied.at[rows // chunk])
    gain_copy.start()
    for index in range(rows // chunk):
        out_copy(index).wait()
    gain_copy.wait()


def finish(line, plane, groups, fold, early, inverse, act, top, gain, pieces):
    rows, features = act.shape
    blocks = line * plane
    vmem = pl.BlockSpec(memory_space=pltpu.VMEM)
    outs = [
        jax.ShapeDtypeStruct((rows, features), jnp.bfloat16),
        jax.ShapeDtypeStruct((rows, features), jnp.float32),
        jax.ShapeDtypeStruct((blocks, 1, features // blocks), jnp.float32),
    ]
    scratch = [
        pltpu.VMEM((blocks,) + pieces[0].shape[1:], jnp.bfloat16),
        pltpu.VMEM((rows, features), jnp.bfloat16),
        pltpu.VMEM((8, features), jnp.float32),
        pltpu.VMEM((rows, 128), jnp.float32),
        pltpu.VMEM((rows, features), jnp.bfloat16),
        pltpu.VMEM(outs[2].shape, jnp.float32),
    ]
    chunk = math.gcd(rows, 32)
    return pl.pallas_call(
        functools.partial(finish_kernel, line, plane, groups, fold, chunk),
        out_shape=outs,
        in_specs=[vmem] * (4 + len(early) + len(pieces)),
        out_specs=[pl.BlockSpec(memory_space=pl.ANY), vmem, pl.BlockSpec(memory_space=pl.ANY)],
        scratch_shapes=scratch + [pltpu.SemaphoreType.DMA((rows // chunk + 1,))],
        compiler_params=pltpu.CompilerParams(
            vmem_limit_bytes=grant(*early, act, top, *pieces, *outs, *scratch)
        ),
        cost_estimate=pl.CostEstimate(
            flops=16 * rows * features, bytes_accessed=12 * rows * features, transcendentals=0
        ),
        name="norm_backward",
    )(*early, inverse, act, top, gain, *pieces)


def hand_kernel(turn, chunk, incoming_ref, local_ref, result_ref, out_ref, loaded, staged, arrived, copied):
    rows, features = local_ref.shape
    parts = [pl.ds(start, chunk) for start in range(0, rows, chunk)]
    is_turn = lax.axis_index("section") == turn

    def through(source, staging, work):
        loads = [
            pltpu.make_async_copy(source.at[part], loaded.at[part], arrived.at[index])
            for index, part in enumerate(parts)
        ]
        stores = [
            pltpu.make_async_copy(staging.at[part], out_ref.at[part], copied.at[index])
            for index, part in enumerate(parts)
        ]
        for load in loads:
            load.start()
        for part, load, store in zip(parts, loads, stores):
            load.wait()
            work(part)
            store.start()
        for store in stores:
            store.wait()

    def add_local(part):
        for left in range(0, features, 128):
            cols = slice(left, left + 128)
            staged[part, cols] = (loaded[part, cols].astype(jnp.float32) + local_ref[part, cols]).astype(jnp.bfloat16)

    @pl.when(is_turn)
    def _():
        through(incoming_ref, staged, add_local)

    @pl.when(jnp.logical_not(is_turn))
    def _():
        through(result_ref, loaded, lambda part: None)


def hand_on(turn, chunk, incoming, local, result):
    rows, features = local.shape
    vmem = pl.BlockSpec(memory_space=pltpu.VMEM)
    hbm = pl.BlockSpec(memory_space=pl.ANY)
    return pl.pallas_call(
        functools.partial(hand_kernel, turn, chunk),
        out_shape=jax.ShapeDtypeStruct((rows, features), jnp.bfloat16),
        in_specs=[hbm, vmem, hbm],
        out_specs=hbm,
        scratch_shapes=[
            pltpu.VMEM((rows, features), jnp.bfloat16),
            pltpu.VMEM((rows, features), jnp.bfloat16),
            pltpu.SemaphoreType.DMA((rows // chunk,)),
            pltpu.SemaphoreType.DMA((rows // chunk,)),
        ],
        compiler_params=pltpu.CompilerParams(vmem_limit_bytes=grant(incoming, local, result)),
        cost_estimate=pl.CostEstimate(flops=0, bytes_accessed=0, transcendentals=0),
        name="hand_on",
    )(incoming, local, result)


def sum_kernel(scale, parts_ref, out_ref):
    total = parts_ref[0]
    for index in range(1, parts_ref.shape[0]):
        total = total + parts_ref[index]
    out_ref[...] = total * scale


def sum_scaled(parts, scale):
    vmem = pl.BlockSpec(memory_space=pltpu.VMEM)
    return pl.pallas_call(
        functools.partial(sum_kernel, scale),
        out_shape=jax.ShapeDtypeStruct(parts.shape[1:], jnp.float32),
        in_specs=[vmem],
        out_specs=vmem,
        compiler_params=pltpu.CompilerParams(vmem_limit_bytes=mebibyte),
        cost_estimate=pl.CostEstimate(flops=parts.size, bytes_accessed=4 * parts.size, transcendentals=0),
        name="sum_scaled",
    )(parts)


def sent_back(group_products, line, plane):
    return [group_products[0]] + [
        along_plane(group_products[step], step, line, plane, back=True) for step in range(1, plane)
    ]


def gathered_products(fold, tokens, shard, line, plane):
    held = {0: shard}
    groups = [(0,)]
    first = products(fold, tokens, [shard])
    if line & (line - 1):
        for step in range(1, line):
            held[step] = along_line(shard, step, line, plane)
        groups.append(tuple(range(1, (line + 1) // 2)))
    elif line > 1:
        distance = line // 2
        while distance:
            held[distance] = along_line(shard, distance, line, plane)
            distance //= 2
        groups.append(tuple(sorted(step for step in held if step)))
        far = line // 2
        held[far], own = lax.optimization_barrier((held[far], first[0]))
        first = [own] + list(first[1:])
        distance = line // 4
        while distance:
            for step in sorted(held):
                if step and step % (2 * distance) == 0 and step + distance not in held:
                    held[step + distance] = along_line(held[step], distance, line, plane)
            distance //= 2
    groups.append(tuple(step for step in range(line) if not any(step in group for group in groups)))
    groups = [group for group in groups if group]
    pieces = [sent_back(first, line, plane)]
    for group in groups[1:]:
        shards = [held[step] for step in group]
        made = list(products(fold, tokens, shards))
        if len(pieces) == 1:
            made[-1], pieces[0] = lax.optimization_barrier((made[-1], pieces[0]))
        pieces.append(sent_back(made, line, plane))
    return groups, pieces


def on_device(activations, key_grads, top_grad, norm_gains, w_key, lengths):
    micro_count, seq_rows, features = activations.shape[2:]
    rows = micro_count * seq_rows
    fold = math.gcd(rows, 16)
    replicas = lax.axis_size("dp")
    sections = lax.axis_size("section")
    plane = plane_size(replicas)
    line = replicas // plane
    grad_scale = 1.0 / math.sqrt(replicas * rows)
    act = activations.reshape(rows, features)

    key_rows = key_grads.reshape(rows, key_grads.shape[-1])
    inverse, own_rows = lax.optimization_barrier((live_inverse(seq_rows, lengths[0], act), key_rows))
    tokens = [own_rows] + [along_plane(key_rows, step, line, plane) for step in range(1, plane)]
    groups, pieces = gathered_products(fold, tokens, w_key[0], line, plane)
    split = max(1, len(groups) - 1)
    early, late = ([part[step] for step in range(plane) for part in some] for some in (pieces[:split], pieces[split:]))
    early = placed_early(line, plane, groups[:split], fold, inverse, act, norm_gains, early)
    top = top_grad.reshape(rows, features)
    passed, local, gain_blocks = finish(
        line, plane, groups[split:], fold, early, inverse, act, top, norm_gains, late
    )

    result = passed
    for turn in range(sections - 2, -1, -1):
        incoming = lax.ppermute(result, "section", [(turn + 1, turn)])
        result = hand_on(turn, seq_rows, incoming, local, result)

    gain_parts = lax.all_to_all(gain_blocks, "dp", split_axis=0, concat_axis=0, tiled=True)
    gain_parts, result = lax.optimization_barrier((gain_parts, result))
    grad_shard = sum_scaled(gain_parts, grad_scale)
    return (result.reshape(activations.shape), grad_shard)


def solution(mesh):
    placed = (
        P("section", "dp", None, None, None),
        P("section", "dp", None, None, None),
        P("dp", None, None, None),
        P("section", None),
        P("section", "dp", None),
        P("dp", None),
    )
    return jax.shard_map(
        on_device,
        mesh=mesh,
        in_specs=placed,
        out_specs=(P("section", "dp", None, None, None), P("section", "dp")),
        check_vma=False,
    )
```

```python
import functools
import math

import jax
import jax.numpy as jnp
from jax import lax
from jax.experimental import pallas as pl
from jax.experimental.pallas import tpu as pltpu
from jax.sharding import PartitionSpec as P

norm_epsilon = 1e-05
mebibyte = 1024 * 1024
product_cost = 10


def grant(*arrays):
    total = 4 * mebibyte
    for array in arrays:
        lanes = -(-array.shape[-1] // 128) * 128
        total += math.prod(array.shape[:-1]) * lanes * jnp.dtype(array.dtype).itemsize
    return -(-total // mebibyte) * mebibyte


def plane_size(replicas):
    size = 1
    while (2 * size) ** 2 <= replicas and replicas % (2 * size) == 0:
        size *= 2
    return size


def ahead(place, step, count):
    if count & (count - 1) == 0:
        return place ^ step
    return (place + step) % count


def behind(place, step, count):
    if count & (count - 1) == 0:
        return place ^ step
    return (place + count - step) % count


def along_line(value, step, line, plane):
    pairs = [
        (z * plane + q, ahead(z, step, line) * plane + q)
        for z in range(line)
        for q in range(plane)
    ]
    return lax.ppermute(value, "dp", pairs)


def along_plane(value, step, line, plane, back=False):
    partner = behind if back else ahead
    pairs = [
        (z * plane + q, z * plane + partner(q, step, plane))
        for z in range(line)
        for q in range(plane)
    ]
    return lax.ppermute(value, "dp", pairs)


def product_kernel(token_count, weight_count, fold, *refs):
    tokens = refs[:token_count]
    weights = refs[token_count : token_count + weight_count]
    outs = refs[token_count + weight_count :]
    for token_ref, out_ref in zip(tokens, outs):
        for index, weight_ref in enumerate(weights):
            product = lax.dot_general(
                token_ref[...],
                weight_ref[...],
                (((1,), (1,)), ((), ())),
                preferred_element_type=jnp.float32,
            ).astype(out_ref.dtype)
            width = product.shape[1]
            for part in range(product.shape[0] // fold):
                out_ref[index, :, part * width : (part + 1) * width] = product[part * fold : (part + 1) * fold, :]


def products(fold, tokens, weights, cost):
    rows, depth = tokens[0].shape
    width = weights[0].shape[0]
    count = len(weights)
    folded = (count, fold, rows // fold * width)
    outs = [jax.ShapeDtypeStruct(folded, jnp.bfloat16) for _ in tokens]
    return pl.pallas_call(
        functools.partial(product_kernel, len(tokens), count, fold),
        out_shape=outs,
        in_specs=[pl.BlockSpec(memory_space=pltpu.VMEM)] * (len(tokens) + count),
        out_specs=[pl.BlockSpec(memory_space=pltpu.VMEM)] * len(tokens),
        compiler_params=pltpu.CompilerParams(vmem_limit_bytes=grant(*tokens, *weights, *outs)),
        cost_estimate=pl.CostEstimate(
            flops=cost * 2 * rows * depth * width * count * len(tokens),
            bytes_accessed=2 * (rows * depth * len(tokens) + depth * width * count + rows * width * count * len(tokens)),
            transcendentals=0,
        ),
        name="token_products",
    )(*tokens, *weights)


def column_tile(features, most=512):
    tile = 128
    for width in range(128, most + 1, 128):
        if features % width == 0:
            tile = width
    return tile


def inverse_kernel(seq_rows, chunk, tile, lengths_ref, act_ref, inverse_ref):
    rows, features = act_ref.shape

    def one_chunk(index, _):
        start = pl.multiple_of(index * chunk, chunk)
        part = pl.ds(start, chunk)
        squares = jnp.zeros((chunk, 128), jnp.float32)
        for left in range(0, features, tile):
            wide = act_ref[part, left : left + tile].astype(jnp.float32)
            wide = wide * wide
            for lane in range(0, tile, 128):
                squares = squares + wide[:, lane : lane + 128]
        mean = jnp.sum(squares, axis=1, keepdims=True) / features
        position = lax.broadcasted_iota(jnp.int32, (chunk, 1), 0) + lax.rem(start, seq_rows)
        keep = position < lengths_ref[lax.div(start, seq_rows)]
        inverse = jnp.where(keep, lax.rsqrt(mean + norm_epsilon), 0.0)
        inverse_ref[part, :] = jnp.broadcast_to(inverse, (chunk, 128))
        return 0

    lax.fori_loop(0, rows // chunk, one_chunk, 0)


def live_inverse(seq_rows, lengths, act):
    rows, features = act.shape
    return pl.pallas_call(
        functools.partial(inverse_kernel, seq_rows, math.gcd(seq_rows, 16), column_tile(features)),
        out_shape=jax.ShapeDtypeStruct((rows, 128), jnp.float32),
        in_specs=[pl.BlockSpec(memory_space=pltpu.SMEM), pl.BlockSpec(memory_space=pltpu.VMEM)],
        out_specs=pl.BlockSpec(memory_space=pltpu.VMEM),
        compiler_params=pltpu.CompilerParams(vmem_limit_bytes=grant(act)),
        cost_estimate=pl.CostEstimate(
            flops=2 * rows * features, bytes_accessed=2 * rows * features, transcendentals=rows
        ),
        name="live_inverse",
    )(lengths, act)


def relative(owner, place, count):
    if count & (count - 1) == 0:
        return owner ^ place
    return (place + count - owner) % count


def place_pieces(line, plane, groups, fold, pieces, held, back):
    width = back.shape[1] // (line * plane)
    me = lax.axis_index("dp")
    z, q = lax.div(me, plane), lax.rem(me, plane)
    for step in range(plane):
        owner_q = ahead(q, step, plane)
        for group_index, group in enumerate(groups):
            piece = pieces[step * len(groups) + group_index]
            for index, line_step in enumerate(group):
                held[behind(z, line_step, line) * plane + owner_q] = piece[index]
    steps = [line_step for group in groups for line_step in group]
    for owner_z in range(line):
        line_step = relative(owner_z, z, line)
        here = functools.reduce(jnp.logical_or, [line_step == step for step in steps])

        @pl.when(here)
        def _():
            for part in range(back.shape[0] // fold):
                rows = slice(part * fold, (part + 1) * fold)
                for block in range(owner_z * plane, (owner_z + 1) * plane):
                    back[rows, block * width : (block + 1) * width] = held[
                        block, :, part * width : (part + 1) * width
                    ]


def add_sums(lefts, part, project, inverse_ref, act_ref, gain_ref, gain_sum, pulls):
    inverse = inverse_ref[part, :]
    pull = pulls[part, :]
    for left in lefts:
        cols = slice(left, left + 128)
        both = act_ref[part, cols].astype(jnp.float32) * project(part, cols)
        pull = pull + both * gain_ref[:, cols]
        both = both * inverse
        folded = both[:8, :]
        for row in range(8, both.shape[0], 8):
            folded = folded + both[row : row + 8, :]
        gain_sum[:, cols] += folded
    pulls[part, :] = pull


def early_kernel(line, plane, groups, fold, chunk, inverse_ref, act_ref, gain_ref, *refs):
    pieces = refs[:-4]
    back, pulls, gain_sum, held = refs[-4:]
    back[...] = jnp.zeros_like(back)
    place_pieces(line, plane, groups, fold, pieces, held, back)
    gain_sum[...] = jnp.zeros_like(gain_sum)
    pulls[...] = jnp.zeros_like(pulls)

    def project(part, cols):
        return back[part, cols].astype(jnp.float32)

    def one_chunk(index, _):
        part = pl.ds(pl.multiple_of(index * chunk, chunk), chunk)
        add_sums(range(0, back.shape[1], 128), part, project, inverse_ref, act_ref, gain_ref, gain_sum, pulls)
        return 0

    lax.fori_loop(0, back.shape[0] // chunk, one_chunk, 0)


def placed_early(line, plane, groups, fold, inverse, act, gain, pieces):
    rows, features = act.shape
    vmem = pl.BlockSpec(memory_space=pltpu.VMEM)
    outs = [
        jax.ShapeDtypeStruct((rows, features), jnp.bfloat16),
        jax.ShapeDtypeStruct((rows, 128), jnp.float32),
        jax.ShapeDtypeStruct((8, features), jnp.float32),
    ]
    scratch = [pltpu.VMEM((line * plane,) + pieces[0].shape[1:], jnp.bfloat16)]
    return pl.pallas_call(
        functools.partial(early_kernel, line, plane, groups, fold, math.gcd(rows, 32)),
        out_shape=outs,
        in_specs=[vmem] * (3 + len(pieces)),
        out_specs=[vmem] * len(outs),
        scratch_shapes=scratch,
        compiler_params=pltpu.CompilerParams(
            vmem_limit_bytes=grant(inverse, act, gain, *pieces, *outs, *scratch)
        ),
        cost_estimate=pl.CostEstimate(
            flops=8 * rows * features, bytes_accessed=8 * rows * features, transcendentals=0
        ),
        name="placed_early",
    )(inverse, act, gain, *pieces)


def finish_kernel(
    line, plane, groups, fold, chunk, early_ref, early_pulls, early_gains, inverse_ref, act_ref, top_ref, gain_ref, *refs
):
    pieces = refs[:-10]
    passed_ref, local_ref, gain_out, held, back, gain_sum, pulls, passing, gain_blocks, copied = refs[-10:]
    rows, features = back.shape
    width = features // (line * plane)
    late_steps = [step for group in groups for step in group]
    late_z = behind(lax.div(lax.axis_index("dp"), plane), late_steps[0], line)
    back[...] = early_ref[...]
    place_pieces(line, plane, groups, fold, pieces, held, back)
    gain_sum[...] = early_gains[...]
    pulls[...] = early_pulls[...]

    def project(part, cols):
        return back[part, cols].astype(jnp.float32) - early_ref[part, cols].astype(jnp.float32)

    def add_late(part, lefts):
        add_sums(lefts, part, project, inverse_ref, act_ref, gain_ref, gain_sum, pulls)

    def out_copy(index):
        part = pl.ds(pl.multiple_of(index * chunk, chunk), chunk)
        return pltpu.make_async_copy(passing.at[part], passed_ref.at[part], copied.at[index])

    def one_chunk(index, _):
        part = pl.ds(pl.multiple_of(index * chunk, chunk), chunk)
        if len(late_steps) > 1:
            add_late(part, range(0, features, 128))
        else:
            for owner_z in range(line):
                first = owner_z * plane * width // 128 * 128
                after = (owner_z + 1) * plane * width

                @pl.when(late_z == owner_z)
                def _():
                    add_late(part, range(first, after, 128))

        inverse = inverse_ref[part, :]
        pull = jnp.sum(pulls[part, :], axis=1, keepdims=True) / features
        pull = jnp.broadcast_to(pull, inverse.shape) * inverse * inverse * inverse
        for left in range(0, features, 128):
            cols = slice(left, left + 128)
            scaled = back[part, cols].astype(jnp.float32) * gain_ref[:, cols]
            local = inverse * scaled - act_ref[part, cols].astype(jnp.float32) * pull
            local_ref[part, cols] = local
            passing[part, cols] = (top_ref[part, cols].astype(jnp.float32) + local).astype(jnp.bfloat16)
        out_copy(index).start()
        return 0

    lax.fori_loop(0, rows // chunk, one_chunk, 0)
    total = jnp.sum(gain_sum[...], axis=0, keepdims=True)
    for block in range(line * plane):
        gain_blocks[block] = total[:, block * width : (block + 1) * width]
    gain_copy = pltpu.make_async_copy(gain_blocks, gain_out, copied.at[rows // chunk])
    gain_copy.start()
    for index in range(rows // chunk):
        out_copy(index).wait()
    gain_copy.wait()


def finish(line, plane, groups, fold, early, inverse, act, top, gain, pieces):
    rows, features = act.shape
    blocks = line * plane
    vmem = pl.BlockSpec(memory_space=pltpu.VMEM)
    outs = [
        jax.ShapeDtypeStruct((rows, features), jnp.bfloat16),
        jax.ShapeDtypeStruct((rows, features), jnp.float32),
        jax.ShapeDtypeStruct((blocks, 1, features // blocks), jnp.float32),
    ]
    scratch = [
        pltpu.VMEM((blocks,) + pieces[0].shape[1:], jnp.bfloat16),
        pltpu.VMEM((rows, features), jnp.bfloat16),
        pltpu.VMEM((8, features), jnp.float32),
        pltpu.VMEM((rows, 128), jnp.float32),
        pltpu.VMEM((rows, features), jnp.bfloat16),
        pltpu.VMEM(outs[2].shape, jnp.float32),
    ]
    chunk = math.gcd(rows, 32)
    return pl.pallas_call(
        functools.partial(finish_kernel, line, plane, groups, fold, chunk),
        out_shape=outs,
        in_specs=[vmem] * (4 + len(early) + len(pieces)),
        out_specs=[pl.BlockSpec(memory_space=pl.ANY), vmem, pl.BlockSpec(memory_space=pl.ANY)],
        scratch_shapes=scratch + [pltpu.SemaphoreType.DMA((rows // chunk + 1,))],
        compiler_params=pltpu.CompilerParams(
            vmem_limit_bytes=grant(*early, act, top, *pieces, *outs, *scratch)
        ),
        cost_estimate=pl.CostEstimate(
            flops=16 * rows * features, bytes_accessed=12 * rows * features, transcendentals=0
        ),
        name="norm_backward",
    )(*early, inverse, act, top, gain, *pieces)


def hand_kernel(turn, chunk, incoming_ref, local_ref, result_ref, out_ref, loaded, staged, arrived, copied):
    rows, features = local_ref.shape
    parts = [pl.ds(start, chunk) for start in range(0, rows, chunk)]
    is_turn = lax.axis_index("section") == turn

    def through(source, staging, work):
        loads = [
            pltpu.make_async_copy(source.at[part], loaded.at[part], arrived.at[index])
            for index, part in enumerate(parts)
        ]
        stores = [
            pltpu.make_async_copy(staging.at[part], out_ref.at[part], copied.at[index])
            for index, part in enumerate(parts)
        ]
        for load in loads:
            load.start()
        for part, load, store in zip(parts, loads, stores):
            load.wait()
            work(part)
            store.start()
        for store in stores:
            store.wait()

    def add_local(part):
        for left in range(0, features, 128):
            cols = slice(left, left + 128)
            staged[part, cols] = (loaded[part, cols].astype(jnp.float32) + local_ref[part, cols]).astype(jnp.bfloat16)

    @pl.when(is_turn)
    def _():
        through(incoming_ref, staged, add_local)

    @pl.when(jnp.logical_not(is_turn))
    def _():
        through(result_ref, loaded, lambda part: None)


def hand_on(turn, chunk, incoming, local, result):
    rows, features = local.shape
    vmem = pl.BlockSpec(memory_space=pltpu.VMEM)
    hbm = pl.BlockSpec(memory_space=pl.ANY)
    return pl.pallas_call(
        functools.partial(hand_kernel, turn, chunk),
        out_shape=jax.ShapeDtypeStruct((rows, features), jnp.bfloat16),
        in_specs=[hbm, vmem, hbm],
        out_specs=hbm,
        scratch_shapes=[
            pltpu.VMEM((rows, features), jnp.bfloat16),
            pltpu.VMEM((rows, features), jnp.bfloat16),
            pltpu.SemaphoreType.DMA((rows // chunk,)),
            pltpu.SemaphoreType.DMA((rows // chunk,)),
        ],
        compiler_params=pltpu.CompilerParams(vmem_limit_bytes=grant(incoming, local, result)),
        cost_estimate=pl.CostEstimate(flops=0, bytes_accessed=0, transcendentals=0),
        name="hand_on",
    )(incoming, local, result)


def sum_kernel(scale, parts_ref, out_ref):
    total = parts_ref[0]
    for index in range(1, parts_ref.shape[0]):
        total = total + parts_ref[index]
    out_ref[...] = total * scale


def sum_scaled(parts, scale):
    vmem = pl.BlockSpec(memory_space=pltpu.VMEM)
    return pl.pallas_call(
        functools.partial(sum_kernel, scale),
        out_shape=jax.ShapeDtypeStruct(parts.shape[1:], jnp.float32),
        in_specs=[vmem],
        out_specs=vmem,
        compiler_params=pltpu.CompilerParams(vmem_limit_bytes=mebibyte),
        cost_estimate=pl.CostEstimate(flops=parts.size, bytes_accessed=4 * parts.size, transcendentals=0),
        name="sum_scaled",
    )(parts)


def sent_back(group_products, line, plane):
    return [group_products[0]] + [
        along_plane(group_products[step], step, line, plane, back=True) for step in range(1, plane)
    ]


def gathered_products(fold, tokens, shard, line, plane):
    held = {0: shard}
    groups = [(0,)]
    first = products(fold, tokens, [shard], 1)
    if line & (line - 1):
        for step in range(1, line):
            held[step] = along_line(shard, step, line, plane)
        groups.append(tuple(range(1, (line + 1) // 2)))
    elif line > 1:
        distance = line // 2
        while distance:
            held[distance] = along_line(shard, distance, line, plane)
            distance //= 2
        groups.append(tuple(sorted(step for step in held if step)))
        far = line // 2
        held[far], own = lax.optimization_barrier((held[far], first[0]))
        first = [own] + list(first[1:])
        distance = line // 4
        while distance:
            for step in sorted(held):
                if step and step % (2 * distance) == 0 and step + distance not in held:
                    held[step + distance] = along_line(held[step], distance, line, plane)
            distance //= 2
    groups.append(tuple(step for step in range(line) if not any(step in group for group in groups)))
    groups = [group for group in groups if group]
    pieces = [sent_back(first, line, plane)]
    for group in groups[1:]:
        shards = [held[step] for step in group]
        made = list(products(fold, tokens, shards, product_cost))
        if len(pieces) == 1:
            made[-1], pieces[0] = lax.optimization_barrier((made[-1], pieces[0]))
        pieces.append(sent_back(made, line, plane))
    return groups, pieces


def on_device(activations, key_grads, top_grad, norm_gains, w_key, lengths):
    micro_count, seq_rows, features = activations.shape[2:]
    rows = micro_count * seq_rows
    fold = math.gcd(rows, 16)
    replicas = lax.axis_size("dp")
    sections = lax.axis_size("section")
    plane = plane_size(replicas)
    line = replicas // plane
    grad_scale = 1.0 / math.sqrt(replicas * rows)
    act = activations.reshape(rows, features)

    key_rows = key_grads.reshape(rows, key_grads.shape[-1])
    inverse, own_rows = lax.optimization_barrier((live_inverse(seq_rows, lengths[0], act), key_rows))
    tokens = [own_rows] + [along_plane(key_rows, step, line, plane) for step in range(1, plane)]
    groups, pieces = gathered_products(fold, tokens, w_key[0], line, plane)
    split = max(1, len(groups) - 1)
    early, late = ([part[step] for step in range(plane) for part in some] for some in (pieces[:split], pieces[split:]))
    early = placed_early(line, plane, groups[:split], fold, inverse, act, norm_gains, early)
    top = top_grad.reshape(rows, features)
    passed, local, gain_blocks = finish(
        line, plane, groups[split:], fold, early, inverse, act, top, norm_gains, late
    )

    result = passed
    for turn in range(sections - 2, -1, -1):
        incoming = lax.ppermute(result, "section", [(turn + 1, turn)])
        result = hand_on(turn, seq_rows, incoming, local, result)

    gain_parts = lax.all_to_all(gain_blocks, "dp", split_axis=0, concat_axis=0, tiled=True)
    gain_parts, result = lax.optimization_barrier((gain_parts, result))
    grad_shard = sum_scaled(gain_parts, grad_scale)
    return (result.reshape(activations.shape), grad_shard)


def solution(mesh):
    placed = (
        P("section", "dp", None, None, None),
        P("section", "dp", None, None, None),
        P("dp", None, None, None),
        P("section", None),
        P("section", "dp", None),
        P("dp", None),
    )
    return jax.shard_map(
        on_device,
        mesh=mesh,
        in_specs=placed,
        out_specs=(P("section", "dp", None, None, None), P("section", "dp")),
        check_vma=False,
    )
```

```python
import functools
import math

import jax
import jax.numpy as jnp
from jax import lax
from jax.experimental import pallas as pl
from jax.experimental.pallas import tpu as pltpu
from jax.sharding import PartitionSpec as P

norm_epsilon = 1e-05
mebibyte = 1024 * 1024
product_cost = 10


def grant(*arrays):
    total = 4 * mebibyte
    for array in arrays:
        lanes = -(-array.shape[-1] // 128) * 128
        total += math.prod(array.shape[:-1]) * lanes * jnp.dtype(array.dtype).itemsize
    return -(-total // mebibyte) * mebibyte


def plane_size(replicas):
    size = 1
    while (2 * size) ** 2 <= replicas and replicas % (2 * size) == 0:
        size *= 2
    return size


def ahead(place, step, count):
    if count & (count - 1) == 0:
        return place ^ step
    return (place + step) % count


def behind(place, step, count):
    if count & (count - 1) == 0:
        return place ^ step
    return (place + count - step) % count


def along_line(value, step, line, plane):
    pairs = [
        (z * plane + q, ahead(z, step, line) * plane + q)
        for z in range(line)
        for q in range(plane)
    ]
    return lax.ppermute(value, "dp", pairs)


def along_plane(value, step, line, plane, back=False):
    partner = behind if back else ahead
    pairs = [
        (z * plane + q, z * plane + partner(q, step, plane))
        for z in range(line)
        for q in range(plane)
    ]
    return lax.ppermute(value, "dp", pairs)


def product_kernel(token_count, weight_count, fold, *refs):
    tokens = refs[:token_count]
    weights = refs[token_count : token_count + weight_count]
    outs = refs[token_count + weight_count :]
    for token_ref, out_ref in zip(tokens, outs):
        for index, weight_ref in enumerate(weights):
            product = lax.dot_general(
                token_ref[...],
                weight_ref[...],
                (((1,), (1,)), ((), ())),
                preferred_element_type=jnp.float32,
            ).astype(out_ref.dtype)
            width = product.shape[1]
            for part in range(product.shape[0] // fold):
                out_ref[index, :, part * width : (part + 1) * width] = product[part * fold : (part + 1) * fold, :]


def products(fold, tokens, weights, cost):
    rows, depth = tokens[0].shape
    width = weights[0].shape[0]
    count = len(weights)
    folded = (count, fold, rows // fold * width)
    outs = [jax.ShapeDtypeStruct(folded, jnp.bfloat16) for _ in tokens]
    return pl.pallas_call(
        functools.partial(product_kernel, len(tokens), count, fold),
        out_shape=outs,
        in_specs=[pl.BlockSpec(memory_space=pltpu.VMEM)] * (len(tokens) + count),
        out_specs=[pl.BlockSpec(memory_space=pltpu.VMEM)] * len(tokens),
        compiler_params=pltpu.CompilerParams(vmem_limit_bytes=grant(*tokens, *weights, *outs)),
        cost_estimate=pl.CostEstimate(
            flops=cost * 2 * rows * depth * width * count * len(tokens),
            bytes_accessed=2 * (rows * depth * len(tokens) + depth * width * count + rows * width * count * len(tokens)),
            transcendentals=0,
        ),
        name="token_products",
    )(*tokens, *weights)


def column_tile(features, most=512):
    tile = 128
    for width in range(128, most + 1, 128):
        if features % width == 0:
            tile = width
    return tile


def inverse_kernel(seq_rows, chunk, tile, lengths_ref, act_ref, inverse_ref):
    rows, features = act_ref.shape

    def one_chunk(index, _):
        start = pl.multiple_of(index * chunk, chunk)
        part = pl.ds(start, chunk)
        squares = jnp.zeros((chunk, 128), jnp.float32)
        for left in range(0, features, tile):
            wide = act_ref[part, left : left + tile].astype(jnp.float32)
            wide = wide * wide
            for lane in range(0, tile, 128):
                squares = squares + wide[:, lane : lane + 128]
        mean = jnp.sum(squares, axis=1, keepdims=True) / features
        position = lax.broadcasted_iota(jnp.int32, (chunk, 1), 0) + lax.rem(start, seq_rows)
        keep = position < lengths_ref[lax.div(start, seq_rows)]
        inverse = jnp.where(keep, lax.rsqrt(mean + norm_epsilon), 0.0)
        inverse_ref[part, :] = jnp.broadcast_to(inverse, (chunk, 128))
        return 0

    lax.fori_loop(0, rows // chunk, one_chunk, 0)


def live_inverse(seq_rows, lengths, act):
    rows, features = act.shape
    return pl.pallas_call(
        functools.partial(inverse_kernel, seq_rows, math.gcd(seq_rows, 16), column_tile(features)),
        out_shape=jax.ShapeDtypeStruct((rows, 128), jnp.float32),
        in_specs=[pl.BlockSpec(memory_space=pltpu.SMEM), pl.BlockSpec(memory_space=pltpu.VMEM)],
        out_specs=pl.BlockSpec(memory_space=pltpu.VMEM),
        compiler_params=pltpu.CompilerParams(vmem_limit_bytes=grant(act)),
        cost_estimate=pl.CostEstimate(
            flops=2 * rows * features, bytes_accessed=2 * rows * features, transcendentals=rows
        ),
        name="live_inverse",
    )(lengths, act)


def relative(owner, place, count):
    if count & (count - 1) == 0:
        return owner ^ place
    return (place + count - owner) % count


def place_pieces(line, plane, groups, fold, pieces, held, back):
    width = back.shape[1] // (line * plane)
    me = lax.axis_index("dp")
    z, q = lax.div(me, plane), lax.rem(me, plane)
    for step in range(plane):
        owner_q = ahead(q, step, plane)
        for group_index, group in enumerate(groups):
            piece = pieces[step * len(groups) + group_index]
            for index, line_step in enumerate(group):
                held[behind(z, line_step, line) * plane + owner_q] = piece[index]
    steps = [line_step for group in groups for line_step in group]
    for owner_z in range(line):
        line_step = relative(owner_z, z, line)
        here = functools.reduce(jnp.logical_or, [line_step == step for step in steps])

        @pl.when(here)
        def _():
            for part in range(back.shape[0] // fold):
                rows = slice(part * fold, (part + 1) * fold)
                for block in range(owner_z * plane, (owner_z + 1) * plane):
                    back[rows, block * width : (block + 1) * width] = held[
                        block, :, part * width : (part + 1) * width
                    ]


def add_sums(lefts, part, project, inverse_ref, act_ref, gain_ref, gain_sum, pulls):
    inverse = inverse_ref[part, :]
    pull = pulls[part, :]
    for left in lefts:
        cols = slice(left, left + 128)
        both = act_ref[part, cols].astype(jnp.float32) * project(part, cols)
        pull = pull + both * gain_ref[:, cols]
        both = both * inverse
        folded = both[:8, :]
        for row in range(8, both.shape[0], 8):
            folded = folded + both[row : row + 8, :]
        gain_sum[:, cols] += folded
    pulls[part, :] = pull


def early_kernel(line, plane, groups, fold, chunk, inverse_ref, act_ref, gain_ref, *refs):
    pieces = refs[:-4]
    back, pulls, gain_sum, held = refs[-4:]
    back[...] = jnp.zeros_like(back)
    place_pieces(line, plane, groups, fold, pieces, held, back)
    gain_sum[...] = jnp.zeros_like(gain_sum)
    pulls[...] = jnp.zeros_like(pulls)

    def project(part, cols):
        return back[part, cols].astype(jnp.float32)

    def one_chunk(index, _):
        part = pl.ds(pl.multiple_of(index * chunk, chunk), chunk)
        add_sums(range(0, back.shape[1], 128), part, project, inverse_ref, act_ref, gain_ref, gain_sum, pulls)
        return 0

    lax.fori_loop(0, back.shape[0] // chunk, one_chunk, 0)


def placed_early(line, plane, groups, fold, inverse, act, gain, pieces):
    rows, features = act.shape
    vmem = pl.BlockSpec(memory_space=pltpu.VMEM)
    outs = [
        jax.ShapeDtypeStruct((rows, features), jnp.bfloat16),
        jax.ShapeDtypeStruct((rows, 128), jnp.float32),
        jax.ShapeDtypeStruct((8, features), jnp.float32),
    ]
    scratch = [pltpu.VMEM((line * plane,) + pieces[0].shape[1:], jnp.bfloat16)]
    return pl.pallas_call(
        functools.partial(early_kernel, line, plane, groups, fold, math.gcd(rows, 32)),
        out_shape=outs,
        in_specs=[vmem] * (3 + len(pieces)),
        out_specs=[vmem] * len(outs),
        scratch_shapes=scratch,
        compiler_params=pltpu.CompilerParams(
            vmem_limit_bytes=grant(inverse, act, gain, *pieces, *outs, *scratch)
        ),
        cost_estimate=pl.CostEstimate(
            flops=8 * rows * features, bytes_accessed=8 * rows * features, transcendentals=0
        ),
        name="placed_early",
    )(inverse, act, gain, *pieces)


def finish_kernel(
    line, plane, groups, fold, chunk, early_ref, early_pulls, early_gains, inverse_ref, act_ref, top_ref, gain_ref, *refs
):
    pieces = refs[:-10]
    passed_ref, local_ref, gain_out, held, back, gain_sum, pulls, passing, gain_blocks, copied = refs[-10:]
    rows, features = back.shape
    width = features // (line * plane)
    late_steps = [step for group in groups for step in group]
    late_z = behind(lax.div(lax.axis_index("dp"), plane), late_steps[0], line)
    back[...] = early_ref[...]
    place_pieces(line, plane, groups, fold, pieces, held, back)
    gain_sum[...] = early_gains[...]
    pulls[...] = early_pulls[...]

    def project(part, cols):
        return back[part, cols].astype(jnp.float32) - early_ref[part, cols].astype(jnp.float32)

    def add_late(part, lefts):
        add_sums(lefts, part, project, inverse_ref, act_ref, gain_ref, gain_sum, pulls)

    def out_copy(index):
        part = pl.ds(pl.multiple_of(index * chunk, chunk), chunk)
        return pltpu.make_async_copy(passing.at[part], passed_ref.at[part], copied.at[index])

    def one_chunk(index, _):
        part = pl.ds(pl.multiple_of(index * chunk, chunk), chunk)
        if len(late_steps) > 1:
            add_late(part, range(0, features, 128))
        else:
            for owner_z in range(line):
                first = owner_z * plane * width // 128 * 128
                after = (owner_z + 1) * plane * width

                @pl.when(late_z == owner_z)
                def _():
                    add_late(part, range(first, after, 128))

        inverse = inverse_ref[part, :]
        pull = jnp.sum(pulls[part, :], axis=1, keepdims=True) / features
        pull = jnp.broadcast_to(pull, inverse.shape) * inverse * inverse * inverse
        for left in range(0, features, 128):
            cols = slice(left, left + 128)
            scaled = back[part, cols].astype(jnp.float32) * gain_ref[:, cols]
            local = inverse * scaled - act_ref[part, cols].astype(jnp.float32) * pull
            local_ref[part, cols] = local
            passing[part, cols] = (top_ref[part, cols].astype(jnp.float32) + local).astype(jnp.bfloat16)
        out_copy(index).start()
        return 0

    lax.fori_loop(0, rows // chunk, one_chunk, 0)
    total = jnp.sum(gain_sum[...], axis=0, keepdims=True)
    for block in range(line * plane):
        gain_blocks[block] = total[:, block * width : (block + 1) * width]
    gain_copy = pltpu.make_async_copy(gain_blocks, gain_out, copied.at[rows // chunk])
    gain_copy.start()
    for index in range(rows // chunk):
        out_copy(index).wait()
    gain_copy.wait()


def finish(line, plane, groups, fold, early, inverse, act, top, gain, pieces):
    rows, features = act.shape
    blocks = line * plane
    vmem = pl.BlockSpec(memory_space=pltpu.VMEM)
    outs = [
        jax.ShapeDtypeStruct((rows, features), jnp.bfloat16),
        jax.ShapeDtypeStruct((rows, features), jnp.float32),
        jax.ShapeDtypeStruct((blocks, 1, features // blocks), jnp.float32),
    ]
    scratch = [
        pltpu.VMEM((blocks,) + pieces[0].shape[1:], jnp.bfloat16),
        pltpu.VMEM((rows, features), jnp.bfloat16),
        pltpu.VMEM((8, features), jnp.float32),
        pltpu.VMEM((rows, 128), jnp.float32),
        pltpu.VMEM((rows, features), jnp.bfloat16),
        pltpu.VMEM(outs[2].shape, jnp.float32),
    ]
    chunk = math.gcd(rows, 32)
    return pl.pallas_call(
        functools.partial(finish_kernel, line, plane, groups, fold, chunk),
        out_shape=outs,
        in_specs=[vmem] * (4 + len(early) + len(pieces)),
        out_specs=[pl.BlockSpec(memory_space=pl.ANY), vmem, pl.BlockSpec(memory_space=pl.ANY)],
        scratch_shapes=scratch + [pltpu.SemaphoreType.DMA((rows // chunk + 1,))],
        compiler_params=pltpu.CompilerParams(
            vmem_limit_bytes=grant(*early, act, top, *pieces, *outs, *scratch)
        ),
        cost_estimate=pl.CostEstimate(
            flops=16 * rows * features, bytes_accessed=12 * rows * features, transcendentals=0
        ),
        name="norm_backward",
    )(*early, inverse, act, top, gain, *pieces)


def hand_kernel(turn, chunk, incoming_ref, local_ref, result_ref, out_ref, loaded, staged, arrived, copied):
    rows, features = local_ref.shape
    parts = [pl.ds(start, chunk) for start in range(0, rows, chunk)]
    is_turn = lax.axis_index("section") == turn

    def through(source, staging, work):
        loads = [
            pltpu.make_async_copy(source.at[part], loaded.at[part], arrived.at[index])
            for index, part in enumerate(parts)
        ]
        stores = [
            pltpu.make_async_copy(staging.at[part], out_ref.at[part], copied.at[index])
            for index, part in enumerate(parts)
        ]
        for load in loads:
            load.start()
        for part, load, store in zip(parts, loads, stores):
            load.wait()
            work(part)
            store.start()
        for store in stores:
            store.wait()

    def add_local(part):
        for left in range(0, features, 128):
            cols = slice(left, left + 128)
            staged[part, cols] = (loaded[part, cols].astype(jnp.float32) + local_ref[part, cols]).astype(jnp.bfloat16)

    @pl.when(is_turn)
    def _():
        through(incoming_ref, staged, add_local)

    @pl.when(jnp.logical_not(is_turn))
    def _():
        through(result_ref, loaded, lambda part: None)


def hand_on(turn, chunk, incoming, local, result):
    rows, features = local.shape
    vmem = pl.BlockSpec(memory_space=pltpu.VMEM)
    hbm = pl.BlockSpec(memory_space=pl.ANY)
    return pl.pallas_call(
        functools.partial(hand_kernel, turn, chunk),
        out_shape=jax.ShapeDtypeStruct((rows, features), jnp.bfloat16),
        in_specs=[hbm, vmem, hbm],
        out_specs=hbm,
        scratch_shapes=[
            pltpu.VMEM((rows, features), jnp.bfloat16),
            pltpu.VMEM((rows, features), jnp.bfloat16),
            pltpu.SemaphoreType.DMA((rows // chunk,)),
            pltpu.SemaphoreType.DMA((rows // chunk,)),
        ],
        compiler_params=pltpu.CompilerParams(vmem_limit_bytes=grant(incoming, local, result)),
        cost_estimate=pl.CostEstimate(flops=0, bytes_accessed=0, transcendentals=0),
        name="hand_on",
    )(incoming, local, result)


def sum_kernel(scale, parts_ref, out_ref):
    total = parts_ref[0]
    for index in range(1, parts_ref.shape[0]):
        total = total + parts_ref[index]
    out_ref[...] = total * scale


def sum_scaled(parts, scale):
    vmem = pl.BlockSpec(memory_space=pltpu.VMEM)
    return pl.pallas_call(
        functools.partial(sum_kernel, scale),
        out_shape=jax.ShapeDtypeStruct(parts.shape[1:], jnp.float32),
        in_specs=[vmem],
        out_specs=vmem,
        compiler_params=pltpu.CompilerParams(vmem_limit_bytes=mebibyte),
        cost_estimate=pl.CostEstimate(flops=parts.size, bytes_accessed=4 * parts.size, transcendentals=0),
        name="sum_scaled",
    )(parts)


def sent_back(group_products, line, plane):
    return [group_products[0]] + [
        along_plane(group_products[step], step, line, plane, back=True) for step in range(1, plane)
    ]


def gathered_products(fold, tokens, shard, line, plane):
    held = {0: shard}
    groups = [(0,)]
    first = products(fold, tokens, [shard], 1)
    if line & (line - 1):
        for step in range(1, line):
            held[step] = along_line(shard, step, line, plane)
        groups.append(tuple(range(1, (line + 1) // 2)))
    elif line > 1:
        distance = line // 2
        while distance:
            held[distance] = along_line(shard, distance, line, plane)
            distance //= 2
        groups.append(tuple(sorted(step for step in held if step)))
        far = line // 2
        held[far], own = lax.optimization_barrier((held[far], first[0]))
        first = [own] + list(first[1:])
        distance = line // 4
        while distance:
            for step in sorted(held):
                if step and step % (2 * distance) == 0 and step + distance not in held:
                    held[step + distance] = along_line(held[step], distance, line, plane)
            distance //= 2
    groups.append(tuple(step for step in range(line) if not any(step in group for group in groups)))
    groups = [group for group in groups if group]
    pieces = [sent_back(first, line, plane)]
    for group in groups[1:]:
        shards = [held[step] for step in group]
        made = list(products(fold, tokens, shards, product_cost))
        if len(pieces) == 1:
            made[-1], pieces[0] = lax.optimization_barrier((made[-1], pieces[0]))
        pieces.append(sent_back(made, line, plane))
    return groups, pieces


def on_device(activations, key_grads, top_grad, norm_gains, w_key, lengths):
    micro_count, seq_rows, features = activations.shape[2:]
    rows = micro_count * seq_rows
    fold = math.gcd(rows, 16)
    replicas = lax.axis_size("dp")
    sections = lax.axis_size("section")
    plane = plane_size(replicas)
    line = replicas // plane
    grad_scale = 1.0 / math.sqrt(replicas * rows)
    act = activations.reshape(rows, features)

    key_rows = key_grads.reshape(rows, key_grads.shape[-1])
    inverse, own_rows = lax.optimization_barrier((live_inverse(seq_rows, lengths[0], act), key_rows))
    tokens = [own_rows] + [along_plane(key_rows, step, line, plane) for step in range(1, plane)]
    groups, pieces = gathered_products(fold, tokens, w_key[0], line, plane)
    split = max(1, len(groups) - 1)
    early, late = ([part[step] for step in range(plane) for part in some] for some in (pieces[:split], pieces[split:]))
    early = placed_early(line, plane, groups[:split], fold, inverse, act, norm_gains, early)
    top = top_grad.reshape(rows, features)
    passed, local, gain_blocks = finish(
        line, plane, groups[split:], fold, early, inverse, act, top, norm_gains, late
    )

    result = passed
    for turn in range(sections - 2, -1, -1):
        incoming = lax.ppermute(result, "section", [(turn + 1, turn), (turn, turn + 1)])
        result = hand_on(turn, seq_rows, incoming, local, result)

    gain_parts = lax.all_to_all(gain_blocks, "dp", split_axis=0, concat_axis=0, tiled=True)
    gain_parts, result = lax.optimization_barrier((gain_parts, result))
    grad_shard = sum_scaled(gain_parts, grad_scale)
    return (result.reshape(activations.shape), grad_shard)


def solution(mesh):
    placed = (
        P("section", "dp", None, None, None),
        P("section", "dp", None, None, None),
        P("dp", None, None, None),
        P("section", None),
        P("section", "dp", None),
        P("dp", None),
    )
    return jax.shard_map(
        on_device,
        mesh=mesh,
        in_specs=placed,
        out_specs=(P("section", "dp", None, None, None), P("section", "dp")),
        check_vma=False,
    )
```

```python
import functools
import math

import jax
import jax.numpy as jnp
from jax import lax
from jax.experimental import pallas as pl
from jax.experimental.pallas import tpu as pltpu
from jax.sharding import PartitionSpec as P

norm_epsilon = 1e-05
mebibyte = 1024 * 1024
product_cost = 10


def grant(*arrays):
    total = 4 * mebibyte
    for array in arrays:
        lanes = -(-array.shape[-1] // 128) * 128
        total += math.prod(array.shape[:-1]) * lanes * jnp.dtype(array.dtype).itemsize
    return -(-total // mebibyte) * mebibyte


def plane_size(replicas):
    size = 1
    while (2 * size) ** 2 <= replicas and replicas % (2 * size) == 0:
        size *= 2
    return size


def ahead(place, step, count):
    if count & (count - 1) == 0:
        return place ^ step
    return (place + step) % count


def behind(place, step, count):
    if count & (count - 1) == 0:
        return place ^ step
    return (place + count - step) % count


def along_line(value, step, line, plane):
    pairs = [
        (z * plane + q, ahead(z, step, line) * plane + q)
        for z in range(line)
        for q in range(plane)
    ]
    return lax.ppermute(value, "dp", pairs)


def along_plane(value, step, line, plane, back=False):
    partner = behind if back else ahead
    pairs = [
        (z * plane + q, z * plane + partner(q, step, plane))
        for z in range(line)
        for q in range(plane)
    ]
    return lax.ppermute(value, "dp", pairs)


def product_kernel(token_count, weight_count, fold, *refs):
    tokens = refs[:token_count]
    weights = refs[token_count : token_count + weight_count]
    outs = refs[token_count + weight_count :]
    for token_ref, out_ref in zip(tokens, outs):
        for index, weight_ref in enumerate(weights):
            product = lax.dot_general(
                token_ref[...],
                weight_ref[...],
                (((1,), (1,)), ((), ())),
                preferred_element_type=jnp.float32,
            ).astype(out_ref.dtype)
            width = product.shape[1]
            for part in range(product.shape[0] // fold):
                out_ref[index, :, part * width : (part + 1) * width] = product[part * fold : (part + 1) * fold, :]


def products(fold, tokens, weights, cost):
    rows, depth = tokens[0].shape
    width = weights[0].shape[0]
    count = len(weights)
    folded = (count, fold, rows // fold * width)
    outs = [jax.ShapeDtypeStruct(folded, jnp.bfloat16) for _ in tokens]
    return pl.pallas_call(
        functools.partial(product_kernel, len(tokens), count, fold),
        out_shape=outs,
        in_specs=[pl.BlockSpec(memory_space=pltpu.VMEM)] * (len(tokens) + count),
        out_specs=[pl.BlockSpec(memory_space=pltpu.VMEM)] * len(tokens),
        compiler_params=pltpu.CompilerParams(vmem_limit_bytes=grant(*tokens, *weights, *outs)),
        cost_estimate=pl.CostEstimate(
            flops=cost * 2 * rows * depth * width * count * len(tokens),
            bytes_accessed=2 * (rows * depth * len(tokens) + depth * width * count + rows * width * count * len(tokens)),
            transcendentals=0,
        ),
        name="token_products",
    )(*tokens, *weights)


def column_tile(features, most=512):
    tile = 128
    for width in range(128, most + 1, 128):
        if features % width == 0:
            tile = width
    return tile


def inverse_kernel(seq_rows, chunk, tile, lengths_ref, act_ref, inverse_ref):
    rows, features = act_ref.shape

    def one_chunk(index, _):
        start = pl.multiple_of(index * chunk, chunk)
        part = pl.ds(start, chunk)
        squares = jnp.zeros((chunk, 128), jnp.float32)
        for left in range(0, features, tile):
            wide = act_ref[part, left : left + tile].astype(jnp.float32)
            wide = wide * wide
            for lane in range(0, tile, 128):
                squares = squares + wide[:, lane : lane + 128]
        mean = jnp.sum(squares, axis=1, keepdims=True) / features
        position = lax.broadcasted_iota(jnp.int32, (chunk, 1), 0) + lax.rem(start, seq_rows)
        keep = position < lengths_ref[lax.div(start, seq_rows)]
        inverse = jnp.where(keep, lax.rsqrt(mean + norm_epsilon), 0.0)
        inverse_ref[part, :] = jnp.broadcast_to(inverse, (chunk, 128))
        return 0

    lax.fori_loop(0, rows // chunk, one_chunk, 0)


def live_inverse(seq_rows, lengths, act):
    rows, features = act.shape
    return pl.pallas_call(
        functools.partial(inverse_kernel, seq_rows, math.gcd(seq_rows, 16), column_tile(features)),
        out_shape=jax.ShapeDtypeStruct((rows, 128), jnp.float32),
        in_specs=[pl.BlockSpec(memory_space=pltpu.SMEM), pl.BlockSpec(memory_space=pltpu.VMEM)],
        out_specs=pl.BlockSpec(memory_space=pltpu.VMEM),
        compiler_params=pltpu.CompilerParams(vmem_limit_bytes=grant(act)),
        cost_estimate=pl.CostEstimate(
            flops=2 * rows * features, bytes_accessed=2 * rows * features, transcendentals=rows
        ),
        name="live_inverse",
    )(lengths, act)


def relative(owner, place, count):
    if count & (count - 1) == 0:
        return owner ^ place
    return (place + count - owner) % count


def place_pieces(line, plane, groups, fold, pieces, held, back):
    width = back.shape[1] // (line * plane)
    me = lax.axis_index("dp")
    z, q = lax.div(me, plane), lax.rem(me, plane)
    for step in range(plane):
        owner_q = ahead(q, step, plane)
        for group_index, group in enumerate(groups):
            piece = pieces[step * len(groups) + group_index]
            for index, line_step in enumerate(group):
                held[behind(z, line_step, line) * plane + owner_q] = piece[index]
    steps = [line_step for group in groups for line_step in group]
    for owner_z in range(line):
        line_step = relative(owner_z, z, line)
        here = functools.reduce(jnp.logical_or, [line_step == step for step in steps])

        @pl.when(here)
        def _():
            for part in range(back.shape[0] // fold):
                rows = slice(part * fold, (part + 1) * fold)
                for block in range(owner_z * plane, (owner_z + 1) * plane):
                    back[rows, block * width : (block + 1) * width] = held[
                        block, :, part * width : (part + 1) * width
                    ]


def add_sums(lefts, part, project, inverse_ref, act_ref, gain_ref, gain_sum, pulls):
    inverse = inverse_ref[part, :]
    pull = pulls[part, :]
    for left in lefts:
        cols = slice(left, left + 128)
        both = act_ref[part, cols].astype(jnp.float32) * project(part, cols)
        pull = pull + both * gain_ref[:, cols]
        both = both * inverse
        folded = both[:8, :]
        for row in range(8, both.shape[0], 8):
            folded = folded + both[row : row + 8, :]
        gain_sum[:, cols] += folded
    pulls[part, :] = pull


def early_kernel(line, plane, groups, fold, chunk, inverse_ref, act_ref, gain_ref, *refs):
    pieces = refs[:-4]
    back, pulls, gain_sum, held = refs[-4:]
    back[...] = jnp.zeros_like(back)
    place_pieces(line, plane, groups, fold, pieces, held, back)
    gain_sum[...] = jnp.zeros_like(gain_sum)
    pulls[...] = jnp.zeros_like(pulls)

    def project(part, cols):
        return back[part, cols].astype(jnp.float32)

    def one_chunk(index, _):
        part = pl.ds(pl.multiple_of(index * chunk, chunk), chunk)
        add_sums(range(0, back.shape[1], 128), part, project, inverse_ref, act_ref, gain_ref, gain_sum, pulls)
        return 0

    lax.fori_loop(0, back.shape[0] // chunk, one_chunk, 0)


def placed_early(line, plane, groups, fold, inverse, act, gain, pieces):
    rows, features = act.shape
    vmem = pl.BlockSpec(memory_space=pltpu.VMEM)
    outs = [
        jax.ShapeDtypeStruct((rows, features), jnp.bfloat16),
        jax.ShapeDtypeStruct((rows, 128), jnp.float32),
        jax.ShapeDtypeStruct((8, features), jnp.float32),
    ]
    scratch = [pltpu.VMEM((line * plane,) + pieces[0].shape[1:], jnp.bfloat16)]
    return pl.pallas_call(
        functools.partial(early_kernel, line, plane, groups, fold, math.gcd(rows, 32)),
        out_shape=outs,
        in_specs=[vmem] * (3 + len(pieces)),
        out_specs=[vmem] * len(outs),
        scratch_shapes=scratch,
        compiler_params=pltpu.CompilerParams(
            vmem_limit_bytes=grant(inverse, act, gain, *pieces, *outs, *scratch)
        ),
        cost_estimate=pl.CostEstimate(
            flops=8 * rows * features, bytes_accessed=8 * rows * features, transcendentals=0
        ),
        name="placed_early",
    )(inverse, act, gain, *pieces)


def finish_kernel(
    line,
    plane,
    groups,
    fold,
    last,
    chunk,
    early_ref,
    early_pulls,
    early_gains,
    inverse_ref,
    act_ref,
    top_ref,
    gain_ref,
    *refs,
):
    pieces = refs[:-10]
    passed_ref, local_ref, gain_out, held, back, gain_sum, pulls, passing, gain_blocks, copied = refs[-10:]
    rows, features = back.shape
    width = features // (line * plane)
    late_steps = [step for group in groups for step in group]
    late_z = behind(lax.div(lax.axis_index("dp"), plane), late_steps[0], line)
    is_last = lax.axis_index("section") == last
    back[...] = early_ref[...]
    place_pieces(line, plane, groups, fold, pieces, held, back)
    gain_sum[...] = early_gains[...]
    pulls[...] = early_pulls[...]

    def project(part, cols):
        return back[part, cols].astype(jnp.float32) - early_ref[part, cols].astype(jnp.float32)

    def add_late(part, lefts):
        add_sums(lefts, part, project, inverse_ref, act_ref, gain_ref, gain_sum, pulls)

    def out_copy(index):
        part = pl.ds(pl.multiple_of(index * chunk, chunk), chunk)
        return pltpu.make_async_copy(passing.at[part], passed_ref.at[part], copied.at[index])

    def one_chunk(index, _):
        part = pl.ds(pl.multiple_of(index * chunk, chunk), chunk)
        if len(late_steps) > 1:
            add_late(part, range(0, features, 128))
        else:
            for owner_z in range(line):
                first = owner_z * plane * width // 128 * 128
                after = (owner_z + 1) * plane * width

                @pl.when(late_z == owner_z)
                def _():
                    add_late(part, range(first, after, 128))

        inverse = inverse_ref[part, :]
        pull = jnp.sum(pulls[part, :], axis=1, keepdims=True) / features
        pull = jnp.broadcast_to(pull, inverse.shape) * inverse * inverse * inverse

        def local_term(cols):
            scaled = back[part, cols].astype(jnp.float32) * gain_ref[:, cols]
            return inverse * scaled - act_ref[part, cols].astype(jnp.float32) * pull

        @pl.when(is_last)
        def _():
            for left in range(0, features, 128):
                cols = slice(left, left + 128)
                passing[part, cols] = (top_ref[part, cols].astype(jnp.float32) + local_term(cols)).astype(jnp.bfloat16)
            out_copy(index).start()

        @pl.when(jnp.logical_not(is_last))
        def _():
            for left in range(0, features, 128):
                cols = slice(left, left + 128)
                local_ref[part, cols] = local_term(cols)

        return 0

    lax.fori_loop(0, rows // chunk, one_chunk, 0)
    total = jnp.sum(gain_sum[...], axis=0, keepdims=True)
    for block in range(line * plane):
        gain_blocks[block] = total[:, block * width : (block + 1) * width]
    gain_copy = pltpu.make_async_copy(gain_blocks, gain_out, copied.at[rows // chunk])
    gain_copy.start()

    @pl.when(is_last)
    def _():
        for index in range(rows // chunk):
            out_copy(index).wait()

    gain_copy.wait()


def finish(line, plane, groups, fold, last, early, inverse, act, top, gain, pieces):
    rows, features = act.shape
    blocks = line * plane
    vmem = pl.BlockSpec(memory_space=pltpu.VMEM)
    outs = [
        jax.ShapeDtypeStruct((rows, features), jnp.bfloat16),
        jax.ShapeDtypeStruct((rows, features), jnp.float32),
        jax.ShapeDtypeStruct((blocks, 1, features // blocks), jnp.float32),
    ]
    scratch = [
        pltpu.VMEM((blocks,) + pieces[0].shape[1:], jnp.bfloat16),
        pltpu.VMEM((rows, features), jnp.bfloat16),
        pltpu.VMEM((8, features), jnp.float32),
        pltpu.VMEM((rows, 128), jnp.float32),
        pltpu.VMEM((rows, features), jnp.bfloat16),
        pltpu.VMEM(outs[2].shape, jnp.float32),
    ]
    chunk = math.gcd(rows, 32)
    return pl.pallas_call(
        functools.partial(finish_kernel, line, plane, groups, fold, last, chunk),
        out_shape=outs,
        in_specs=[vmem] * (4 + len(early) + len(pieces)),
        out_specs=[pl.BlockSpec(memory_space=pl.ANY), vmem, pl.BlockSpec(memory_space=pl.ANY)],
        scratch_shapes=scratch + [pltpu.SemaphoreType.DMA((rows // chunk + 1,))],
        compiler_params=pltpu.CompilerParams(
            vmem_limit_bytes=grant(*early, act, top, *pieces, *outs, *scratch)
        ),
        cost_estimate=pl.CostEstimate(
            flops=16 * rows * features, bytes_accessed=12 * rows * features, transcendentals=0
        ),
        name="norm_backward",
    )(*early, inverse, act, top, gain, *pieces)


def hand_kernel(turn, chunk, incoming_ref, local_ref, result_ref, out_ref, loaded, staged, arrived, copied):
    rows, features = local_ref.shape
    parts = [pl.ds(start, chunk) for start in range(0, rows, chunk)]
    is_turn = lax.axis_index("section") == turn

    def through(source, staging, work):
        loads = [
            pltpu.make_async_copy(source.at[part], loaded.at[part], arrived.at[index])
            for index, part in enumerate(parts)
        ]
        stores = [
            pltpu.make_async_copy(staging.at[part], out_ref.at[part], copied.at[index])
            for index, part in enumerate(parts)
        ]
        for load in loads:
            load.start()
        for part, load, store in zip(parts, loads, stores):
            load.wait()
            work(part)
            store.start()
        for store in stores:
            store.wait()

    def add_local(part):
        for left in range(0, features, 128):
            cols = slice(left, left + 128)
            staged[part, cols] = (loaded[part, cols].astype(jnp.float32) + local_ref[part, cols]).astype(jnp.bfloat16)

    @pl.when(is_turn)
    def _():
        through(incoming_ref, staged, add_local)

    @pl.when(jnp.logical_not(is_turn))
    def _():
        through(result_ref, loaded, lambda part: None)


def hand_on(turn, chunk, incoming, local, result):
    rows, features = local.shape
    vmem = pl.BlockSpec(memory_space=pltpu.VMEM)
    hbm = pl.BlockSpec(memory_space=pl.ANY)
    return pl.pallas_call(
        functools.partial(hand_kernel, turn, chunk),
        out_shape=jax.ShapeDtypeStruct((rows, features), jnp.bfloat16),
        in_specs=[hbm, vmem, hbm],
        out_specs=hbm,
        scratch_shapes=[
            pltpu.VMEM((rows, features), jnp.bfloat16),
            pltpu.VMEM((rows, features), jnp.bfloat16),
            pltpu.SemaphoreType.DMA((rows // chunk,)),
            pltpu.SemaphoreType.DMA((rows // chunk,)),
        ],
        compiler_params=pltpu.CompilerParams(vmem_limit_bytes=grant(incoming, local, result)),
        cost_estimate=pl.CostEstimate(flops=0, bytes_accessed=0, transcendentals=0),
        name="hand_on",
    )(incoming, local, result)


def sum_kernel(scale, parts_ref, out_ref):
    total = parts_ref[0]
    for index in range(1, parts_ref.shape[0]):
        total = total + parts_ref[index]
    out_ref[...] = total * scale


def sum_scaled(parts, scale):
    vmem = pl.BlockSpec(memory_space=pltpu.VMEM)
    return pl.pallas_call(
        functools.partial(sum_kernel, scale),
        out_shape=jax.ShapeDtypeStruct(parts.shape[1:], jnp.float32),
        in_specs=[vmem],
        out_specs=vmem,
        compiler_params=pltpu.CompilerParams(vmem_limit_bytes=mebibyte),
        cost_estimate=pl.CostEstimate(flops=parts.size, bytes_accessed=4 * parts.size, transcendentals=0),
        name="sum_scaled",
    )(parts)


def sent_back(group_products, line, plane):
    return [group_products[0]] + [
        along_plane(group_products[step], step, line, plane, back=True) for step in range(1, plane)
    ]


def gathered_products(fold, tokens, shard, line, plane):
    held = {0: shard}
    groups = [(0,)]
    first = products(fold, tokens, [shard], 1)
    if line & (line - 1):
        for step in range(1, line):
            held[step] = along_line(shard, step, line, plane)
        groups.append(tuple(range(1, (line + 1) // 2)))
    elif line > 1:
        distance = line // 2
        while distance:
            held[distance] = along_line(shard, distance, line, plane)
            distance //= 2
        groups.append(tuple(sorted(step for step in held if step)))
        far = line // 2
        held[far], own = lax.optimization_barrier((held[far], first[0]))
        first = [own] + list(first[1:])
        distance = line // 4
        while distance:
            for step in sorted(held):
                if step and step % (2 * distance) == 0 and step + distance not in held:
                    held[step + distance] = along_line(held[step], distance, line, plane)
            distance //= 2
    groups.append(tuple(step for step in range(line) if not any(step in group for group in groups)))
    groups = [group for group in groups if group]
    pieces = [sent_back(first, line, plane)]
    for group in groups[1:]:
        shards = [held[step] for step in group]
        made = list(products(fold, tokens, shards, product_cost))
        if len(pieces) == 1:
            made[-1], pieces[0] = lax.optimization_barrier((made[-1], pieces[0]))
        pieces.append(sent_back(made, line, plane))
    return groups, pieces


def on_device(activations, key_grads, top_grad, norm_gains, w_key, lengths):
    micro_count, seq_rows, features = activations.shape[2:]
    rows = micro_count * seq_rows
    fold = math.gcd(rows, 16)
    replicas = lax.axis_size("dp")
    sections = lax.axis_size("section")
    plane = plane_size(replicas)
    line = replicas // plane
    grad_scale = 1.0 / math.sqrt(replicas * rows)
    act = activations.reshape(rows, features)

    key_rows = key_grads.reshape(rows, key_grads.shape[-1])
    inverse, own_rows = lax.optimization_barrier((live_inverse(seq_rows, lengths[0], act), key_rows))
    tokens = [own_rows] + [along_plane(key_rows, step, line, plane) for step in range(1, plane)]
    groups, pieces = gathered_products(fold, tokens, w_key[0], line, plane)
    split = max(1, len(groups) - 1)
    early, late = ([part[step] for step in range(plane) for part in some] for some in (pieces[:split], pieces[split:]))
    early = placed_early(line, plane, groups[:split], fold, inverse, act, norm_gains, early)
    top = top_grad.reshape(rows, features)
    passed, local, gain_blocks = finish(
        line, plane, groups[split:], fold, sections - 1, early, inverse, act, top, norm_gains, late
    )

    result = passed
    for turn in range(sections - 2, -1, -1):
        incoming = lax.ppermute(result, "section", [(turn + 1, turn), (turn, turn + 1)])
        result = hand_on(turn, seq_rows, incoming, local, result)

    gain_parts = lax.all_to_all(gain_blocks, "dp", split_axis=0, concat_axis=0, tiled=True)
    gain_parts, result = lax.optimization_barrier((gain_parts, result))
    grad_shard = sum_scaled(gain_parts, grad_scale)
    return (result.reshape(activations.shape), grad_shard)


def solution(mesh):
    placed = (
        P("section", "dp", None, None, None),
        P("section", "dp", None, None, None),
        P("dp", None, None, None),
        P("section", None),
        P("section", "dp", None),
        P("dp", None),
    )
    return jax.shard_map(
        on_device,
        mesh=mesh,
        in_specs=placed,
        out_specs=(P("section", "dp", None, None, None), P("section", "dp")),
        check_vma=False,
    )
```

```python
import functools
import math

import jax
import jax.numpy as jnp
from jax import lax
from jax.experimental import pallas as pl
from jax.experimental.pallas import tpu as pltpu
from jax.sharding import PartitionSpec as P

norm_epsilon = 1e-05
mebibyte = 1024 * 1024
product_cost = 10


def grant(*arrays):
    total = 4 * mebibyte
    for array in arrays:
        lanes = -(-array.shape[-1] // 128) * 128
        total += math.prod(array.shape[:-1]) * lanes * jnp.dtype(array.dtype).itemsize
    return -(-total // mebibyte) * mebibyte


def plane_size(replicas):
    size = 1
    while (2 * size) ** 2 <= replicas and replicas % (2 * size) == 0:
        size *= 2
    return size


def ahead(place, step, count):
    if count & (count - 1) == 0:
        return place ^ step
    return (place + step) % count


def behind(place, step, count):
    if count & (count - 1) == 0:
        return place ^ step
    return (place + count - step) % count


def along_line(value, step, line, plane):
    pairs = [
        (z * plane + q, ahead(z, step, line) * plane + q)
        for z in range(line)
        for q in range(plane)
    ]
    return lax.ppermute(value, "dp", pairs)


def along_plane(value, step, line, plane, back=False):
    partner = behind if back else ahead
    pairs = [
        (z * plane + q, z * plane + partner(q, step, plane))
        for z in range(line)
        for q in range(plane)
    ]
    return lax.ppermute(value, "dp", pairs)


def product_kernel(token_count, weight_count, fold, *refs):
    tokens = refs[:token_count]
    weights = refs[token_count : token_count + weight_count]
    outs = refs[token_count + weight_count :]
    for token_ref, out_ref in zip(tokens, outs):
        for index, weight_ref in enumerate(weights):
            product = lax.dot_general(
                token_ref[...],
                weight_ref[...],
                (((1,), (1,)), ((), ())),
                preferred_element_type=jnp.float32,
            ).astype(out_ref.dtype)
            width = product.shape[1]
            for part in range(product.shape[0] // fold):
                out_ref[index, :, part * width : (part + 1) * width] = product[part * fold : (part + 1) * fold, :]


def products(fold, tokens, weights, cost):
    rows, depth = tokens[0].shape
    width = weights[0].shape[0]
    count = len(weights)
    folded = (count, fold, rows // fold * width)
    outs = [jax.ShapeDtypeStruct(folded, jnp.bfloat16) for _ in tokens]
    return pl.pallas_call(
        functools.partial(product_kernel, len(tokens), count, fold),
        out_shape=outs,
        in_specs=[pl.BlockSpec(memory_space=pltpu.VMEM)] * (len(tokens) + count),
        out_specs=[pl.BlockSpec(memory_space=pltpu.VMEM)] * len(tokens),
        compiler_params=pltpu.CompilerParams(vmem_limit_bytes=grant(*tokens, *weights, *outs)),
        cost_estimate=pl.CostEstimate(
            flops=cost * 2 * rows * depth * width * count * len(tokens),
            bytes_accessed=2 * (rows * depth * len(tokens) + depth * width * count + rows * width * count * len(tokens)),
            transcendentals=0,
        ),
        name="token_products",
    )(*tokens, *weights)


def column_tile(features, most=512):
    tile = 128
    for width in range(128, most + 1, 128):
        if features % width == 0:
            tile = width
    return tile


def inverse_kernel(seq_rows, chunk, tile, lengths_ref, act_ref, inverse_ref):
    rows, features = act_ref.shape

    def one_chunk(index, _):
        start = pl.multiple_of(index * chunk, chunk)
        part = pl.ds(start, chunk)
        squares = jnp.zeros((chunk, 128), jnp.float32)
        for left in range(0, features, tile):
            wide = act_ref[part, left : left + tile].astype(jnp.float32)
            wide = wide * wide
            for lane in range(0, tile, 128):
                squares = squares + wide[:, lane : lane + 128]
        mean = jnp.sum(squares, axis=1, keepdims=True) / features
        position = lax.broadcasted_iota(jnp.int32, (chunk, 1), 0) + lax.rem(start, seq_rows)
        keep = position < lengths_ref[lax.div(start, seq_rows)]
        inverse = jnp.where(keep, lax.rsqrt(mean + norm_epsilon), 0.0)
        inverse_ref[part, :] = jnp.broadcast_to(inverse, (chunk, 128))
        return 0

    lax.fori_loop(0, rows // chunk, one_chunk, 0)


def live_inverse(seq_rows, lengths, act):
    rows, features = act.shape
    return pl.pallas_call(
        functools.partial(inverse_kernel, seq_rows, math.gcd(seq_rows, 16), column_tile(features)),
        out_shape=jax.ShapeDtypeStruct((rows, 128), jnp.float32),
        in_specs=[pl.BlockSpec(memory_space=pltpu.SMEM), pl.BlockSpec(memory_space=pltpu.VMEM)],
        out_specs=pl.BlockSpec(memory_space=pltpu.VMEM),
        compiler_params=pltpu.CompilerParams(vmem_limit_bytes=grant(act)),
        cost_estimate=pl.CostEstimate(
            flops=2 * rows * features, bytes_accessed=2 * rows * features, transcendentals=rows
        ),
        name="live_inverse",
    )(lengths, act)


def relative(owner, place, count):
    if count & (count - 1) == 0:
        return owner ^ place
    return (place + count - owner) % count


def place_pieces(line, plane, groups, fold, pieces, held, back):
    width = back.shape[1] // (line * plane)
    me = lax.axis_index("dp")
    z, q = lax.div(me, plane), lax.rem(me, plane)
    for step in range(plane):
        owner_q = ahead(q, step, plane)
        for group_index, group in enumerate(groups):
            piece = pieces[step * len(groups) + group_index]
            for index, line_step in enumerate(group):
                held[behind(z, line_step, line) * plane + owner_q] = piece[index]
    steps = [line_step for group in groups for line_step in group]
    for owner_z in range(line):
        line_step = relative(owner_z, z, line)
        here = functools.reduce(jnp.logical_or, [line_step == step for step in steps])

        @pl.when(here)
        def _():
            for part in range(back.shape[0] // fold):
                rows = slice(part * fold, (part + 1) * fold)
                for block in range(owner_z * plane, (owner_z + 1) * plane):
                    back[rows, block * width : (block + 1) * width] = held[
                        block, :, part * width : (part + 1) * width
                    ]


def add_sums(lefts, part, project, inverse_ref, act_ref, gain_ref, gain_sum, pulls):
    inverse = inverse_ref[part, :]
    pull = pulls[part, :]
    for left in lefts:
        cols = slice(left, left + 128)
        both = act_ref[part, cols].astype(jnp.float32) * project(part, cols)
        pull = pull + both * gain_ref[:, cols]
        both = both * inverse
        folded = both[:8, :]
        for row in range(8, both.shape[0], 8):
            folded = folded + both[row : row + 8, :]
        gain_sum[:, cols] += folded
    pulls[part, :] = pull


def early_kernel(line, plane, groups, fold, chunk, inverse_ref, act_ref, gain_ref, *refs):
    pieces = refs[:-4]
    back, pulls, gain_sum, held = refs[-4:]
    back[...] = jnp.zeros_like(back)
    place_pieces(line, plane, groups, fold, pieces, held, back)
    gain_sum[...] = jnp.zeros_like(gain_sum)
    pulls[...] = jnp.zeros_like(pulls)

    def project(part, cols):
        return back[part, cols].astype(jnp.float32)

    def one_chunk(index, _):
        part = pl.ds(pl.multiple_of(index * chunk, chunk), chunk)
        add_sums(range(0, back.shape[1], 128), part, project, inverse_ref, act_ref, gain_ref, gain_sum, pulls)
        return 0

    lax.fori_loop(0, back.shape[0] // chunk, one_chunk, 0)


def placed_early(line, plane, groups, fold, inverse, act, gain, pieces):
    rows, features = act.shape
    vmem = pl.BlockSpec(memory_space=pltpu.VMEM)
    outs = [
        jax.ShapeDtypeStruct((rows, features), jnp.bfloat16),
        jax.ShapeDtypeStruct((rows, 128), jnp.float32),
        jax.ShapeDtypeStruct((8, features), jnp.float32),
    ]
    scratch = [pltpu.VMEM((line * plane,) + pieces[0].shape[1:], jnp.bfloat16)]
    return pl.pallas_call(
        functools.partial(early_kernel, line, plane, groups, fold, math.gcd(rows, 32)),
        out_shape=outs,
        in_specs=[vmem] * (3 + len(pieces)),
        out_specs=[vmem] * len(outs),
        scratch_shapes=scratch,
        compiler_params=pltpu.CompilerParams(
            vmem_limit_bytes=grant(inverse, act, gain, *pieces, *outs, *scratch)
        ),
        cost_estimate=pl.CostEstimate(
            flops=8 * rows * features, bytes_accessed=8 * rows * features, transcendentals=0
        ),
        name="placed_early",
    )(inverse, act, gain, *pieces)


def finish_kernel(
    line,
    plane,
    groups,
    fold,
    last,
    chunk,
    early_ref,
    early_pulls,
    early_gains,
    inverse_ref,
    act_ref,
    top_ref,
    gain_ref,
    *refs,
):
    pieces = refs[:-10]
    passed_ref, local_ref, gain_out, held, back, gain_sum, pulls, passing, gain_blocks, copied = refs[-10:]
    rows, features = back.shape
    width = features // (line * plane)
    late_steps = [step for group in groups for step in group]
    late_z = behind(lax.div(lax.axis_index("dp"), plane), late_steps[0], line)
    is_last = lax.axis_index("section") == last
    back[...] = early_ref[...]
    place_pieces(line, plane, groups, fold, pieces, held, back)
    gain_sum[...] = early_gains[...]
    pulls[...] = early_pulls[...]

    def project(part, cols):
        return back[part, cols].astype(jnp.float32) - early_ref[part, cols].astype(jnp.float32)

    def add_late(part, lefts):
        add_sums(lefts, part, project, inverse_ref, act_ref, gain_ref, gain_sum, pulls)

    def out_copy(index):
        part = pl.ds(pl.multiple_of(index * chunk, chunk), chunk)
        return pltpu.make_async_copy(passing.at[part], passed_ref.at[part], copied.at[index])

    def late_sums(index, _):
        part = pl.ds(pl.multiple_of(index * chunk, chunk), chunk)
        if len(late_steps) > 1:
            add_late(part, range(0, features, 128))
        else:
            for owner_z in range(line):
                first = owner_z * plane * width // 128 * 128
                after = (owner_z + 1) * plane * width

                @pl.when(late_z == owner_z)
                def _():
                    add_late(part, range(first, after, 128))

        return 0

    def terms(index, _):
        part = pl.ds(pl.multiple_of(index * chunk, chunk), chunk)
        inverse = inverse_ref[part, :]
        pull = jnp.sum(pulls[part, :], axis=1, keepdims=True) / features
        pull = jnp.broadcast_to(pull, inverse.shape) * inverse * inverse * inverse

        def local_term(cols):
            scaled = back[part, cols].astype(jnp.float32) * gain_ref[:, cols]
            return inverse * scaled - act_ref[part, cols].astype(jnp.float32) * pull

        @pl.when(is_last)
        def _():
            for left in range(0, features, 128):
                cols = slice(left, left + 128)
                passing[part, cols] = (top_ref[part, cols].astype(jnp.float32) + local_term(cols)).astype(jnp.bfloat16)
            out_copy(index).start()

        @pl.when(jnp.logical_not(is_last))
        def _():
            for left in range(0, features, 128):
                cols = slice(left, left + 128)
                local_ref[part, cols] = local_term(cols)

        return 0

    lax.fori_loop(0, rows // chunk, late_sums, 0)
    total = jnp.sum(gain_sum[...], axis=0, keepdims=True)
    for block in range(line * plane):
        gain_blocks[block] = total[:, block * width : (block + 1) * width]
    gain_copy = pltpu.make_async_copy(gain_blocks, gain_out, copied.at[rows // chunk])
    gain_copy.start()
    lax.fori_loop(0, rows // chunk, terms, 0)

    @pl.when(is_last)
    def _():
        for index in range(rows // chunk):
            out_copy(index).wait()

    gain_copy.wait()


def finish(line, plane, groups, fold, last, early, inverse, act, top, gain, pieces):
    rows, features = act.shape
    blocks = line * plane
    vmem = pl.BlockSpec(memory_space=pltpu.VMEM)
    outs = [
        jax.ShapeDtypeStruct((rows, features), jnp.bfloat16),
        jax.ShapeDtypeStruct((rows, features), jnp.float32),
        jax.ShapeDtypeStruct((blocks, 1, features // blocks), jnp.float32),
    ]
    scratch = [
        pltpu.VMEM((blocks,) + pieces[0].shape[1:], jnp.bfloat16),
        pltpu.VMEM((rows, features), jnp.bfloat16),
        pltpu.VMEM((8, features), jnp.float32),
        pltpu.VMEM((rows, 128), jnp.float32),
        pltpu.VMEM((rows, features), jnp.bfloat16),
        pltpu.VMEM(outs[2].shape, jnp.float32),
    ]
    chunk = math.gcd(rows, 32)
    return pl.pallas_call(
        functools.partial(finish_kernel, line, plane, groups, fold, last, chunk),
        out_shape=outs,
        in_specs=[vmem] * (4 + len(early) + len(pieces)),
        out_specs=[pl.BlockSpec(memory_space=pl.ANY), vmem, pl.BlockSpec(memory_space=pl.ANY)],
        scratch_shapes=scratch + [pltpu.SemaphoreType.DMA((rows // chunk + 1,))],
        compiler_params=pltpu.CompilerParams(
            vmem_limit_bytes=grant(*early, act, top, *pieces, *outs, *scratch)
        ),
        cost_estimate=pl.CostEstimate(
            flops=16 * rows * features, bytes_accessed=12 * rows * features, transcendentals=0
        ),
        name="norm_backward",
    )(*early, inverse, act, top, gain, *pieces)


def hand_kernel(turn, chunk, incoming_ref, local_ref, result_ref, out_ref, loaded, staged, arrived, copied):
    rows, features = local_ref.shape
    parts = [pl.ds(start, chunk) for start in range(0, rows, chunk)]
    is_turn = lax.axis_index("section") == turn

    def through(source, staging, work):
        loads = [
            pltpu.make_async_copy(source.at[part], loaded.at[part], arrived.at[index])
            for index, part in enumerate(parts)
        ]
        stores = [
            pltpu.make_async_copy(staging.at[part], out_ref.at[part], copied.at[index])
            for index, part in enumerate(parts)
        ]
        for load in loads:
            load.start()
        for part, load, store in zip(parts, loads, stores):
            load.wait()
            work(part)
            store.start()
        for store in stores:
            store.wait()

    def add_local(part):
        for left in range(0, features, 128):
            cols = slice(left, left + 128)
            staged[part, cols] = (loaded[part, cols].astype(jnp.float32) + local_ref[part, cols]).astype(jnp.bfloat16)

    @pl.when(is_turn)
    def _():
        through(incoming_ref, staged, add_local)

    @pl.when(jnp.logical_not(is_turn))
    def _():
        through(result_ref, loaded, lambda part: None)


def hand_on(turn, chunk, incoming, local, result):
    rows, features = local.shape
    vmem = pl.BlockSpec(memory_space=pltpu.VMEM)
    hbm = pl.BlockSpec(memory_space=pl.ANY)
    return pl.pallas_call(
        functools.partial(hand_kernel, turn, chunk),
        out_shape=jax.ShapeDtypeStruct((rows, features), jnp.bfloat16),
        in_specs=[hbm, vmem, hbm],
        out_specs=hbm,
        scratch_shapes=[
            pltpu.VMEM((rows, features), jnp.bfloat16),
            pltpu.VMEM((rows, features), jnp.bfloat16),
            pltpu.SemaphoreType.DMA((rows // chunk,)),
            pltpu.SemaphoreType.DMA((rows // chunk,)),
        ],
        compiler_params=pltpu.CompilerParams(vmem_limit_bytes=grant(incoming, local, result)),
        cost_estimate=pl.CostEstimate(flops=0, bytes_accessed=0, transcendentals=0),
        name="hand_on",
    )(incoming, local, result)


def sum_kernel(scale, parts_ref, out_ref):
    total = parts_ref[0]
    for index in range(1, parts_ref.shape[0]):
        total = total + parts_ref[index]
    out_ref[...] = total * scale


def sum_scaled(parts, scale):
    vmem = pl.BlockSpec(memory_space=pltpu.VMEM)
    return pl.pallas_call(
        functools.partial(sum_kernel, scale),
        out_shape=jax.ShapeDtypeStruct(parts.shape[1:], jnp.float32),
        in_specs=[vmem],
        out_specs=vmem,
        compiler_params=pltpu.CompilerParams(vmem_limit_bytes=mebibyte),
        cost_estimate=pl.CostEstimate(flops=parts.size, bytes_accessed=4 * parts.size, transcendentals=0),
        name="sum_scaled",
    )(parts)


def sent_back(group_products, line, plane):
    return [group_products[0]] + [
        along_plane(group_products[step], step, line, plane, back=True) for step in range(1, plane)
    ]


def gathered_products(fold, tokens, shard, line, plane):
    held = {0: shard}
    groups = [(0,)]
    first = products(fold, tokens, [shard], 1)
    if line & (line - 1):
        for step in range(1, line):
            held[step] = along_line(shard, step, line, plane)
        groups.append(tuple(range(1, (line + 1) // 2)))
    elif line > 1:
        distance = line // 2
        while distance:
            held[distance] = along_line(shard, distance, line, plane)
            distance //= 2
        groups.append(tuple(sorted(step for step in held if step)))
        far = line // 2
        held[far], own = lax.optimization_barrier((held[far], first[0]))
        first = [own] + list(first[1:])
        distance = line // 4
        while distance:
            for step in sorted(held):
                if step and step % (2 * distance) == 0 and step + distance not in held:
                    held[step + distance] = along_line(held[step], distance, line, plane)
            distance //= 2
    groups.append(tuple(step for step in range(line) if not any(step in group for group in groups)))
    groups = [group for group in groups if group]
    pieces = [sent_back(first, line, plane)]
    for group in groups[1:]:
        shards = [held[step] for step in group]
        made = list(products(fold, tokens, shards, product_cost))
        if len(pieces) == 1:
            made[-1], pieces[0] = lax.optimization_barrier((made[-1], pieces[0]))
        pieces.append(sent_back(made, line, plane))
    return groups, pieces


def on_device(activations, key_grads, top_grad, norm_gains, w_key, lengths):
    micro_count, seq_rows, features = activations.shape[2:]
    rows = micro_count * seq_rows
    fold = math.gcd(rows, 16)
    replicas = lax.axis_size("dp")
    sections = lax.axis_size("section")
    plane = plane_size(replicas)
    line = replicas // plane
    grad_scale = 1.0 / math.sqrt(replicas * rows)
    act = activations.reshape(rows, features)

    key_rows = key_grads.reshape(rows, key_grads.shape[-1])
    inverse, own_rows = lax.optimization_barrier((live_inverse(seq_rows, lengths[0], act), key_rows))
    tokens = [own_rows] + [along_plane(key_rows, step, line, plane) for step in range(1, plane)]
    groups, pieces = gathered_products(fold, tokens, w_key[0], line, plane)
    split = max(1, len(groups) - 1)
    early, late = ([part[step] for step in range(plane) for part in some] for some in (pieces[:split], pieces[split:]))
    early = placed_early(line, plane, groups[:split], fold, inverse, act, norm_gains, early)
    top = top_grad.reshape(rows, features)
    passed, local, gain_blocks = finish(
        line, plane, groups[split:], fold, sections - 1, early, inverse, act, top, norm_gains, late
    )

    result = passed
    for turn in range(sections - 2, -1, -1):
        incoming = lax.ppermute(result, "section", [(turn + 1, turn), (turn, turn + 1)])
        result = hand_on(turn, seq_rows, incoming, local, result)

    gain_parts = lax.all_to_all(gain_blocks, "dp", split_axis=0, concat_axis=0, tiled=True)
    gain_parts, result = lax.optimization_barrier((gain_parts, result))
    grad_shard = sum_scaled(gain_parts, grad_scale)
    return (result.reshape(activations.shape), grad_shard)


def solution(mesh):
    placed = (
        P("section", "dp", None, None, None),
        P("section", "dp", None, None, None),
        P("dp", None, None, None),
        P("section", None),
        P("section", "dp", None),
        P("dp", None),
    )
    return jax.shard_map(
        on_device,
        mesh=mesh,
        in_specs=placed,
        out_specs=(P("section", "dp", None, None, None), P("section", "dp")),
        check_vma=False,
    )
```

```python
import functools
import math

import jax
import jax.numpy as jnp
from jax import lax
from jax.experimental import pallas as pl
from jax.experimental.pallas import tpu as pltpu
from jax.sharding import PartitionSpec as P

norm_epsilon = 1e-05
mebibyte = 1024 * 1024
product_cost = 10


def grant(*arrays):
    total = 4 * mebibyte
    for array in arrays:
        lanes = -(-array.shape[-1] // 128) * 128
        total += math.prod(array.shape[:-1]) * lanes * jnp.dtype(array.dtype).itemsize
    return -(-total // mebibyte) * mebibyte


def plane_size(replicas):
    size = 1
    while (2 * size) ** 2 <= replicas and replicas % (2 * size) == 0:
        size *= 2
    return size


def ahead(place, step, count):
    if count & (count - 1) == 0:
        return place ^ step
    return (place + step) % count


def behind(place, step, count):
    if count & (count - 1) == 0:
        return place ^ step
    return (place + count - step) % count


def along_line(value, step, line, plane):
    pairs = [
        (z * plane + q, ahead(z, step, line) * plane + q)
        for z in range(line)
        for q in range(plane)
    ]
    return lax.ppermute(value, "dp", pairs)


def along_plane(value, step, line, plane, back=False):
    partner = behind if back else ahead
    pairs = [
        (z * plane + q, z * plane + partner(q, step, plane))
        for z in range(line)
        for q in range(plane)
    ]
    return lax.ppermute(value, "dp", pairs)


def product_kernel(token_count, weight_count, fold, *refs):
    tokens = refs[:token_count]
    weights = refs[token_count : token_count + weight_count]
    outs = refs[token_count + weight_count :]
    for token_ref, out_ref in zip(tokens, outs):
        for index, weight_ref in enumerate(weights):
            product = lax.dot_general(
                token_ref[...],
                weight_ref[...],
                (((1,), (1,)), ((), ())),
                preferred_element_type=jnp.float32,
            ).astype(out_ref.dtype)
            width = product.shape[1]
            for part in range(product.shape[0] // fold):
                out_ref[index, :, part * width : (part + 1) * width] = product[part * fold : (part + 1) * fold, :]


def products(fold, tokens, weights, cost):
    rows, depth = tokens[0].shape
    width = weights[0].shape[0]
    count = len(weights)
    folded = (count, fold, rows // fold * width)
    outs = [jax.ShapeDtypeStruct(folded, jnp.bfloat16) for _ in tokens]
    return pl.pallas_call(
        functools.partial(product_kernel, len(tokens), count, fold),
        out_shape=outs,
        in_specs=[pl.BlockSpec(memory_space=pltpu.VMEM)] * (len(tokens) + count),
        out_specs=[pl.BlockSpec(memory_space=pltpu.VMEM)] * len(tokens),
        compiler_params=pltpu.CompilerParams(vmem_limit_bytes=grant(*tokens, *weights, *outs)),
        cost_estimate=pl.CostEstimate(
            flops=cost * 2 * rows * depth * width * count * len(tokens),
            bytes_accessed=2 * (rows * depth * len(tokens) + depth * width * count + rows * width * count * len(tokens)),
            transcendentals=0,
        ),
        name="token_products",
    )(*tokens, *weights)


def column_tile(features, most=512):
    tile = 128
    for width in range(128, most + 1, 128):
        if features % width == 0:
            tile = width
    return tile


def inverse_kernel(seq_rows, chunk, tile, lengths_ref, act_ref, inverse_ref):
    rows, features = act_ref.shape

    def one_chunk(index, _):
        start = pl.multiple_of(index * chunk, chunk)
        part = pl.ds(start, chunk)
        squares = jnp.zeros((chunk, 128), jnp.float32)
        for left in range(0, features, tile):
            wide = act_ref[part, left : left + tile].astype(jnp.float32)
            wide = wide * wide
            for lane in range(0, tile, 128):
                squares = squares + wide[:, lane : lane + 128]
        mean = jnp.sum(squares, axis=1, keepdims=True) / features
        position = lax.broadcasted_iota(jnp.int32, (chunk, 1), 0) + lax.rem(start, seq_rows)
        keep = position < lengths_ref[lax.div(start, seq_rows)]
        inverse = jnp.where(keep, lax.rsqrt(mean + norm_epsilon), 0.0)
        inverse_ref[part, :] = jnp.broadcast_to(inverse, (chunk, 128))
        return 0

    lax.fori_loop(0, rows // chunk, one_chunk, 0)


def live_inverse(seq_rows, lengths, act):
    rows, features = act.shape
    return pl.pallas_call(
        functools.partial(inverse_kernel, seq_rows, math.gcd(seq_rows, 16), column_tile(features)),
        out_shape=jax.ShapeDtypeStruct((rows, 128), jnp.float32),
        in_specs=[pl.BlockSpec(memory_space=pltpu.SMEM), pl.BlockSpec(memory_space=pltpu.VMEM)],
        out_specs=pl.BlockSpec(memory_space=pltpu.VMEM),
        compiler_params=pltpu.CompilerParams(vmem_limit_bytes=grant(act)),
        cost_estimate=pl.CostEstimate(
            flops=2 * rows * features, bytes_accessed=2 * rows * features, transcendentals=rows
        ),
        name="live_inverse",
    )(lengths, act)


def relative(owner, place, count):
    if count & (count - 1) == 0:
        return owner ^ place
    return (place + count - owner) % count


def place_pieces(line, plane, groups, fold, pieces, held, back):
    width = back.shape[1] // (line * plane)
    me = lax.axis_index("dp")
    z, q = lax.div(me, plane), lax.rem(me, plane)
    for step in range(plane):
        owner_q = ahead(q, step, plane)
        for group_index, group in enumerate(groups):
            piece = pieces[step * len(groups) + group_index]
            for index, line_step in enumerate(group):
                held[behind(z, line_step, line) * plane + owner_q] = piece[index]
    steps = [line_step for group in groups for line_step in group]
    for owner_z in range(line):
        line_step = relative(owner_z, z, line)
        here = functools.reduce(jnp.logical_or, [line_step == step for step in steps])

        @pl.when(here)
        def _():
            for part in range(back.shape[0] // fold):
                rows = slice(part * fold, (part + 1) * fold)
                for block in range(owner_z * plane, (owner_z + 1) * plane):
                    back[rows, block * width : (block + 1) * width] = held[
                        block, :, part * width : (part + 1) * width
                    ]


def add_sums(lefts, part, project, inverse_ref, act_ref, gain_ref, gain_sum, pulls):
    inverse = inverse_ref[part, :]
    pull = pulls[part, :]
    for left in lefts:
        cols = slice(left, left + 128)
        both = act_ref[part, cols].astype(jnp.float32) * project(part, cols)
        pull = pull + both * gain_ref[:, cols]
        both = both * inverse
        folded = both[:8, :]
        for row in range(8, both.shape[0], 8):
            folded = folded + both[row : row + 8, :]
        gain_sum[:, cols] += folded
    pulls[part, :] = pull


def early_kernel(line, plane, groups, fold, chunk, inverse_ref, act_ref, gain_ref, *refs):
    pieces = refs[:-4]
    back, pulls, gain_sum, held = refs[-4:]
    back[...] = jnp.zeros_like(back)
    place_pieces(line, plane, groups, fold, pieces, held, back)
    gain_sum[...] = jnp.zeros_like(gain_sum)
    pulls[...] = jnp.zeros_like(pulls)

    def project(part, cols):
        return back[part, cols].astype(jnp.float32)

    def one_chunk(index, _):
        part = pl.ds(pl.multiple_of(index * chunk, chunk), chunk)
        add_sums(range(0, back.shape[1], 128), part, project, inverse_ref, act_ref, gain_ref, gain_sum, pulls)
        return 0

    lax.fori_loop(0, back.shape[0] // chunk, one_chunk, 0)


def placed_early(line, plane, groups, fold, inverse, act, gain, pieces):
    rows, features = act.shape
    vmem = pl.BlockSpec(memory_space=pltpu.VMEM)
    outs = [
        jax.ShapeDtypeStruct((rows, features), jnp.bfloat16),
        jax.ShapeDtypeStruct((rows, 128), jnp.float32),
        jax.ShapeDtypeStruct((8, features), jnp.float32),
    ]
    scratch = [pltpu.VMEM((line * plane,) + pieces[0].shape[1:], jnp.bfloat16)]
    return pl.pallas_call(
        functools.partial(early_kernel, line, plane, groups, fold, math.gcd(rows, 32)),
        out_shape=outs,
        in_specs=[vmem] * (3 + len(pieces)),
        out_specs=[vmem] * len(outs),
        scratch_shapes=scratch,
        compiler_params=pltpu.CompilerParams(
            vmem_limit_bytes=grant(inverse, act, gain, *pieces, *outs, *scratch)
        ),
        cost_estimate=pl.CostEstimate(
            flops=8 * rows * features, bytes_accessed=8 * rows * features, transcendentals=0
        ),
        name="placed_early",
    )(inverse, act, gain, *pieces)


def finish_kernel(
    line,
    plane,
    groups,
    fold,
    last,
    chunk,
    early_ref,
    early_pulls,
    early_gains,
    inverse_ref,
    act_ref,
    top_ref,
    gain_ref,
    *refs,
):
    pieces = refs[:-10]
    passed_ref, local_ref, gain_out, held, back, gain_sum, pulls, passing, gain_blocks, copied = refs[-10:]
    rows, features = back.shape
    width = features // (line * plane)
    late_steps = [step for group in groups for step in group]
    late_z = behind(lax.div(lax.axis_index("dp"), plane), late_steps[0], line)
    is_last = lax.axis_index("section") == last
    back[...] = early_ref[...]
    place_pieces(line, plane, groups, fold, pieces, held, back)
    gain_sum[...] = early_gains[...]
    pulls[...] = early_pulls[...]

    def project(part, cols):
        return back[part, cols].astype(jnp.float32) - early_ref[part, cols].astype(jnp.float32)

    def add_late(part, lefts):
        add_sums(lefts, part, project, inverse_ref, act_ref, gain_ref, gain_sum, pulls)

    def out_copy(index):
        part = pl.ds(pl.multiple_of(index * chunk, chunk), chunk)
        return pltpu.make_async_copy(passing.at[part], passed_ref.at[part], copied.at[index])

    def late_sums(lefts):
        def one_chunk(index, _):
            add_late(pl.ds(pl.multiple_of(index * chunk, chunk), chunk), lefts)
            return 0

        lax.fori_loop(0, rows // chunk, one_chunk, 0)

    if len(late_steps) > 1:
        late_sums(range(0, features, 128))
    else:
        for owner_z in range(line):
            first = owner_z * plane * width // 128 * 128
            after = (owner_z + 1) * plane * width

            @pl.when(late_z == owner_z)
            def _():
                late_sums(range(first, after, 128))

    def terms(index, _):
        part = pl.ds(pl.multiple_of(index * chunk, chunk), chunk)
        inverse = inverse_ref[part, :]
        pull = jnp.sum(pulls[part, :], axis=1, keepdims=True) / features
        pull = jnp.broadcast_to(pull, inverse.shape) * inverse * inverse * inverse

        def local_term(cols):
            scaled = back[part, cols].astype(jnp.float32) * gain_ref[:, cols]
            return inverse * scaled - act_ref[part, cols].astype(jnp.float32) * pull

        @pl.when(is_last)
        def _():
            for left in range(0, features, 128):
                cols = slice(left, left + 128)
                passing[part, cols] = (top_ref[part, cols].astype(jnp.float32) + local_term(cols)).astype(jnp.bfloat16)
            out_copy(index).start()

        @pl.when(jnp.logical_not(is_last))
        def _():
            for left in range(0, features, 128):
                cols = slice(left, left + 128)
                local_ref[part, cols] = local_term(cols)

        return 0

    total = jnp.sum(gain_sum[...], axis=0, keepdims=True)
    for block in range(line * plane):
        gain_blocks[block] = total[:, block * width : (block + 1) * width]
    gain_copy = pltpu.make_async_copy(gain_blocks, gain_out, copied.at[rows // chunk])
    gain_copy.start()
    lax.fori_loop(0, rows // chunk, terms, 0)

    @pl.when(is_last)
    def _():
        for index in range(rows // chunk):
            out_copy(index).wait()

    gain_copy.wait()


def finish(line, plane, groups, fold, last, early, inverse, act, top, gain, pieces):
    rows, features = act.shape
    blocks = line * plane
    vmem = pl.BlockSpec(memory_space=pltpu.VMEM)
    outs = [
        jax.ShapeDtypeStruct((rows, features), jnp.bfloat16),
        jax.ShapeDtypeStruct((rows, features), jnp.float32),
        jax.ShapeDtypeStruct((blocks, 1, features // blocks), jnp.float32),
    ]
    scratch = [
        pltpu.VMEM((blocks,) + pieces[0].shape[1:], jnp.bfloat16),
        pltpu.VMEM((rows, features), jnp.bfloat16),
        pltpu.VMEM((8, features), jnp.float32),
        pltpu.VMEM((rows, 128), jnp.float32),
        pltpu.VMEM((rows, features), jnp.bfloat16),
        pltpu.VMEM(outs[2].shape, jnp.float32),
    ]
    chunk = math.gcd(rows, 48)
    return pl.pallas_call(
        functools.partial(finish_kernel, line, plane, groups, fold, last, chunk),
        out_shape=outs,
        in_specs=[vmem] * (4 + len(early) + len(pieces)),
        out_specs=[pl.BlockSpec(memory_space=pl.ANY), vmem, pl.BlockSpec(memory_space=pl.ANY)],
        scratch_shapes=scratch + [pltpu.SemaphoreType.DMA((rows // chunk + 1,))],
        compiler_params=pltpu.CompilerParams(
            vmem_limit_bytes=grant(*early, act, top, *pieces, *outs, *scratch)
        ),
        cost_estimate=pl.CostEstimate(
            flops=16 * rows * features, bytes_accessed=12 * rows * features, transcendentals=0
        ),
        name="norm_backward",
    )(*early, inverse, act, top, gain, *pieces)


def hand_kernel(turn, chunk, incoming_ref, local_ref, result_ref, out_ref, loaded, staged, arrived, copied):
    rows, features = local_ref.shape
    parts = [pl.ds(start, chunk) for start in range(0, rows, chunk)]
    is_turn = lax.axis_index("section") == turn

    def through(source, staging, work):
        loads = [
            pltpu.make_async_copy(source.at[part], loaded.at[part], arrived.at[index])
            for index, part in enumerate(parts)
        ]
        stores = [
            pltpu.make_async_copy(staging.at[part], out_ref.at[part], copied.at[index])
            for index, part in enumerate(parts)
        ]
        for load in loads:
            load.start()
        for part, load, store in zip(parts, loads, stores):
            load.wait()
            work(part)
            store.start()
        for store in stores:
            store.wait()

    def add_local(part):
        for left in range(0, features, 128):
            cols = slice(left, left + 128)
            staged[part, cols] = (loaded[part, cols].astype(jnp.float32) + local_ref[part, cols]).astype(jnp.bfloat16)

    @pl.when(is_turn)
    def _():
        through(incoming_ref, staged, add_local)

    @pl.when(jnp.logical_not(is_turn))
    def _():
        through(result_ref, loaded, lambda part: None)


def hand_on(turn, chunk, incoming, local, result):
    rows, features = local.shape
    vmem = pl.BlockSpec(memory_space=pltpu.VMEM)
    hbm = pl.BlockSpec(memory_space=pl.ANY)
    return pl.pallas_call(
        functools.partial(hand_kernel, turn, chunk),
        out_shape=jax.ShapeDtypeStruct((rows, features), jnp.bfloat16),
        in_specs=[hbm, vmem, hbm],
        out_specs=hbm,
        scratch_shapes=[
            pltpu.VMEM((rows, features), jnp.bfloat16),
            pltpu.VMEM((rows, features), jnp.bfloat16),
            pltpu.SemaphoreType.DMA((rows // chunk,)),
            pltpu.SemaphoreType.DMA((rows // chunk,)),
        ],
        compiler_params=pltpu.CompilerParams(vmem_limit_bytes=grant(incoming, local, result)),
        cost_estimate=pl.CostEstimate(flops=0, bytes_accessed=0, transcendentals=0),
        name="hand_on",
    )(incoming, local, result)


def sum_kernel(scale, parts_ref, out_ref):
    total = parts_ref[0]
    for index in range(1, parts_ref.shape[0]):
        total = total + parts_ref[index]
    out_ref[...] = total * scale


def sum_scaled(parts, scale):
    vmem = pl.BlockSpec(memory_space=pltpu.VMEM)
    return pl.pallas_call(
        functools.partial(sum_kernel, scale),
        out_shape=jax.ShapeDtypeStruct(parts.shape[1:], jnp.float32),
        in_specs=[vmem],
        out_specs=vmem,
        compiler_params=pltpu.CompilerParams(vmem_limit_bytes=mebibyte),
        cost_estimate=pl.CostEstimate(flops=parts.size, bytes_accessed=4 * parts.size, transcendentals=0),
        name="sum_scaled",
    )(parts)


def sent_back(group_products, line, plane):
    return [group_products[0]] + [
        along_plane(group_products[step], step, line, plane, back=True) for step in range(1, plane)
    ]


def gathered_products(fold, tokens, shard, line, plane):
    held = {0: shard}
    groups = [(0,)]
    first = products(fold, tokens, [shard], 1)
    if line & (line - 1):
        for step in range(1, line):
            held[step] = along_line(shard, step, line, plane)
        groups.append(tuple(range(1, (line + 1) // 2)))
    elif line > 1:
        distance = line // 2
        while distance:
            held[distance] = along_line(shard, distance, line, plane)
            distance //= 2
        groups.append(tuple(sorted(step for step in held if step)))
        far = line // 2
        held[far], own = lax.optimization_barrier((held[far], first[0]))
        first = [own] + list(first[1:])
        distance = line // 4
        while distance:
            for step in sorted(held):
                if step and step % (2 * distance) == 0 and step + distance not in held:
                    held[step + distance] = along_line(held[step], distance, line, plane)
            distance //= 2
    groups.append(tuple(step for step in range(line) if not any(step in group for group in groups)))
    groups = [group for group in groups if group]
    pieces = [sent_back(first, line, plane)]
    for group in groups[1:]:
        shards = [held[step] for step in group]
        made = list(products(fold, tokens, shards, product_cost))
        if len(pieces) == 1:
            made[-1], pieces[0] = lax.optimization_barrier((made[-1], pieces[0]))
        pieces.append(sent_back(made, line, plane))
    return groups, pieces


def on_device(activations, key_grads, top_grad, norm_gains, w_key, lengths):
    micro_count, seq_rows, features = activations.shape[2:]
    rows = micro_count * seq_rows
    fold = math.gcd(rows, 16)
    replicas = lax.axis_size("dp")
    sections = lax.axis_size("section")
    plane = plane_size(replicas)
    line = replicas // plane
    grad_scale = 1.0 / math.sqrt(replicas * rows)
    act = activations.reshape(rows, features)

    key_rows = key_grads.reshape(rows, key_grads.shape[-1])
    inverse, own_rows = lax.optimization_barrier((live_inverse(seq_rows, lengths[0], act), key_rows))
    tokens = [own_rows] + [along_plane(key_rows, step, line, plane) for step in range(1, plane)]
    groups, pieces = gathered_products(fold, tokens, w_key[0], line, plane)
    split = max(1, len(groups) - 1)
    early, late = ([part[step] for step in range(plane) for part in some] for some in (pieces[:split], pieces[split:]))
    early = placed_early(line, plane, groups[:split], fold, inverse, act, norm_gains, early)
    top = top_grad.reshape(rows, features)
    passed, local, gain_blocks = finish(
        line, plane, groups[split:], fold, sections - 1, early, inverse, act, top, norm_gains, late
    )

    result = passed
    for turn in range(sections - 2, -1, -1):
        incoming = lax.ppermute(result, "section", [(turn + 1, turn), (turn, turn + 1)])
        result = hand_on(turn, seq_rows, incoming, local, result)

    gain_parts = lax.all_to_all(gain_blocks, "dp", split_axis=0, concat_axis=0, tiled=True)
    gain_parts, result = lax.optimization_barrier((gain_parts, result))
    grad_shard = sum_scaled(gain_parts, grad_scale)
    return (result.reshape(activations.shape), grad_shard)


def solution(mesh):
    placed = (
        P("section", "dp", None, None, None),
        P("section", "dp", None, None, None),
        P("dp", None, None, None),
        P("section", None),
        P("section", "dp", None),
        P("dp", None),
    )
    return jax.shard_map(
        on_device,
        mesh=mesh,
        in_specs=placed,
        out_specs=(P("section", "dp", None, None, None), P("section", "dp")),
        check_vma=False,
    )
```

```python
import functools
import math

import jax
import jax.numpy as jnp
from jax import lax
from jax.experimental import pallas as pl
from jax.experimental.pallas import tpu as pltpu
from jax.sharding import PartitionSpec as P

norm_epsilon = 1e-05
mebibyte = 1024 * 1024
product_cost = 10


def grant(*arrays):
    total = 4 * mebibyte
    for array in arrays:
        lanes = -(-array.shape[-1] // 128) * 128
        total += math.prod(array.shape[:-1]) * lanes * jnp.dtype(array.dtype).itemsize
    return -(-total // mebibyte) * mebibyte


def plane_size(replicas):
    size = 1
    while (2 * size) ** 2 <= replicas and replicas % (2 * size) == 0:
        size *= 2
    return size


def ahead(place, step, count):
    if count & (count - 1) == 0:
        return place ^ step
    return (place + step) % count


def behind(place, step, count):
    if count & (count - 1) == 0:
        return place ^ step
    return (place + count - step) % count


def along_line(value, step, line, plane):
    pairs = [
        (z * plane + q, ahead(z, step, line) * plane + q)
        for z in range(line)
        for q in range(plane)
    ]
    return lax.ppermute(value, "dp", pairs)


def along_plane(value, step, line, plane, back=False):
    partner = behind if back else ahead
    pairs = [
        (z * plane + q, z * plane + partner(q, step, plane))
        for z in range(line)
        for q in range(plane)
    ]
    return lax.ppermute(value, "dp", pairs)


def product_kernel(token_count, weight_count, fold, *refs):
    tokens = refs[:token_count]
    weights = refs[token_count : token_count + weight_count]
    outs = refs[token_count + weight_count :]
    for token_ref, out_ref in zip(tokens, outs):
        for index, weight_ref in enumerate(weights):
            product = lax.dot_general(
                token_ref[...],
                weight_ref[...],
                (((1,), (1,)), ((), ())),
                preferred_element_type=jnp.float32,
            ).astype(out_ref.dtype)
            width = product.shape[1]
            for part in range(product.shape[0] // fold):
                out_ref[index, :, part * width : (part + 1) * width] = product[part * fold : (part + 1) * fold, :]


def products(fold, tokens, weights, cost):
    rows, depth = tokens[0].shape
    width = weights[0].shape[0]
    count = len(weights)
    folded = (count, fold, rows // fold * width)
    outs = [jax.ShapeDtypeStruct(folded, jnp.bfloat16) for _ in tokens]
    return pl.pallas_call(
        functools.partial(product_kernel, len(tokens), count, fold),
        out_shape=outs,
        in_specs=[pl.BlockSpec(memory_space=pltpu.VMEM)] * (len(tokens) + count),
        out_specs=[pl.BlockSpec(memory_space=pltpu.VMEM)] * len(tokens),
        compiler_params=pltpu.CompilerParams(vmem_limit_bytes=grant(*tokens, *weights, *outs)),
        cost_estimate=pl.CostEstimate(
            flops=cost * 2 * rows * depth * width * count * len(tokens),
            bytes_accessed=2 * (rows * depth * len(tokens) + depth * width * count + rows * width * count * len(tokens)),
            transcendentals=0,
        ),
        name="token_products",
    )(*tokens, *weights)


def column_tile(features, most=512):
    tile = 128
    for width in range(128, most + 1, 128):
        if features % width == 0:
            tile = width
    return tile


def inverse_kernel(seq_rows, chunk, tile, lengths_ref, act_ref, inverse_ref):
    rows, features = act_ref.shape

    def one_chunk(index, _):
        start = pl.multiple_of(index * chunk, chunk)
        part = pl.ds(start, chunk)
        squares = jnp.zeros((chunk, 128), jnp.float32)
        for left in range(0, features, tile):
            wide = act_ref[part, left : left + tile].astype(jnp.float32)
            wide = wide * wide
            for lane in range(0, tile, 128):
                squares = squares + wide[:, lane : lane + 128]
        mean = jnp.sum(squares, axis=1, keepdims=True) / features
        position = lax.broadcasted_iota(jnp.int32, (chunk, 1), 0) + lax.rem(start, seq_rows)
        keep = position < lengths_ref[lax.div(start, seq_rows)]
        inverse = jnp.where(keep, lax.rsqrt(mean + norm_epsilon), 0.0)
        inverse_ref[part, :] = jnp.broadcast_to(inverse, (chunk, 128))
        return 0

    lax.fori_loop(0, rows // chunk, one_chunk, 0)


def live_inverse(seq_rows, lengths, act):
    rows, features = act.shape
    return pl.pallas_call(
        functools.partial(inverse_kernel, seq_rows, math.gcd(seq_rows, 16), column_tile(features)),
        out_shape=jax.ShapeDtypeStruct((rows, 128), jnp.float32),
        in_specs=[pl.BlockSpec(memory_space=pltpu.SMEM), pl.BlockSpec(memory_space=pltpu.VMEM)],
        out_specs=pl.BlockSpec(memory_space=pltpu.VMEM),
        compiler_params=pltpu.CompilerParams(vmem_limit_bytes=grant(act)),
        cost_estimate=pl.CostEstimate(
            flops=2 * rows * features, bytes_accessed=2 * rows * features, transcendentals=rows
        ),
        name="live_inverse",
    )(lengths, act)


def relative(owner, place, count):
    if count & (count - 1) == 0:
        return owner ^ place
    return (place + count - owner) % count


def place_pieces(line, plane, groups, fold, pieces, held, back):
    width = back.shape[1] // (line * plane)
    me = lax.axis_index("dp")
    z, q = lax.div(me, plane), lax.rem(me, plane)
    for step in range(plane):
        owner_q = ahead(q, step, plane)
        for group_index, group in enumerate(groups):
            piece = pieces[step * len(groups) + group_index]
            for index, line_step in enumerate(group):
                held[behind(z, line_step, line) * plane + owner_q] = piece[index]
    steps = [line_step for group in groups for line_step in group]
    for owner_z in range(line):
        line_step = relative(owner_z, z, line)
        here = functools.reduce(jnp.logical_or, [line_step == step for step in steps])

        @pl.when(here)
        def _():
            for part in range(back.shape[0] // fold):
                rows = slice(part * fold, (part + 1) * fold)
                for block in range(owner_z * plane, (owner_z + 1) * plane):
                    back[rows, block * width : (block + 1) * width] = held[
                        block, :, part * width : (part + 1) * width
                    ]


def add_sums(lefts, part, project, inverse_ref, act_ref, gain_ref, gain_sum, pulls):
    inverse = inverse_ref[part, :]
    pull = pulls[part, :]
    for left in lefts:
        cols = slice(left, left + 128)
        both = act_ref[part, cols].astype(jnp.float32) * project(part, cols)
        pull = pull + both * gain_ref[:, cols]
        both = both * inverse
        folded = both[:8, :]
        for row in range(8, both.shape[0], 8):
            folded = folded + both[row : row + 8, :]
        gain_sum[:, cols] += folded
    pulls[part, :] = pull


def early_kernel(line, plane, groups, fold, chunk, inverse_ref, act_ref, gain_ref, *refs):
    pieces = refs[:-4]
    back, pulls, gain_sum, held = refs[-4:]
    back[...] = jnp.zeros_like(back)
    place_pieces(line, plane, groups, fold, pieces, held, back)
    gain_sum[...] = jnp.zeros_like(gain_sum)
    pulls[...] = jnp.zeros_like(pulls)

    def project(part, cols):
        return back[part, cols].astype(jnp.float32)

    def one_chunk(index, _):
        part = pl.ds(pl.multiple_of(index * chunk, chunk), chunk)
        add_sums(range(0, back.shape[1], 128), part, project, inverse_ref, act_ref, gain_ref, gain_sum, pulls)
        return 0

    lax.fori_loop(0, back.shape[0] // chunk, one_chunk, 0)


def placed_early(line, plane, groups, fold, inverse, act, gain, pieces):
    rows, features = act.shape
    vmem = pl.BlockSpec(memory_space=pltpu.VMEM)
    outs = [
        jax.ShapeDtypeStruct((rows, features), jnp.bfloat16),
        jax.ShapeDtypeStruct((rows, 128), jnp.float32),
        jax.ShapeDtypeStruct((8, features), jnp.float32),
    ]
    scratch = [pltpu.VMEM((line * plane,) + pieces[0].shape[1:], jnp.bfloat16)]
    return pl.pallas_call(
        functools.partial(early_kernel, line, plane, groups, fold, math.gcd(rows, 48)),
        out_shape=outs,
        in_specs=[vmem] * (3 + len(pieces)),
        out_specs=[vmem] * len(outs),
        scratch_shapes=scratch,
        compiler_params=pltpu.CompilerParams(
            vmem_limit_bytes=grant(inverse, act, gain, *pieces, *outs, *scratch)
        ),
        cost_estimate=pl.CostEstimate(
            flops=8 * rows * features, bytes_accessed=8 * rows * features, transcendentals=0
        ),
        name="placed_early",
    )(inverse, act, gain, *pieces)


def finish_kernel(
    line,
    plane,
    groups,
    fold,
    last,
    chunk,
    early_ref,
    early_pulls,
    early_gains,
    inverse_ref,
    act_ref,
    top_ref,
    gain_ref,
    *refs,
):
    pieces = refs[:-10]
    passed_ref, local_ref, gain_out, held, back, gain_sum, pulls, passing, gain_blocks, copied = refs[-10:]
    rows, features = back.shape
    width = features // (line * plane)
    late_steps = [step for group in groups for step in group]
    late_z = behind(lax.div(lax.axis_index("dp"), plane), late_steps[0], line)
    is_last = lax.axis_index("section") == last
    back[...] = early_ref[...]
    place_pieces(line, plane, groups, fold, pieces, held, back)
    gain_sum[...] = early_gains[...]
    pulls[...] = early_pulls[...]

    def project(part, cols):
        return back[part, cols].astype(jnp.float32) - early_ref[part, cols].astype(jnp.float32)

    def add_late(part, lefts):
        add_sums(lefts, part, project, inverse_ref, act_ref, gain_ref, gain_sum, pulls)

    def out_copy(index):
        part = pl.ds(pl.multiple_of(index * chunk, chunk), chunk)
        return pltpu.make_async_copy(passing.at[part], passed_ref.at[part], copied.at[index])

    def late_sums(lefts):
        def one_chunk(index, _):
            add_late(pl.ds(pl.multiple_of(index * chunk, chunk), chunk), lefts)
            return 0

        lax.fori_loop(0, rows // chunk, one_chunk, 0)

    if len(late_steps) > 1:
        late_sums(range(0, features, 128))
    else:
        for owner_z in range(line):
            first = owner_z * plane * width // 128 * 128
            after = (owner_z + 1) * plane * width

            @pl.when(late_z == owner_z)
            def _():
                late_sums(range(first, after, 128))

    def terms(index, _):
        part = pl.ds(pl.multiple_of(index * chunk, chunk), chunk)
        inverse = inverse_ref[part, :]
        pull = jnp.sum(pulls[part, :], axis=1, keepdims=True) / features
        pull = jnp.broadcast_to(pull, inverse.shape) * inverse * inverse * inverse

        def local_term(cols):
            scaled = back[part, cols].astype(jnp.float32) * gain_ref[:, cols]
            return inverse * scaled - act_ref[part, cols].astype(jnp.float32) * pull

        @pl.when(is_last)
        def _():
            for left in range(0, features, 128):
                cols = slice(left, left + 128)
                passing[part, cols] = (top_ref[part, cols].astype(jnp.float32) + local_term(cols)).astype(jnp.bfloat16)
            out_copy(index).start()

        @pl.when(jnp.logical_not(is_last))
        def _():
            for left in range(0, features, 128):
                cols = slice(left, left + 128)
                local_ref[part, cols] = local_term(cols)

        return 0

    total = jnp.sum(gain_sum[...], axis=0, keepdims=True)
    for block in range(line * plane):
        gain_blocks[block] = total[:, block * width : (block + 1) * width]
    gain_copy = pltpu.make_async_copy(gain_blocks, gain_out, copied.at[rows // chunk])
    gain_copy.start()
    lax.fori_loop(0, rows // chunk, terms, 0)

    @pl.when(is_last)
    def _():
        for index in range(rows // chunk):
            out_copy(index).wait()

    gain_copy.wait()


def finish(line, plane, groups, fold, last, early, inverse, act, top, gain, pieces):
    rows, features = act.shape
    blocks = line * plane
    vmem = pl.BlockSpec(memory_space=pltpu.VMEM)
    outs = [
        jax.ShapeDtypeStruct((rows, features), jnp.bfloat16),
        jax.ShapeDtypeStruct((rows, features), jnp.float32),
        jax.ShapeDtypeStruct((blocks, 1, features // blocks), jnp.float32),
    ]
    scratch = [
        pltpu.VMEM((blocks,) + pieces[0].shape[1:], jnp.bfloat16),
        pltpu.VMEM((rows, features), jnp.bfloat16),
        pltpu.VMEM((8, features), jnp.float32),
        pltpu.VMEM((rows, 128), jnp.float32),
        pltpu.VMEM((rows, features), jnp.bfloat16),
        pltpu.VMEM(outs[2].shape, jnp.float32),
    ]
    chunk = math.gcd(rows, 48)
    return pl.pallas_call(
        functools.partial(finish_kernel, line, plane, groups, fold, last, chunk),
        out_shape=outs,
        in_specs=[vmem] * (4 + len(early) + len(pieces)),
        out_specs=[pl.BlockSpec(memory_space=pl.ANY), vmem, pl.BlockSpec(memory_space=pl.ANY)],
        scratch_shapes=scratch + [pltpu.SemaphoreType.DMA((rows // chunk + 1,))],
        compiler_params=pltpu.CompilerParams(
            vmem_limit_bytes=grant(*early, act, top, *pieces, *outs, *scratch)
        ),
        cost_estimate=pl.CostEstimate(
            flops=16 * rows * features, bytes_accessed=12 * rows * features, transcendentals=0
        ),
        name="norm_backward",
    )(*early, inverse, act, top, gain, *pieces)


def hand_kernel(turn, chunk, incoming_ref, local_ref, result_ref, out_ref, loaded, staged, arrived, copied):
    rows, features = local_ref.shape
    parts = [pl.ds(start, chunk) for start in range(0, rows, chunk)]
    is_turn = lax.axis_index("section") == turn

    def through(source, staging, work):
        loads = [
            pltpu.make_async_copy(source.at[part], loaded.at[part], arrived.at[index])
            for index, part in enumerate(parts)
        ]
        stores = [
            pltpu.make_async_copy(staging.at[part], out_ref.at[part], copied.at[index])
            for index, part in enumerate(parts)
        ]
        for load in loads:
            load.start()
        for part, load, store in zip(parts, loads, stores):
            load.wait()
            work(part)
            store.start()
        for store in stores:
            store.wait()

    def add_local(part):
        for left in range(0, features, 128):
            cols = slice(left, left + 128)
            staged[part, cols] = (loaded[part, cols].astype(jnp.float32) + local_ref[part, cols]).astype(jnp.bfloat16)

    @pl.when(is_turn)
    def _():
        through(incoming_ref, staged, add_local)

    @pl.when(jnp.logical_not(is_turn))
    def _():
        through(result_ref, loaded, lambda part: None)


def hand_on(turn, chunk, incoming, local, result):
    rows, features = local.shape
    vmem = pl.BlockSpec(memory_space=pltpu.VMEM)
    hbm = pl.BlockSpec(memory_space=pl.ANY)
    return pl.pallas_call(
        functools.partial(hand_kernel, turn, chunk),
        out_shape=jax.ShapeDtypeStruct((rows, features), jnp.bfloat16),
        in_specs=[hbm, vmem, hbm],
        out_specs=hbm,
        scratch_shapes=[
            pltpu.VMEM((rows, features), jnp.bfloat16),
            pltpu.VMEM((rows, features), jnp.bfloat16),
            pltpu.SemaphoreType.DMA((rows // chunk,)),
            pltpu.SemaphoreType.DMA((rows // chunk,)),
        ],
        compiler_params=pltpu.CompilerParams(vmem_limit_bytes=grant(incoming, local, result)),
        cost_estimate=pl.CostEstimate(flops=0, bytes_accessed=0, transcendentals=0),
        name="hand_on",
    )(incoming, local, result)


def sum_kernel(scale, parts_ref, out_ref):
    total = parts_ref[0]
    for index in range(1, parts_ref.shape[0]):
        total = total + parts_ref[index]
    out_ref[...] = total * scale


def sum_scaled(parts, scale):
    vmem = pl.BlockSpec(memory_space=pltpu.VMEM)
    return pl.pallas_call(
        functools.partial(sum_kernel, scale),
        out_shape=jax.ShapeDtypeStruct(parts.shape[1:], jnp.float32),
        in_specs=[vmem],
        out_specs=vmem,
        compiler_params=pltpu.CompilerParams(vmem_limit_bytes=mebibyte),
        cost_estimate=pl.CostEstimate(flops=parts.size, bytes_accessed=4 * parts.size, transcendentals=0),
        name="sum_scaled",
    )(parts)


def sent_back(group_products, line, plane):
    return [group_products[0]] + [
        along_plane(group_products[step], step, line, plane, back=True) for step in range(1, plane)
    ]


def gathered_products(fold, tokens, shard, line, plane):
    held = {0: shard}
    groups = [(0,)]
    first = products(fold, tokens, [shard], 1)
    if line & (line - 1):
        for step in range(1, line):
            held[step] = along_line(shard, step, line, plane)
        groups.append(tuple(range(1, (line + 1) // 2)))
    elif line > 1:
        distance = line // 2
        while distance:
            held[distance] = along_line(shard, distance, line, plane)
            distance //= 2
        groups.append(tuple(sorted(step for step in held if step)))
        far = line // 2
        held[far], own = lax.optimization_barrier((held[far], first[0]))
        first = [own] + list(first[1:])
        distance = line // 4
        while distance:
            for step in sorted(held):
                if step and step % (2 * distance) == 0 and step + distance not in held:
                    held[step + distance] = along_line(held[step], distance, line, plane)
            distance //= 2
    groups.append(tuple(step for step in range(line) if not any(step in group for group in groups)))
    groups = [group for group in groups if group]
    pieces = [sent_back(first, line, plane)]
    for group in groups[1:]:
        shards = [held[step] for step in group]
        made = list(products(fold, tokens, shards, product_cost))
        if len(pieces) == 1:
            made[-1], pieces[0] = lax.optimization_barrier((made[-1], pieces[0]))
        pieces.append(sent_back(made, line, plane))
    return groups, pieces


def on_device(activations, key_grads, top_grad, norm_gains, w_key, lengths):
    micro_count, seq_rows, features = activations.shape[2:]
    rows = micro_count * seq_rows
    fold = math.gcd(rows, 16)
    replicas = lax.axis_size("dp")
    sections = lax.axis_size("section")
    plane = plane_size(replicas)
    line = replicas // plane
    grad_scale = 1.0 / math.sqrt(replicas * rows)
    act = activations.reshape(rows, features)

    key_rows = key_grads.reshape(rows, key_grads.shape[-1])
    inverse, own_rows = lax.optimization_barrier((live_inverse(seq_rows, lengths[0], act), key_rows))
    tokens = [own_rows] + [along_plane(key_rows, step, line, plane) for step in range(1, plane)]
    groups, pieces = gathered_products(fold, tokens, w_key[0], line, plane)
    split = max(1, len(groups) - 1)
    early, late = ([part[step] for step in range(plane) for part in some] for some in (pieces[:split], pieces[split:]))
    early = placed_early(line, plane, groups[:split], fold, inverse, act, norm_gains, early)
    top = top_grad.reshape(rows, features)
    passed, local, gain_blocks = finish(
        line, plane, groups[split:], fold, sections - 1, early, inverse, act, top, norm_gains, late
    )

    result = passed
    for turn in range(sections - 2, -1, -1):
        incoming = lax.ppermute(result, "section", [(turn + 1, turn), (turn, turn + 1)])
        result = hand_on(turn, seq_rows, incoming, local, result)

    gain_parts = lax.all_to_all(gain_blocks, "dp", split_axis=0, concat_axis=0, tiled=True)
    gain_parts, result = lax.optimization_barrier((gain_parts, result))
    grad_shard = sum_scaled(gain_parts, grad_scale)
    return (result.reshape(activations.shape), grad_shard)


def solution(mesh):
    placed = (
        P("section", "dp", None, None, None),
        P("section", "dp", None, None, None),
        P("dp", None, None, None),
        P("section", None),
        P("section", "dp", None),
        P("dp", None),
    )
    return jax.shard_map(
        on_device,
        mesh=mesh,
        in_specs=placed,
        out_specs=(P("section", "dp", None, None, None), P("section", "dp")),
        check_vma=False,
    )
```
